256 devices in a mesh: gx: 32 (over z_hi, x, core), gy: 8 (over y, z_lo).
Axes of the slice: x: 4, y: 4, z: 8 (z_hi: 4, z_lo: 2; z = z_hi * 2 + z_lo), core: 2. Of those that a mesh axis runs over, the one named last changes fastest.
Arguments:
- noisy_field: bfloat16 [16, 256, 1024], P(None, 'gx', 'gy'), may hold values from -6 to 6
- first_weight: bfloat16 [16, 1, 3, 3, 3], replicated, may hold values from -1.5 to 1.5
- down_weight: bfloat16 [32, 16, 3, 3, 3], replicated, may hold values from -0.375 to 0.375
- coarse_weight: bfloat16 [64, 32, 3, 3, 3], replicated, may hold values from -0.25 to 0.25
- middle_weight: bfloat16 [32, 96, 3, 3, 3], replicated, may hold values from -0.15625 to 0.15625
- fine_weight: bfloat16 [16, 48, 3, 3, 3], replicated, may hold values from -0.25 to 0.25
- head_weight: bfloat16 [16], replicated, may hold values from -1.5 to 1.5
Outputs:
- noise_estimate: float32 [16, 256, 1024], P(None, 'gx', 'gy')
The draws below stay inside these ranges and needn't reach their ends.
All inputs are finite; a program needn't handle non-finite values.
Results may differ from the reference program's by a relative error of at most 0.005.
Values may be sent and summed in bfloat16 or wider, within the bound.
No kernel may reach another device: no remote copies, remote signals or barrier semaphores. Data moves between devices by JAX's collectives and lax.ppermute only.
A program may use at most 128 MiB of HBM per device.

```python
import math
import jax
import jax.numpy as jnp
from jax import lax

CZ = 16
C1 = 16
C2 = 32
C3 = 64
NX = 256
NY = 1024


def block_levels(stream_key, shape, cuts, smallest, top_value):
    factor_of = 1.0
    for axis_at, parts in cuts:
        heights = jax.random.uniform(jax.random.fold_in(jax.random.fold_in(stream_key, 6), axis_at), (parts,), jnp.float32, smallest / len(cuts), top_value / len(cuts))
        factor_of = factor_of * jnp.repeat(jnp.exp(heights), shape[axis_at] // parts).reshape((-1,) + (1,) * (len(shape) - 1 - axis_at))
    return factor_of


def bell_draw(own_key, extent, scale, bound, split=(), kind=jnp.bfloat16):
    drawn = jax.random.normal(own_key, extent, jnp.float32) * scale
    if len(split) > 0:
        drawn = block_levels(own_key, extent, split, -0.22, 0.18) * drawn
    return jnp.clip(drawn, min=-bound, max=bound).astype(kind)


def setup_inputs(seed: int = 0) -> dict:
    arg_keys = jax.random.split(jax.random.key(seed), 8)
    return {
        "noisy_field": bell_draw(arg_keys[0], (CZ, NX, NY), 1.0, 6.0, ((1, 32), (2, 8))),
        "first_weight": bell_draw(arg_keys[1], (C1, 1, 3, 3, 3), 14 ** -0.5, 1.5),
        "down_weight": bell_draw(arg_keys[2], (C2, C1, 3, 3, 3), (14 * C1) ** -0.5, 0.375),
        "coarse_weight": bell_draw(arg_keys[3], (C3, C2, 3, 3, 3), (14 * C2) ** -0.5, 0.25),
        "middle_weight": bell_draw(arg_keys[4], (C2, C3 + C2, 3, 3, 3), (14 * (C3 + C2)) ** -0.5, 0.15625),
        "fine_weight": bell_draw(arg_keys[5], (C1, C2 + C1, 3, 3, 3), (14 * (C2 + C1)) ** -0.5, 0.25),
        "head_weight": bell_draw(arg_keys[6], (C1,), C1 ** -0.5, 1.5),
    }


def upsample(feature):
    return jnp.repeat(jnp.repeat(jnp.repeat(feature, 2, 1), 2, 2), 2, 3)


def average_pool(feature):
    channels, depth, extent_x, extent_y = feature.shape
    grouped = feature.astype(jnp.float32).reshape(channels, depth // 2, 2, extent_x // 2, 2, extent_y // 2, 2)
    return grouped.mean(axis=(2, 4, 6)).astype(jnp.bfloat16)


def convolve(window_cells, kernel):
    return lax.conv_general_dilated(window_cells[None], kernel, (1, 1, 1), "VALID", dimension_numbers=("NCDHW", "OIDHW", "NCDHW"), precision=lax.Precision.HIGHEST)[0]


def conv_level(pairs, channels):
    feature, kernel, coarse_flag = pairs[0]
    scale = 2 if coarse_flag else 1
    depth = feature.shape[1] * scale
    extent_x = feature.shape[2] * scale
    extent_y = feature.shape[3] * scale
    block_rows = math.gcd(extent_x, 32)
    prepared = [(jnp.pad(item, ((0, 0), (1, 1), (1, 1), (1, 1))), weights.astype(jnp.float32), flag) for item, weights, flag in pairs]

    def block_conv(position):
        offset = (position * block_rows).astype(jnp.int32)
        accumulated = jnp.zeros((channels, depth, block_rows, extent_y), jnp.float32)
        for padded, weights, flag in prepared:
            if flag:
                window_cells = lax.dynamic_slice_in_dim(padded, (offset // 2).astype(jnp.int32), block_rows // 2 + 2, 2)
                window_cells = upsample(window_cells)[:, 1:-1, 1:block_rows + 3, 1:-1]
            else:
                window_cells = lax.dynamic_slice_in_dim(padded, offset, block_rows + 2, 2)
            accumulated = accumulated + convolve(window_cells.astype(jnp.float32), weights)
        return jax.nn.silu(accumulated).astype(jnp.bfloat16)

    blocks = lax.map(block_conv, jnp.arange(extent_x // block_rows, dtype=jnp.int32))
    return jnp.transpose(blocks, (1, 2, 0, 3, 4)).reshape(channels, depth, extent_x, extent_y)


def reference(noisy_field, first_weight, down_weight, coarse_weight, middle_weight, fine_weight, head_weight):
    fine_skip = conv_level([(noisy_field[None], first_weight, False)], C1)
    pooled_fine = average_pool(fine_skip)
    middle_skip = conv_level([(pooled_fine, down_weight, False)], C2)
    pooled_middle = average_pool(middle_skip)
    coarse = conv_level([(pooled_middle, coarse_weight, False)], C3)
    middle_up = conv_level([(coarse, middle_weight[:, :C3], True), (middle_skip, middle_weight[:, C3:], False)], C2)
    fine_up = conv_level([(middle_up, fine_weight[:, :C2], True), (fine_skip, fine_weight[:, C2:], False)], C1)
    return jnp.einsum("c,czxy->zxy", head_weight.astype(jnp.float32), fine_up.astype(jnp.float32))
```

```python
import jax
import jax.numpy as jnp
from jax import lax
from jax.experimental import pallas as pl
from jax.experimental.pallas import tpu as pltpu
from jax.sharding import PartitionSpec as P

BF = jnp.bfloat16
F32 = jnp.float32
J = 48
VMEM = pl.BlockSpec(memory_space=pltpu.VMEM)


def dot(a, b):
    return jnp.dot(a, b, preferred_element_type=F32)


def dot_nt(a, b):
    return lax.dot_general(a, b, (((1,), (1,)), ((), ())), preferred_element_type=F32)


def dot_tn(a, b):
    return lax.dot_general(a, b, (((0,), (0,)), ((), ())), preferred_element_type=F32)


def iota(shape, axis):
    return lax.broadcasted_iota(jnp.int32, shape, axis)


def natural(channels):
    return lambda lane: lane // channels


def halves(channels):
    return lambda lane: 2 * ((lane // channels) % (128 // channels)) + lane // 128


def repeat_matrix(channels):
    return (iota((channels, 256), 1) % channels == iota((channels, 256), 0)).astype(BF)


def ones_where(cond):
    return jnp.where(cond, 1.0, 0.0).astype(BF)


def band_masks(rows, depth, depth_of):
    place = depth_of(iota((rows, 256), 1))
    return [ones_where(place == depth + 1 - tap) for tap in range(3)]


def up_masks(rows, depth, depth_of):
    place = depth_of(iota((rows, 256), 1))
    inner = (place == 2 * depth) | (place == 2 * depth + 1)
    outer = (place == 2 * depth + 2) | (place == 2 * depth - 1)
    return ones_where(inner), ones_where(outer)


SETS = (((0,), (1, 2)), ((0, 1), (2,)))


def weights_kernel(
    first, down, coarse, middle, fine, head,
    w_first, w_down, w_coarse, w_mid_skip, w_mid_up, w_fine_skip, w_fine_up, w_head,
    tiled,
):
    r16, r32, r64 = repeat_matrix(16), repeat_matrix(32), repeat_matrix(64)

    w_first[...] = jnp.zeros_like(w_first)
    for dx in range(3):
        rows = [dot(first[dz * 3 + dx], r16) * 0.5 for dz in range(3)]
        place = halves(16)(iota((16, 256), 1))
        depth = iota((16, 256), 0)
        for dy in range(3):
            block = jnp.zeros((16, 256), F32)
            for dz in range(3):
                block = block + jnp.where(place == depth + 1 - dz, rows[dz][dy : dy + 1], 0.0)
            block = block.astype(BF)
            for even in range(2):
                w_first[even, pl.ds(dy * 64 + (even + dx) * 16, 16), :] = block

    def banded(out, taps, channels, row_depths, depth_of):
        size = channels * len(row_depths)
        for at, depth in enumerate(row_depths):
            masks = band_masks(channels, depth, depth_of)
            for xy in range(9):
                block = sum(masks[dz] * taps[dz][xy] for dz in range(3))
                out[pl.ds(xy * size + at * channels, channels), :] = block

    def folded(out, get, channels, depths, depth_of):
        size = channels * depths
        place = depth_of(iota((channels, 256), 1))
        even = place % 2 == 0
        masks = [up_masks(channels, depth, depth_of) for depth in range(depths)]
        for px in range(2):
            for tx in range(2):
                by_y = [
                    [sum(get(dz, dx, dy) for dx in SETS[px][tx]) for dy in range(3)]
                    for dz in range(3)
                ]
                for py in range(2):
                    for ty in range(2):
                        w0, w1, w2 = [
                            sum(by_y[dz][dy] for dy in SETS[py][ty]) for dz in range(3)
                        ]
                        inner = jnp.where(even, w1 + w2, w0 + w1).astype(BF)
                        outer = jnp.where(even, w0, w2).astype(BF)
                        for depth in range(depths):
                            block = masks[depth][0] * inner + masks[depth][1] * outer
                            at = (tx * 2 + ty) * size + depth * channels
                            out[px * 2 + py, pl.ds(at, channels), :] = block

    flat = down[...].reshape(27 * 16, 32)
    all_taps = (dot(flat, r32) * (1 / 16)).astype(BF)
    taps = [[all_taps[(dz * 9 + xy) * 16 : (dz * 9 + xy + 1) * 16] for xy in range(9)] for dz in range(3)]
    banded(w_down, taps, 16, list(range(8)), halves(32))

    flat = coarse[...].reshape(27 * 32, 64)
    all_taps = (dot(flat, r64) * (1 / 16)).astype(BF)
    taps = [[all_taps[(dz * 9 + xy) * 32 : (dz * 9 + xy + 1) * 32] for xy in range(9)] for dz in range(3)]
    banded(w_coarse, taps, 32, list(range(4)), natural(64))

    for tap in range(27):
        tiled[tap] = dot_tn(middle[tap], r32) * 0.5
    taps = [[tiled[dz * 9 + xy, 64:96, :].astype(BF) for xy in range(9)] for dz in range(3)]
    banded(w_mid_skip, taps, 32, [0, 2, 4, 6, 1, 3, 5, 7], natural(32))
    folded(w_mid_up, lambda dz, dx, dy: tiled[dz * 9 + dx * 3 + dy, 0:64, :], 64, 4, natural(32))

    for tap in range(27):
        tiled[tap, 0:48, :] = dot_tn(fine[tap], r16) * 0.5
    taps = [[tiled[dz * 9 + xy, 32:48, :].astype(BF) for xy in range(9)] for dz in range(3)]
    banded(w_fine_skip, taps, 16, list(range(0, 16, 2)) + list(range(1, 16, 2)), natural(16))
    folded(w_fine_up, lambda dz, dx, dy: tiled[dz * 9 + dx * 3 + dy, 0:32, :], 32, 8, natural(16))

    row = dot(jnp.broadcast_to(head[...], (16, 16)), r16)
    w_head[...] = jnp.where(iota((16, 256), 1) // 16 == iota((16, 256), 0), row, 0.0).astype(BF)


def join_kernel(own, high, low, out):
    near = iota((128, 128), 1) < 64
    mine = own[...].astype(F32).reshape(128, 128)
    rim = jnp.where(
        near, high[...].astype(F32).reshape(128, 128), low[...].astype(F32).reshape(128, 128)
    )
    both = jnp.concatenate([mine, rim], axis=1).astype(BF)
    row, col = iota((128, 128), 0), iota((128, 128), 1)
    swap = (col == (row % 16) * 8 + row // 16).astype(BF)
    out[...] = dot(swap, both).astype(BF)


def silu_half(h):
    return h + h * jnp.tanh(h)


def net_kernel(
    own, swap_in, swap_out, low2, high2,
    w_first, w_down, w_coarse, w_mid_skip, w_mid_up, w_fine_skip, w_fine_up, w_head,
    out,
    fine_s, pool_fine_s, mid_s, pool_mid_s, coarse_s, up_s, last_s,
):
    gx, gy = lax.axis_index("gx"), lax.axis_index("gy")
    cells_x, cells_y = lax.axis_size("gx") * 2, lax.axis_size("gy") * 32

    def row_flag(cell):
        at = gx * 2 + cell
        return jnp.where((at >= 0) & (at < cells_x), 1.0, 0.0)

    def cell_of(j):
        return jnp.where(j < 40, j, j - J)

    at_y = gy * 32 + cell_of(iota((J, 256), 0))
    y_mask = jnp.where((at_y >= 0) & (at_y < cells_y), 1.0, 0.0)

    odd = gx % 2 == 1
    inner, outer = swap_in[...], swap_out[...]
    flag = jnp.where(odd, 1.0, 0.0).astype(BF)
    keep = jnp.where(odd, 0.0, 1.0).astype(BF)
    low1 = inner * flag + outer * keep
    high1 = inner * keep + outer * flag
    field = jnp.concatenate([low2[...], low1, own[...], high1, high2[...]], axis=0)
    wide = field.astype(F32)
    shifted = [
        pltpu.roll(wide, 1, 1).astype(BF),
        field,
        pltpu.roll(wide, 255, 1).astype(BF),
    ]
    row = iota((4 * J, 256), 0)
    cell = cell_of(row % J)
    y = 4 * cell + row // J
    at_row = gy * 32 + cell
    pick = (
        (iota((4 * J, 256), 1) == (y + 256) % 256) & (at_row >= 0) & (at_row < cells_y)
    ).astype(BF)

    for m in range(-5, 9):
        at = (2 * m + 10) * 16
        window = jnp.concatenate([part[at : at + 64] for part in shifted], axis=0)
        lhs = (dot_nt(pick, window) * row_flag(m // 2)).astype(BF)
        pooled = [jnp.zeros((J, 128), F32) for _ in range(2)]
        for even in range(2):
            x = 2 * m + even
            value = silu_half(dot(lhs, w_first[even])).reshape(4, J, 256)
            for part in range(2):
                both = value[2 * part] + value[2 * part + 1]
                pooled[part] = pooled[part] + both[:, :128] + both[:, 128:]
            if -1 <= x <= 8:
                for group in range(4):
                    fine_s[group + 1, x + 1] = value[group, :32].astype(BF)
                fine_s[0, x + 1] = pltpu.roll(value[3], 1, 0)[:32].astype(BF)
                fine_s[5, x + 1] = pltpu.roll(value[0], J - 1, 0)[:32].astype(BF)
        pool_fine_s[0, m + 5] = pltpu.roll(pooled[1], 1, 0).astype(BF)
        pool_fine_s[1, m + 5] = pooled[0].astype(BF)
        pool_fine_s[2, m + 5] = pooled[1].astype(BF)
        pool_fine_s[3, m + 5] = pltpu.roll(pooled[0], J - 1, 0).astype(BF)

    sums = [jnp.zeros((J, 128), F32) for _ in range(6)]
    for py in range(2):
        lhs = jnp.concatenate(
            [
                pool_fine_s[py + dy, dx : dx + 12].reshape(12 * J, 128)
                for dx in range(3)
                for dy in range(3)
            ],
            axis=1,
        )
        value = silu_half(dot(lhs, w_down[...])).reshape(12, J, 256)
        for at in range(12):
            m = at - 4
            masked = value[at] * (y_mask * row_flag(m // 2))
            sums[at // 2] = sums[at // 2] + masked[:, :128] + masked[:, 128:]
            if -2 <= m <= 5:
                mid_s[py + 1, m + 2] = masked.astype(BF)
                shift = 1 if py else J - 1
                mid_s[0 if py else 3, m + 2] = pltpu.roll(masked, shift, 0).astype(BF)
    for at in range(6):
        pool_mid_s[0, at] = pltpu.roll(sums[at], 1, 0).astype(BF)
        pool_mid_s[1, at] = sums[at].astype(BF)
        pool_mid_s[2, at] = pltpu.roll(sums[at], J - 1, 0).astype(BF)

    lhs = jnp.concatenate(
        [
            pool_mid_s[dy, dx : dx + 4].reshape(4 * J, 128)
            for dx in range(3)
            for dy in range(3)
        ],
        axis=1,
    )
    value = silu_half(dot(lhs, w_coarse[...])).reshape(4, J, 256)
    for at in range(4):
        masked = value[at] * (y_mask * row_flag(at - 1))
        coarse_s[0, at] = pltpu.roll(masked, 1, 0).astype(BF)
        coarse_s[1, at] = masked.astype(BF)
        coarse_s[2, at] = pltpu.roll(masked, J - 1, 0).astype(BF)

    lhs = jnp.concatenate(
        [
            mid_s[dy : dy + 2, dx : dx + 6].reshape(12 * J, 256)
            for dx in range(3)
            for dy in range(3)
        ],
        axis=1,
    )
    skip = dot(lhs, w_mid_skip[...]).reshape(2, 6, J, 256)
    for py in range(2):
        lhs = jnp.concatenate(
            [
                coarse_s[py + ty, tx : tx + 3].reshape(3 * J, 256)
                for tx in range(2)
                for ty in range(2)
            ],
            axis=1,
        )
        for px in range(2):
            up = dot(lhs, w_mid_up[px * 2 + py]).reshape(3, J, 256)
            for k in range(3):
                at = 2 * k if px else 2 * k + 1
                value = silu_half(skip[py, at] + up[k])
                masked = value * (y_mask * row_flag((at - 1) // 2))
                up_s[py + 1, at] = masked[:32].astype(BF)
                shift = 1 if py else J - 1
                up_s[0 if py else 3, at] = pltpu.roll(masked, shift, 0)[:32].astype(BF)

    for py in range(2):
        skip = []
        for half in range(2):
            group = 2 * half + py
            lhs = jnp.concatenate(
                [
                    fine_s[group + dy, dx : dx + 8].reshape(256, 256)
                    for dx in range(3)
                    for dy in range(3)
                ],
                axis=1,
            )
            skip.append(dot(lhs, w_fine_skip[...]).reshape(8, 32, 256))
        for px in range(2):
            lhs = jnp.concatenate(
                [
                    up_s[py + ty : py + ty + 2, px + tx : px + tx + 4].reshape(256, 256)
                    for tx in range(2)
                    for ty in range(2)
                ],
                axis=1,
            )
            up = dot(lhs, w_fine_up[px * 2 + py]).reshape(2, 4, 32, 256)
            for half in range(2):
                group = 2 * half + py
                for k in range(4):
                    x = 2 * k + px
                    value = silu_half(skip[half][x] + up[half, k])
                    last_s[x, pl.ds(group * 32, 32), :] = value.astype(BF)

    heads = jnp.concatenate([dot_nt(w_head[...], last_s[x]) for x in range(8)], axis=0)
    high = heads.astype(BF)
    rest = heads - high.astype(F32)
    low = rest.astype(BF)
    lowest = (rest - low.astype(F32)).astype(BF)
    row, col = iota((128, 128), 0), iota((128, 128), 1)
    order = (col == 4 * (row % 32) + row // 32).astype(BF)
    noise = dot(
        jnp.concatenate([high, low, lowest], axis=1),
        jnp.concatenate([order, order, order], axis=0),
    ).reshape(8, 16, 128)
    for x in range(8):
        out[:, x, :] = noise[x]


def body(
    noisy_field, first_weight, down_weight, coarse_weight, middle_weight, fine_weight, head_weight
):
    def shape(*dims, kind=BF):
        return jax.ShapeDtypeStruct(dims, kind)

    weights = pl.pallas_call(
        weights_kernel,
        out_shape=(
            shape(2, 192, 256),
            shape(1152, 256),
            shape(1152, 256),
            shape(2304, 256),
            shape(4, 1024, 256),
            shape(2304, 256),
            shape(4, 1024, 256),
            shape(16, 256),
        ),
        in_specs=[VMEM] * 6,
        out_specs=(VMEM,) * 8,
        scratch_shapes=[pltpu.VMEM((27, 96, 256), F32)],
        compiler_params=pltpu.CompilerParams(vmem_limit_bytes=32 * 2**20),
        cost_estimate=pl.CostEstimate(
            flops=2 * 10**9, bytes_accessed=9 * 10**6, transcendentals=0
        ),
    )(
        first_weight.transpose(1, 2, 3, 4, 0).reshape(9, 3, 16),
        down_weight.transpose(2, 3, 4, 1, 0).reshape(27, 16, 32),
        coarse_weight.transpose(2, 3, 4, 1, 0).reshape(27, 32, 64),
        middle_weight.transpose(2, 3, 4, 0, 1).reshape(27, 32, 96),
        fine_weight.transpose(2, 3, 4, 0, 1).reshape(27, 16, 48),
        head_weight.reshape(1, 16),
    )

    count = lax.axis_size("gy")
    low = lax.ppermute(noisy_field, "gy", [(i, i + 1) for i in range(count - 1)])
    high = lax.ppermute(noisy_field, "gy", [(i + 1, i) for i in range(count - 1)])
    own = pl.pallas_call(
        join_kernel,
        out_shape=shape(128, 256),
        in_specs=[VMEM] * 3,
        out_specs=VMEM,
    )(noisy_field, high, low)

    count = lax.axis_size("gx")
    inner = [(i, i ^ 1) for i in range(count)]
    outer = [(i, ((i + 1) ^ 1) - 1) for i in range(1, count - 1)]
    swap_in = lax.ppermute(own, "gx", inner)
    swap_out = lax.ppermute(own, "gx", outer)
    low2 = lax.ppermute(own[80:], "gx", [(i, i + 2) for i in range(count - 2)])
    high2 = lax.ppermute(own[:48], "gx", [(i + 2, i) for i in range(count - 2)])

    return pl.pallas_call(
        net_kernel,
        out_shape=shape(16, 8, 128, kind=F32),
        in_specs=[VMEM] * 13,
        out_specs=VMEM,
        scratch_shapes=[
            pltpu.VMEM((6, 10, 32, 256), BF),
            pltpu.VMEM((4, 14, J, 128), BF),
            pltpu.VMEM((4, 8, J, 256), BF),
            pltpu.VMEM((3, 6, J, 128), BF),
            pltpu.VMEM((3, 4, J, 256), BF),
            pltpu.VMEM((4, 6, 32, 256), BF),
            pltpu.VMEM((8, 128, 256), BF),
        ],
        compiler_params=pltpu.CompilerParams(vmem_limit_bytes=40 * 2**20),
        cost_estimate=pl.CostEstimate(
            flops=6 * 10**9, bytes_accessed=9 * 10**6, transcendentals=10**6
        ),
    )(own, swap_in, swap_out, low2, high2, *weights)


def solution(mesh):
    placed = (P(None, "gx", "gy"), P(), P(), P(), P(), P(), P())
    return jax.shard_map(
        body, mesh=mesh, in_specs=placed, out_specs=P(None, "gx", "gy"), check_vma=False
    )
```

```python
import jax
import jax.numpy as jnp
from jax import lax
from jax.experimental import pallas as pl
from jax.experimental.pallas import tpu as pltpu
from jax.sharding import PartitionSpec as P

BF = jnp.bfloat16
F32 = jnp.float32
J = 48
VMEM = pl.BlockSpec(memory_space=pltpu.VMEM)
ANY = pl.BlockSpec(memory_space=pl.ANY)


def dot(a, b):
    return jnp.dot(a, b, preferred_element_type=F32)


def dot_nt(a, b):
    return lax.dot_general(a, b, (((1,), (1,)), ((), ())), preferred_element_type=F32)


def dot_tn(a, b):
    return lax.dot_general(a, b, (((0,), (0,)), ((), ())), preferred_element_type=F32)


def iota(shape, axis):
    return lax.broadcasted_iota(jnp.int32, shape, axis)


def natural(channels):
    return lambda lane: lane // channels


def halves(channels):
    return lambda lane: 2 * ((lane // channels) % (128 // channels)) + lane // 128


def repeat_matrix(channels):
    return (iota((channels, 256), 1) % channels == iota((channels, 256), 0)).astype(BF)


def ones_where(cond):
    return jnp.where(cond, 1.0, 0.0).astype(BF)


def band_masks(rows, depth, depth_of):
    place = depth_of(iota((rows, 256), 1))
    return [ones_where(place == depth + 1 - tap) for tap in range(3)]


def up_masks(rows, depth, depth_of):
    place = depth_of(iota((rows, 256), 1))
    inner = (place == 2 * depth) | (place == 2 * depth + 1)
    outer = (place == 2 * depth + 2) | (place == 2 * depth - 1)
    return ones_where(inner), ones_where(outer)


SETS = (((0,), (1, 2)), ((0, 1), (2,)))


def weights_kernel(*refs):
    raw, refs = refs[:6], refs[6:]
    w_first, w_down, w_coarse, w_mid_skip, w_mid_up, w_fine_skip, w_fine_up, w_head = refs[:8]
    tiled, sems = refs[8], refs[-1]
    first, down, coarse, middle, fine, head = refs[9:15]
    copies = [
        pltpu.make_async_copy(source, target, sems.at[at])
        for at, (source, target) in enumerate(zip(raw, refs[9:15]))
    ]
    for copy in copies:
        copy.start()
    r16, r32, r64 = repeat_matrix(16), repeat_matrix(32), repeat_matrix(64)
    for copy in copies:
        copy.wait()

    w_first[...] = jnp.zeros_like(w_first)
    for dx in range(3):
        rows = [dot(first[dz * 3 + dx], r16) * 0.5 for dz in range(3)]
        place = halves(16)(iota((16, 256), 1))
        depth = iota((16, 256), 0)
        for dy in range(3):
            block = jnp.zeros((16, 256), F32)
            for dz in range(3):
                block = block + jnp.where(place == depth + 1 - dz, rows[dz][dy : dy + 1], 0.0)
            block = block.astype(BF)
            for even in range(2):
                w_first[even, pl.ds(dy * 64 + (even + dx) * 16, 16), :] = block

    def banded(out, taps, channels, row_depths, depth_of):
        size = channels * len(row_depths)
        for at, depth in enumerate(row_depths):
            masks = band_masks(channels, depth, depth_of)
            for xy in range(9):
                block = sum(masks[dz] * taps[dz][xy] for dz in range(3))
                out[pl.ds(xy * size + at * channels, channels), :] = block

    def folded(out, get, channels, depths, depth_of):
        size = channels * depths
        place = depth_of(iota((channels, 256), 1))
        even = place % 2 == 0
        masks = [up_masks(channels, depth, depth_of) for depth in range(depths)]
        for px in range(2):
            for tx in range(2):
                by_y = [
                    [sum(get(dz, dx, dy) for dx in SETS[px][tx]) for dy in range(3)]
                    for dz in range(3)
                ]
                for py in range(2):
                    for ty in range(2):
                        w0, w1, w2 = [
                            sum(by_y[dz][dy] for dy in SETS[py][ty]) for dz in range(3)
                        ]
                        inner = jnp.where(even, w1 + w2, w0 + w1).astype(BF)
                        outer = jnp.where(even, w0, w2).astype(BF)
                        for depth in range(depths):
                            block = masks[depth][0] * inner + masks[depth][1] * outer
                            at = (tx * 2 + ty) * size + depth * channels
                            out[px * 2 + py, pl.ds(at, channels), :] = block

    flat = down[...].reshape(27 * 16, 32)
    all_taps = (dot(flat, r32) * (1 / 16)).astype(BF)
    taps = [[all_taps[(dz * 9 + xy) * 16 : (dz * 9 + xy + 1) * 16] for xy in range(9)] for dz in range(3)]
    banded(w_down, taps, 16, list(range(8)), halves(32))

    flat = coarse[...].reshape(27 * 32, 64)
    all_taps = (dot(flat, r64) * (1 / 16)).astype(BF)
    taps = [[all_taps[(dz * 9 + xy) * 32 : (dz * 9 + xy + 1) * 32] for xy in range(9)] for dz in range(3)]
    banded(w_coarse, taps, 32, list(range(4)), natural(64))

    for tap in range(27):
        tiled[tap] = dot_tn(middle[tap], r32) * 0.5
    taps = [[tiled[dz * 9 + xy, 64:96, :].astype(BF) for xy in range(9)] for dz in range(3)]
    banded(w_mid_skip, taps, 32, [0, 2, 4, 6, 1, 3, 5, 7], natural(32))
    folded(w_mid_up, lambda dz, dx, dy: tiled[dz * 9 + dx * 3 + dy, 0:64, :], 64, 4, natural(32))

    for tap in range(27):
        tiled[tap, 0:48, :] = dot_tn(fine[tap], r16) * 0.5
    taps = [[tiled[dz * 9 + xy, 32:48, :].astype(BF) for xy in range(9)] for dz in range(3)]
    banded(w_fine_skip, taps, 16, list(range(0, 16, 2)) + list(range(1, 16, 2)), natural(16))
    folded(w_fine_up, lambda dz, dx, dy: tiled[dz * 9 + dx * 3 + dy, 0:32, :], 32, 8, natural(16))

    row = dot(jnp.broadcast_to(head[...], (16, 16)), r16)
    w_head[...] = jnp.where(iota((16, 256), 1) // 16 == iota((16, 256), 0), row, 0.0).astype(BF)


def join_kernel(own, high, low, after, out, first_rows, last_rows):
    near = iota((128, 128), 1) < 64
    mine = own[...].astype(F32).reshape(128, 128)
    rim = jnp.where(
        near, high[...].astype(F32).reshape(128, 128), low[...].astype(F32).reshape(128, 128)
    )
    both = jnp.concatenate([mine, rim], axis=1).astype(BF)
    row, col = iota((128, 128), 0), iota((128, 128), 1)
    swap = (col == (row % 16) * 8 + row // 16).astype(BF)
    rows = dot(swap, both).astype(BF)
    out[...] = rows
    first_rows[...] = rows[:48]
    last_rows[...] = rows[80:]


def silu_half(h):
    return h + h * jnp.tanh(h)


def net_kernel(
    own, swap_in, swap_out, low2, high2,
    w_first, w_down, w_coarse, w_mid_skip, w_mid_up, w_fine_skip, w_fine_up, w_head,
    out,
    fine_s, pool_fine_s, mid_s, pool_mid_s, coarse_s, up_s, last_s,
):
    gx, gy = lax.axis_index("gx"), lax.axis_index("gy")
    cells_x, cells_y = lax.axis_size("gx") * 2, lax.axis_size("gy") * 32

    def row_flag(cell):
        at = gx * 2 + cell
        return jnp.where((at >= 0) & (at < cells_x), 1.0, 0.0)

    def cell_of(j):
        return jnp.where(j < 40, j, j - J)

    at_y = gy * 32 + cell_of(iota((J, 256), 0))
    y_mask = jnp.where((at_y >= 0) & (at_y < cells_y), 1.0, 0.0)

    odd = gx % 2 == 1
    inner, outer = swap_in[...], swap_out[...]
    flag = jnp.where(odd, 1.0, 0.0).astype(BF)
    keep = jnp.where(odd, 0.0, 1.0).astype(BF)
    low1 = inner * flag + outer * keep
    high1 = inner * keep + outer * flag
    field = jnp.concatenate([low2[...], low1, own[...], high1, high2[...]], axis=0)
    wide = field.astype(F32)
    shifted = [
        pltpu.roll(wide, 1, 1).astype(BF),
        field,
        pltpu.roll(wide, 255, 1).astype(BF),
    ]
    row = iota((4 * J, 256), 0)
    cell = cell_of(row % J)
    y = 4 * cell + row // J
    at_row = gy * 32 + cell
    pick = (
        (iota((4 * J, 256), 1) == (y + 256) % 256) & (at_row >= 0) & (at_row < cells_y)
    ).astype(BF)

    for m in range(-5, 9):
        at = (2 * m + 10) * 16
        window = jnp.concatenate([part[at : at + 64] for part in shifted], axis=0)
        lhs = (dot_nt(pick, window) * row_flag(m // 2)).astype(BF)
        pooled = [jnp.zeros((J, 128), F32) for _ in range(2)]
        for even in range(2):
            x = 2 * m + even
            value = silu_half(dot(lhs, w_first[even])).reshape(4, J, 256)
            for part in range(2):
                both = value[2 * part] + value[2 * part + 1]
                pooled[part] = pooled[part] + both[:, :128] + both[:, 128:]
            if -1 <= x <= 8:
                for group in range(4):
                    fine_s[group + 1, x + 1] = value[group, :32].astype(BF)
                fine_s[0, x + 1] = pltpu.roll(value[3], 1, 0)[:32].astype(BF)
                fine_s[5, x + 1] = pltpu.roll(value[0], J - 1, 0)[:32].astype(BF)
        pool_fine_s[0, m + 5] = pltpu.roll(pooled[1], 1, 0).astype(BF)
        pool_fine_s[1, m + 5] = pooled[0].astype(BF)
        pool_fine_s[2, m + 5] = pooled[1].astype(BF)
        pool_fine_s[3, m + 5] = pltpu.roll(pooled[0], J - 1, 0).astype(BF)

    sums = [jnp.zeros((J, 128), F32) for _ in range(6)]
    for py in range(2):
        lhs = jnp.concatenate(
            [
                pool_fine_s[py + dy, dx : dx + 12].reshape(12 * J, 128)
                for dx in range(3)
                for dy in range(3)
            ],
            axis=1,
        )
        value = silu_half(dot(lhs, w_down[...])).reshape(12, J, 256)
        for at in range(12):
            m = at - 4
            masked = value[at] * (y_mask * row_flag(m // 2))
            sums[at // 2] = sums[at // 2] + masked[:, :128] + masked[:, 128:]
            if -2 <= m <= 5:
                mid_s[py + 1, m + 2] = masked.astype(BF)
                shift = 1 if py else J - 1
                mid_s[0 if py else 3, m + 2] = pltpu.roll(masked, shift, 0).astype(BF)
    for at in range(6):
        pool_mid_s[0, at] = pltpu.roll(sums[at], 1, 0).astype(BF)
        pool_mid_s[1, at] = sums[at].astype(BF)
        pool_mid_s[2, at] = pltpu.roll(sums[at], J - 1, 0).astype(BF)

    lhs = jnp.concatenate(
        [
            pool_mid_s[dy, dx : dx + 4].reshape(4 * J, 128)
            for dx in range(3)
            for dy in range(3)
        ],
        axis=1,
    )
    value = silu_half(dot(lhs, w_coarse[...])).reshape(4, J, 256)
    for at in range(4):
        masked = value[at] * (y_mask * row_flag(at - 1))
        coarse_s[0, at] = pltpu.roll(masked, 1, 0).astype(BF)
        coarse_s[1, at] = masked.astype(BF)
        coarse_s[2, at] = pltpu.roll(masked, J - 1, 0).astype(BF)

    lhs = jnp.concatenate(
        [
            mid_s[dy : dy + 2, dx : dx + 6].reshape(12 * J, 256)
            for dx in range(3)
            for dy in range(3)
        ],
        axis=1,
    )
    skip = dot(lhs, w_mid_skip[...]).reshape(2, 6, J, 256)
    for py in range(2):
        lhs = jnp.concatenate(
            [
                coarse_s[py + ty, tx : tx + 3].reshape(3 * J, 256)
                for tx in range(2)
                for ty in range(2)
            ],
            axis=1,
        )
        for px in range(2):
            up = dot(lhs, w_mid_up[px * 2 + py]).reshape(3, J, 256)
            for k in range(3):
                at = 2 * k if px else 2 * k + 1
                value = silu_half(skip[py, at] + up[k])
                masked = value * (y_mask * row_flag((at - 1) // 2))
                up_s[py + 1, at] = masked[:32].astype(BF)
                shift = 1 if py else J - 1
                up_s[0 if py else 3, at] = pltpu.roll(masked, shift, 0)[:32].astype(BF)

    for py in range(2):
        skip = []
        for half in range(2):
            group = 2 * half + py
            lhs = jnp.concatenate(
                [
                    fine_s[group + dy, dx : dx + 8].reshape(256, 256)
                    for dx in range(3)
                    for dy in range(3)
                ],
                axis=1,
            )
            skip.append(dot(lhs, w_fine_skip[...]).reshape(8, 32, 256))
        for px in range(2):
            lhs = jnp.concatenate(
                [
                    up_s[py + ty : py + ty + 2, px + tx : px + tx + 4].reshape(256, 256)
                    for tx in range(2)
                    for ty in range(2)
                ],
                axis=1,
            )
            up = dot(lhs, w_fine_up[px * 2 + py]).reshape(2, 4, 32, 256)
            for half in range(2):
                group = 2 * half + py
                for k in range(4):
                    x = 2 * k + px
                    value = silu_half(skip[half][x] + up[half, k])
                    last_s[x, pl.ds(group * 32, 32), :] = value.astype(BF)

    heads = jnp.concatenate([dot_nt(w_head[...], last_s[x]) for x in range(8)], axis=0)
    high = heads.astype(BF)
    rest = heads - high.astype(F32)
    low = rest.astype(BF)
    lowest = (rest - low.astype(F32)).astype(BF)
    row, col = iota((128, 128), 0), iota((128, 128), 1)
    order = (col == 4 * (row % 32) + row // 32).astype(BF)
    noise = dot(
        jnp.concatenate([high, low, lowest], axis=1),
        jnp.concatenate([order, order, order], axis=0),
    ).reshape(8, 16, 128)
    for x in range(8):
        out[:, x, :] = noise[x]


def body(
    noisy_field, first_weight, down_weight, coarse_weight, middle_weight, fine_weight, head_weight
):
    def shape(*dims, kind=BF):
        return jax.ShapeDtypeStruct(dims, kind)

    weights = pl.pallas_call(
        weights_kernel,
        out_shape=(
            shape(2, 192, 256),
            shape(1152, 256),
            shape(1152, 256),
            shape(2304, 256),
            shape(4, 1024, 256),
            shape(2304, 256),
            shape(4, 1024, 256),
            shape(16, 256),
        ),
        in_specs=[ANY] * 6,
        out_specs=(VMEM,) * 8,
        scratch_shapes=[
            pltpu.VMEM((27, 96, 256), F32),
            pltpu.VMEM((9, 3, 16), BF),
            pltpu.VMEM((27, 16, 32), BF),
            pltpu.VMEM((27, 32, 64), BF),
            pltpu.VMEM((27, 32, 96), BF),
            pltpu.VMEM((27, 16, 48), BF),
            pltpu.VMEM((1, 16), BF),
            pltpu.SemaphoreType.DMA((6,)),
        ],
        compiler_params=pltpu.CompilerParams(vmem_limit_bytes=32 * 2**20),
        cost_estimate=pl.CostEstimate(
            flops=2 * 10**9, bytes_accessed=9 * 10**6, transcendentals=0
        ),
    )(
        *(
            pltpu.with_memory_space_constraint(weight, pltpu.HBM)
            for weight in (
                first_weight.transpose(1, 2, 3, 4, 0).reshape(9, 3, 16),
                down_weight.transpose(2, 3, 4, 1, 0).reshape(27, 16, 32),
                coarse_weight.transpose(2, 3, 4, 1, 0).reshape(27, 32, 64),
                middle_weight.transpose(2, 3, 4, 0, 1).reshape(27, 32, 96),
                fine_weight.transpose(2, 3, 4, 0, 1).reshape(27, 16, 48),
                head_weight.reshape(1, 16),
            )
        )
    )

    count = lax.axis_size("gy")
    low = lax.ppermute(noisy_field, "gy", [(i, i + 1) for i in range(count - 1)])
    high = lax.ppermute(noisy_field, "gy", [(i + 1, i) for i in range(count - 1)])
    own, first_rows, last_rows = pl.pallas_call(
        join_kernel,
        out_shape=(shape(128, 256), shape(48, 256), shape(48, 256)),
        in_specs=[VMEM] * 3 + [ANY],
        out_specs=(VMEM,) * 3,
        compiler_params=pltpu.CompilerParams(vmem_limit_bytes=4 * 2**20),
        cost_estimate=pl.CostEstimate(flops=10**7, bytes_accessed=2 * 10**5, transcendentals=0),
    )(noisy_field, high, low, weights[-1])

    count = lax.axis_size("gx")
    inner = [(i, i ^ 1) for i in range(count)]
    outer = [(i, ((i + 1) ^ 1) - 1) for i in range(1, count - 1)]
    swap_in = lax.ppermute(own, "gx", inner)
    swap_out = lax.ppermute(own, "gx", outer)
    low2 = lax.ppermute(last_rows, "gx", [(i, i + 2) for i in range(count - 2)])
    high2 = lax.ppermute(first_rows, "gx", [(i + 2, i) for i in range(count - 2)])

    return pl.pallas_call(
        net_kernel,
        out_shape=shape(16, 8, 128, kind=F32),
        in_specs=[VMEM] * 13,
        out_specs=VMEM,
        scratch_shapes=[
            pltpu.VMEM((6, 10, 32, 256), BF),
            pltpu.VMEM((4, 14, J, 128), BF),
            pltpu.VMEM((4, 8, J, 256), BF),
            pltpu.VMEM((3, 6, J, 128), BF),
            pltpu.VMEM((3, 4, J, 256), BF),
            pltpu.VMEM((4, 6, 32, 256), BF),
            pltpu.VMEM((8, 128, 256), BF),
        ],
        compiler_params=pltpu.CompilerParams(vmem_limit_bytes=40 * 2**20),
        cost_estimate=pl.CostEstimate(
            flops=6 * 10**9, bytes_accessed=9 * 10**6, transcendentals=10**6
        ),
    )(own, swap_in, swap_out, low2, high2, *weights)


def solution(mesh):
    placed = (P(None, "gx", "gy"), P(), P(), P(), P(), P(), P())
    return jax.shard_map(
        body, mesh=mesh, in_specs=placed, out_specs=P(None, "gx", "gy"), check_vma=False
    )
```

```python
import jax
import jax.numpy as jnp
from jax import lax
from jax.experimental import pallas as pl
from jax.experimental.pallas import tpu as pltpu
from jax.sharding import PartitionSpec as P

BF = jnp.bfloat16
F32 = jnp.float32
J = 48
VMEM = pl.BlockSpec(memory_space=pltpu.VMEM)
ANY = pl.BlockSpec(memory_space=pl.ANY)


def dot(a, b):
    return jnp.dot(a, b, preferred_element_type=F32)


def dot_nt(a, b):
    return lax.dot_general(a, b, (((1,), (1,)), ((), ())), preferred_element_type=F32)


def dot_tn(a, b):
    return lax.dot_general(a, b, (((0,), (0,)), ((), ())), preferred_element_type=F32)


def iota(shape, axis):
    return lax.broadcasted_iota(jnp.int32, shape, axis)


def natural(channels):
    return lambda lane: lane // channels


def halves(channels):
    return lambda lane: 2 * ((lane // channels) % (128 // channels)) + lane // 128


def repeat_matrix(channels):
    return (iota((channels, 256), 1) % channels == iota((channels, 256), 0)).astype(BF)


def ones_where(cond):
    return jnp.where(cond, 1.0, 0.0).astype(BF)


def band_masks(rows, depth, depth_of):
    place = depth_of(iota((rows, 256), 1))
    return [ones_where(place == depth + 1 - tap) for tap in range(3)]


def up_masks(rows, depth, depth_of):
    place = depth_of(iota((rows, 256), 1))
    inner = (place == 2 * depth) | (place == 2 * depth + 1)
    outer = (place == 2 * depth + 2) | (place == 2 * depth - 1)
    return ones_where(inner), ones_where(outer)


SETS = (((0,), (1, 2)), ((0, 1), (2,)))


def banded(out, taps, channels, row_depths, depth_of):
    size = channels * len(row_depths)
    for at, depth in enumerate(row_depths):
        masks = band_masks(channels, depth, depth_of)
        for xy in range(9):
            block = sum(masks[dz] * taps[dz][xy] for dz in range(3))
            out[pl.ds(xy * size + at * channels, channels), :] = block


def folded(out, get, channels, depths, depth_of):
    size = channels * depths
    place = depth_of(iota((channels, 256), 1))
    even = place % 2 == 0
    masks = [up_masks(channels, depth, depth_of) for depth in range(depths)]
    for px in range(2):
        for tx in range(2):
            by_y = [
                [sum(get(dz, dx, dy) for dx in SETS[px][tx]) for dy in range(3)]
                for dz in range(3)
            ]
            for py in range(2):
                for ty in range(2):
                    w0, w1, w2 = [
                        sum(by_y[dz][dy] for dy in SETS[py][ty]) for dz in range(3)
                    ]
                    inner = jnp.where(even, w1 + w2, w0 + w1).astype(BF)
                    outer = jnp.where(even, w0, w2).astype(BF)
                    for depth in range(depths):
                        block = masks[depth][0] * inner + masks[depth][1] * outer
                        at = (tx * 2 + ty) * size + depth * channels
                        out[px * 2 + py, pl.ds(at, channels), :] = block


def encoder_weights_kernel(
    raw_first, raw_down, raw_coarse, raw_middle, raw_fine, raw_head,
    w_first, w_down, w_coarse, w_head, middle, fine,
    first, down, coarse, head, sems,
):
    copies = [
        pltpu.make_async_copy(source, target, sems.at[at])
        for at, (source, target) in enumerate(
            (
                (raw_first, first),
                (raw_down, down),
                (raw_coarse, coarse),
                (raw_head, head),
                (raw_middle, middle),
                (raw_fine, fine),
            )
        )
    ]
    for copy in copies:
        copy.start()
    r16, r32, r64 = repeat_matrix(16), repeat_matrix(32), repeat_matrix(64)
    for copy in copies[:4]:
        copy.wait()

    w_first[...] = jnp.zeros_like(w_first)
    for dx in range(3):
        rows = [dot(first[dz * 3 + dx], r16) * 0.5 for dz in range(3)]
        place = halves(16)(iota((16, 256), 1))
        depth = iota((16, 256), 0)
        for dy in range(3):
            block = jnp.zeros((16, 256), F32)
            for dz in range(3):
                block = block + jnp.where(place == depth + 1 - dz, rows[dz][dy : dy + 1], 0.0)
            block = block.astype(BF)
            for even in range(2):
                w_first[even, pl.ds(dy * 64 + (even + dx) * 16, 16), :] = block

    flat = down[...].reshape(27 * 16, 32)
    all_taps = (dot(flat, r32) * (1 / 16)).astype(BF)
    taps = [[all_taps[(dz * 9 + xy) * 16 : (dz * 9 + xy + 1) * 16] for xy in range(9)] for dz in range(3)]
    banded(w_down, taps, 16, list(range(8)), halves(32))

    flat = coarse[...].reshape(27 * 32, 64)
    all_taps = (dot(flat, r64) * (1 / 16)).astype(BF)
    taps = [[all_taps[(dz * 9 + xy) * 32 : (dz * 9 + xy + 1) * 32] for xy in range(9)] for dz in range(3)]
    banded(w_coarse, taps, 32, list(range(4)), natural(64))

    row = dot(jnp.broadcast_to(head[...], (16, 16)), r16)
    w_head[...] = jnp.where(iota((16, 256), 1) // 16 == iota((16, 256), 0), row, 0.0).astype(BF)
    for copy in copies[4:]:
        copy.wait()


def decoder_weights_kernel(
    middle, fine, after, w_mid_skip, w_mid_up, w_fine_skip, w_fine_up, tiled
):
    r16, r32 = repeat_matrix(16), repeat_matrix(32)
    for tap in range(27):
        tiled[tap] = dot_tn(middle[tap], r32) * 0.5
    taps = [[tiled[dz * 9 + xy, 64:96, :].astype(BF) for xy in range(9)] for dz in range(3)]
    banded(w_mid_skip, taps, 32, [0, 2, 4, 6, 1, 3, 5, 7], natural(32))
    folded(w_mid_up, lambda dz, dx, dy: tiled[dz * 9 + dx * 3 + dy, 0:64, :], 64, 4, natural(32))

    for tap in range(27):
        tiled[tap, 0:48, :] = dot_tn(fine[tap], r16) * 0.5
    taps = [[tiled[dz * 9 + xy, 32:48, :].astype(BF) for xy in range(9)] for dz in range(3)]
    banded(w_fine_skip, taps, 16, list(range(0, 16, 2)) + list(range(1, 16, 2)), natural(16))
    folded(w_fine_up, lambda dz, dx, dy: tiled[dz * 9 + dx * 3 + dy, 0:32, :], 32, 8, natural(16))


def join_kernel(own, high, low, after, out):
    near = iota((128, 128), 1) < 64
    mine = own[...].astype(F32).reshape(128, 128)
    rim = jnp.where(
        near, high[...].astype(F32).reshape(128, 128), low[...].astype(F32).reshape(128, 128)
    )
    both = jnp.concatenate([mine, rim], axis=1).astype(BF)
    row, col = iota((128, 128), 0), iota((128, 128), 1)
    swap = (col == (row % 16) * 8 + row // 16).astype(BF)
    out[...] = dot(swap, both).astype(BF)


def chip_edge_kernel(own, twin, out):
    odd = lax.axis_index("gx") % 2 == 1
    for_high = jnp.concatenate([twin[80:], own[...]], axis=0)
    for_low = jnp.concatenate([own[...], twin[:48]], axis=0)
    out[...] = jnp.where(odd, for_high, for_low)


def twin_edge_kernel(edge, after, out):
    odd = lax.axis_index("gx") % 2 == 1
    out[...] = jnp.where(odd, edge[:48], edge[128:])


def silu_half(h):
    return h + h * jnp.tanh(h)


def net_kernel(
    own, twin, chip_edge, twin_edge,
    w_first, w_down, w_coarse, w_mid_skip, w_mid_up, w_fine_skip, w_fine_up, w_head,
    out,
    fine_s, pool_fine_s, mid_s, pool_mid_s, coarse_s, up_s, last_s,
):
    gx, gy = lax.axis_index("gx"), lax.axis_index("gy")
    cells_x, cells_y = lax.axis_size("gx") * 2, lax.axis_size("gy") * 32

    def row_flag(cell):
        at = gx * 2 + cell
        return jnp.where((at >= 0) & (at < cells_x), 1.0, 0.0)

    def cell_of(j):
        return jnp.where(j < 40, j, j - J)

    at_y = gy * 32 + cell_of(iota((J, 256), 0))
    y_mask = jnp.where((at_y >= 0) & (at_y < cells_y), 1.0, 0.0)

    mine, other, edge, rest = own[...], twin[...], chip_edge[...], twin_edge[...]
    field = jnp.where(
        gx % 2 == 1,
        jnp.concatenate([rest, other, mine, edge], axis=0),
        jnp.concatenate([edge, mine, other, rest], axis=0),
    )
    wide = field.astype(F32)
    shifted = [
        pltpu.roll(wide, 1, 1).astype(BF),
        field,
        pltpu.roll(wide, 255, 1).astype(BF),
    ]
    row = iota((4 * J, 256), 0)
    cell = cell_of(row % J)
    y = 4 * cell + row // J
    at_row = gy * 32 + cell
    pick = (
        (iota((4 * J, 256), 1) == (y + 256) % 256) & (at_row >= 0) & (at_row < cells_y)
    ).astype(BF)

    for m in range(-5, 9):
        at = (2 * m + 10) * 16
        window = jnp.concatenate([part[at : at + 64] for part in shifted], axis=0)
        lhs = (dot_nt(pick, window) * row_flag(m // 2)).astype(BF)
        pooled = [jnp.zeros((J, 128), F32) for _ in range(2)]
        for even in range(2):
            x = 2 * m + even
            value = silu_half(dot(lhs, w_first[even])).reshape(4, J, 256)
            for part in range(2):
                both = value[2 * part] + value[2 * part + 1]
                pooled[part] = pooled[part] + both[:, :128] + both[:, 128:]
            if -1 <= x <= 8:
                for group in range(4):
                    fine_s[group + 1, x + 1] = value[group, :32].astype(BF)
                fine_s[0, x + 1] = pltpu.roll(value[3], 1, 0)[:32].astype(BF)
                fine_s[5, x + 1] = pltpu.roll(value[0], J - 1, 0)[:32].astype(BF)
        pool_fine_s[0, m + 5] = pltpu.roll(pooled[1], 1, 0).astype(BF)
        pool_fine_s[1, m + 5] = pooled[0].astype(BF)
        pool_fine_s[2, m + 5] = pooled[1].astype(BF)
        pool_fine_s[3, m + 5] = pltpu.roll(pooled[0], J - 1, 0).astype(BF)

    sums = [jnp.zeros((J, 128), F32) for _ in range(6)]
    for py in range(2):
        lhs = jnp.concatenate(
            [
                pool_fine_s[py + dy, dx : dx + 12].reshape(12 * J, 128)
                for dx in range(3)
                for dy in range(3)
            ],
            axis=1,
        )
        value = silu_half(dot(lhs, w_down[...])).reshape(12, J, 256)
        for at in range(12):
            m = at - 4
            masked = value[at] * (y_mask * row_flag(m // 2))
            sums[at // 2] = sums[at // 2] + masked[:, :128] + masked[:, 128:]
            if -2 <= m <= 5:
                mid_s[py + 1, m + 2] = masked.astype(BF)
                shift = 1 if py else J - 1
                mid_s[0 if py else 3, m + 2] = pltpu.roll(masked, shift, 0).astype(BF)
    for at in range(6):
        pool_mid_s[0, at] = pltpu.roll(sums[at], 1, 0).astype(BF)
        pool_mid_s[1, at] = sums[at].astype(BF)
        pool_mid_s[2, at] = pltpu.roll(sums[at], J - 1, 0).astype(BF)

    lhs = jnp.concatenate(
        [
            pool_mid_s[dy, dx : dx + 4].reshape(4 * J, 128)
            for dx in range(3)
            for dy in range(3)
        ],
        axis=1,
    )
    value = silu_half(dot(lhs, w_coarse[...])).reshape(4, J, 256)
    for at in range(4):
        masked = value[at] * (y_mask * row_flag(at - 1))
        coarse_s[0, at] = pltpu.roll(masked, 1, 0).astype(BF)
        coarse_s[1, at] = masked.astype(BF)
        coarse_s[2, at] = pltpu.roll(masked, J - 1, 0).astype(BF)

    lhs = jnp.concatenate(
        [
            mid_s[dy : dy + 2, dx : dx + 6].reshape(12 * J, 256)
            for dx in range(3)
            for dy in range(3)
        ],
        axis=1,
    )
    skip = dot(lhs, w_mid_skip[...]).reshape(2, 6, J, 256)
    for py in range(2):
        lhs = jnp.concatenate(
            [
                coarse_s[py + ty, tx : tx + 3].reshape(3 * J, 256)
                for tx in range(2)
                for ty in range(2)
            ],
            axis=1,
        )
        for px in range(2):
            up = dot(lhs, w_mid_up[px * 2 + py]).reshape(3, J, 256)
            for k in range(3):
                at = 2 * k if px else 2 * k + 1
                value = silu_half(skip[py, at] + up[k])
                masked = value * (y_mask * row_flag((at - 1) // 2))
                up_s[py + 1, at] = masked[:32].astype(BF)
                shift = 1 if py else J - 1
                up_s[0 if py else 3, at] = pltpu.roll(masked, shift, 0)[:32].astype(BF)

    for py in range(2):
        skip = []
        for half in range(2):
            group = 2 * half + py
            lhs = jnp.concatenate(
                [
                    fine_s[group + dy, dx : dx + 8].reshape(256, 256)
                    for dx in range(3)
                    for dy in range(3)
                ],
                axis=1,
            )
            skip.append(dot(lhs, w_fine_skip[...]).reshape(8, 32, 256))
        for px in range(2):
            lhs = jnp.concatenate(
                [
                    up_s[py + ty : py + ty + 2, px + tx : px + tx + 4].reshape(256, 256)
                    for tx in range(2)
                    for ty in range(2)
                ],
                axis=1,
            )
            up = dot(lhs, w_fine_up[px * 2 + py]).reshape(2, 4, 32, 256)
            for half in range(2):
                group = 2 * half + py
                for k in range(4):
                    x = 2 * k + px
                    value = silu_half(skip[half][x] + up[half, k])
                    last_s[x, pl.ds(group * 32, 32), :] = value.astype(BF)

    heads = jnp.concatenate([dot_nt(w_head[...], last_s[x]) for x in range(8)], axis=0)
    high = heads.astype(BF)
    rest = heads - high.astype(F32)
    low = rest.astype(BF)
    lowest = (rest - low.astype(F32)).astype(BF)
    row, col = iota((128, 128), 0), iota((128, 128), 1)
    order = (col == 4 * (row % 32) + row // 32).astype(BF)
    noise = dot(
        jnp.concatenate([high, low, lowest], axis=1),
        jnp.concatenate([order, order, order], axis=0),
    ).reshape(8, 16, 128)
    for x in range(8):
        out[:, x, :] = noise[x]


def body(
    noisy_field, first_weight, down_weight, coarse_weight, middle_weight, fine_weight, head_weight
):
    def shape(*dims, kind=BF):
        return jax.ShapeDtypeStruct(dims, kind)

    def cost(flops, moved):
        return pl.CostEstimate(flops=flops, bytes_accessed=moved, transcendentals=0)

    def small(limit):
        return pltpu.CompilerParams(vmem_limit_bytes=limit * 2**20)

    w_first, w_down, w_coarse, w_head, middle, fine = pl.pallas_call(
        encoder_weights_kernel,
        out_shape=(
            shape(2, 192, 256),
            shape(1152, 256),
            shape(1152, 256),
            shape(16, 256),
            shape(27, 32, 96),
            shape(27, 16, 48),
        ),
        in_specs=[ANY] * 6,
        out_specs=(VMEM,) * 6,
        scratch_shapes=[
            pltpu.VMEM((9, 3, 16), BF),
            pltpu.VMEM((27, 16, 32), BF),
            pltpu.VMEM((27, 32, 64), BF),
            pltpu.VMEM((1, 16), BF),
            pltpu.SemaphoreType.DMA((6,)),
        ],
        compiler_params=small(16),
        cost_estimate=cost(10**9, 3 * 10**6),
    )(
        *(
            pltpu.with_memory_space_constraint(weight, pltpu.HBM)
            for weight in (
                first_weight.transpose(1, 2, 3, 4, 0).reshape(9, 3, 16),
                down_weight.transpose(2, 3, 4, 1, 0).reshape(27, 16, 32),
                coarse_weight.transpose(2, 3, 4, 1, 0).reshape(27, 32, 64),
                middle_weight.transpose(2, 3, 4, 0, 1).reshape(27, 32, 96),
                fine_weight.transpose(2, 3, 4, 0, 1).reshape(27, 16, 48),
                head_weight.reshape(1, 16),
            )
        )
    )

    count = lax.axis_size("gy")
    low = lax.ppermute(noisy_field, "gy", [(i, i + 1) for i in range(count - 1)])
    high = lax.ppermute(noisy_field, "gy", [(i + 1, i) for i in range(count - 1)])
    own = pl.pallas_call(
        join_kernel,
        out_shape=shape(128, 256),
        in_specs=[VMEM] * 3 + [ANY],
        out_specs=VMEM,
        compiler_params=small(4),
        cost_estimate=cost(10**7, 2 * 10**5),
    )(noisy_field, high, low, w_head)

    count = lax.axis_size("gx")
    in_chip = [(i, i ^ 1) for i in range(count)]
    between = [(i, ((i + 1) ^ 1) - 1) for i in range(1, count - 1)]
    twin = lax.ppermute(own, "gx", in_chip)
    edge = pl.pallas_call(
        chip_edge_kernel,
        out_shape=shape(176, 256),
        in_specs=[VMEM] * 2,
        out_specs=VMEM,
        compiler_params=small(4),
        cost_estimate=cost(10**5, 3 * 10**5),
    )(own, twin)
    chip_edge = lax.ppermute(edge, "gx", between)
    decoder_weights = pl.pallas_call(
        decoder_weights_kernel,
        out_shape=(
            shape(2304, 256),
            shape(4, 1024, 256),
            shape(2304, 256),
            shape(4, 1024, 256),
        ),
        in_specs=[VMEM] * 2 + [ANY],
        out_specs=(VMEM,) * 4,
        scratch_shapes=[pltpu.VMEM((27, 96, 256), F32)],
        compiler_params=small(24),
        cost_estimate=cost(2 * 10**9, 9 * 10**6),
    )(middle, fine, edge)
    rest = pl.pallas_call(
        twin_edge_kernel,
        out_shape=shape(48, 256),
        in_specs=[VMEM, ANY],
        out_specs=VMEM,
        compiler_params=small(4),
        cost_estimate=cost(10**5, 10**5),
    )(chip_edge, decoder_weights[0])
    twin_edge = lax.ppermute(rest, "gx", in_chip)

    return pl.pallas_call(
        net_kernel,
        out_shape=shape(16, 8, 128, kind=F32),
        in_specs=[VMEM] * 12,
        out_specs=VMEM,
        scratch_shapes=[
            pltpu.VMEM((6, 10, 32, 256), BF),
            pltpu.VMEM((4, 14, J, 128), BF),
            pltpu.VMEM((4, 8, J, 256), BF),
            pltpu.VMEM((3, 6, J, 128), BF),
            pltpu.VMEM((3, 4, J, 256), BF),
            pltpu.VMEM((4, 6, 32, 256), BF),
            pltpu.VMEM((8, 128, 256), BF),
        ],
        compiler_params=small(40),
        cost_estimate=pl.CostEstimate(
            flops=6 * 10**9, bytes_accessed=9 * 10**6, transcendentals=10**6
        ),
    )(own, twin, chip_edge, twin_edge, w_first, w_down, w_coarse, *decoder_weights, w_head)


def solution(mesh):
    placed = (P(None, "gx", "gy"), P(), P(), P(), P(), P(), P())
    return jax.shard_map(
        body, mesh=mesh, in_specs=placed, out_specs=P(None, "gx", "gy"), check_vma=False
    )
```

```python
import jax
import jax.numpy as jnp
from jax import lax
from jax.experimental import pallas as pl
from jax.experimental.pallas import tpu as pltpu
from jax.sharding import PartitionSpec as P

BF = jnp.bfloat16
F32 = jnp.float32
J = 48
VMEM = pl.BlockSpec(memory_space=pltpu.VMEM)
ANY = pl.BlockSpec(memory_space=pl.ANY)


def dot(a, b):
    return jnp.dot(a, b, preferred_element_type=F32)


def dot_nt(a, b):
    return lax.dot_general(a, b, (((1,), (1,)), ((), ())), preferred_element_type=F32)


def dot_tn(a, b):
    return lax.dot_general(a, b, (((0,), (0,)), ((), ())), preferred_element_type=F32)


def iota(shape, axis):
    return lax.broadcasted_iota(jnp.int32, shape, axis)


def natural(channels):
    return lambda lane: lane // channels


def halves(channels):
    return lambda lane: 2 * ((lane // channels) % (128 // channels)) + lane // 128


def repeat_matrix(channels):
    return (iota((channels, 256), 1) % channels == iota((channels, 256), 0)).astype(BF)


def ones_where(cond):
    return jnp.where(cond, 1.0, 0.0).astype(BF)


def band_masks(rows, depth, depth_of):
    place = depth_of(iota((rows, 256), 1))
    return [ones_where(place == depth + 1 - tap) for tap in range(3)]


def up_masks(rows, depth, depth_of):
    place = depth_of(iota((rows, 256), 1))
    inner = (place == 2 * depth) | (place == 2 * depth + 1)
    outer = (place == 2 * depth + 2) | (place == 2 * depth - 1)
    return ones_where(inner), ones_where(outer)


def cell_of(j):
    return jnp.where(j < 40, j, j - J)


def cell_inside(axis, held, cell):
    at = lax.axis_index(axis) * held + cell
    return (at >= 0) & (at < lax.axis_size(axis) * held)


SETS = (((0,), (1, 2)), ((0, 1), (2,)))


def banded(out, taps, channels, row_depths, depth_of):
    size = channels * len(row_depths)
    for at, depth in enumerate(row_depths):
        masks = band_masks(channels, depth, depth_of)
        for xy in range(9):
            block = sum(masks[dz] * taps[dz][xy] for dz in range(3))
            out[pl.ds(xy * size + at * channels, channels), :] = block


def folded(out, get, channels, depths, depth_of):
    size = channels * depths
    place = depth_of(iota((channels, 256), 1))
    even = place % 2 == 0
    masks = [up_masks(channels, depth, depth_of) for depth in range(depths)]
    for px in range(2):
        for tx in range(2):
            by_y = [
                [sum(get(dz, dx, dy) for dx in SETS[px][tx]) for dy in range(3)]
                for dz in range(3)
            ]
            for py in range(2):
                for ty in range(2):
                    w0, w1, w2 = [
                        sum(by_y[dz][dy] for dy in SETS[py][ty]) for dz in range(3)
                    ]
                    inner = jnp.where(even, w1 + w2, w0 + w1).astype(BF)
                    outer = jnp.where(even, w0, w2).astype(BF)
                    for depth in range(depths):
                        block = masks[depth][0] * inner + masks[depth][1] * outer
                        at = (tx * 2 + ty) * size + depth * channels
                        out[px * 2 + py, pl.ds(at, channels), :] = block


def encoder_weights_kernel(
    raw_first, raw_down, raw_coarse, raw_middle, raw_fine, raw_head,
    w_first, w_down, w_coarse, w_head, middle, fine, pick,
    first, down, coarse, head, sems,
):
    copies = [
        pltpu.make_async_copy(source, target, sems.at[at])
        for at, (source, target) in enumerate(
            (
                (raw_first, first),
                (raw_down, down),
                (raw_coarse, coarse),
                (raw_head, head),
                (raw_middle, middle),
                (raw_fine, fine),
            )
        )
    ]
    for copy in copies:
        copy.start()
    r16, r32, r64 = repeat_matrix(16), repeat_matrix(32), repeat_matrix(64)
    row = iota((4 * J, 256), 0)
    cell = cell_of(row % J)
    inside = cell_inside("gy", 32, cell)
    pick[...] = ((iota((4 * J, 256), 1) == (4 * cell + row // J + 256) % 256) & inside).astype(BF)
    for copy in copies[:4]:
        copy.wait()

    w_first[...] = jnp.zeros_like(w_first)
    for dx in range(3):
        rows = [dot(first[dz * 3 + dx], r16) * 0.5 for dz in range(3)]
        place = halves(16)(iota((16, 256), 1))
        depth = iota((16, 256), 0)
        for dy in range(3):
            block = jnp.zeros((16, 256), F32)
            for dz in range(3):
                block = block + jnp.where(place == depth + 1 - dz, rows[dz][dy : dy + 1], 0.0)
            block = block.astype(BF)
            for even in range(2):
                w_first[even, pl.ds(dy * 64 + (even + dx) * 16, 16), :] = block

    flat = down[...].reshape(27 * 16, 32)
    all_taps = (dot(flat, r32) * (1 / 16)).astype(BF)
    taps = [[all_taps[(dz * 9 + xy) * 16 : (dz * 9 + xy + 1) * 16] for xy in range(9)] for dz in range(3)]
    banded(w_down, taps, 16, list(range(8)), halves(32))

    flat = coarse[...].reshape(27 * 32, 64)
    all_taps = (dot(flat, r64) * (1 / 16)).astype(BF)
    taps = [[all_taps[(dz * 9 + xy) * 32 : (dz * 9 + xy + 1) * 32] for xy in range(9)] for dz in range(3)]
    banded(w_coarse, taps, 32, list(range(4)), natural(64))

    row = dot(jnp.broadcast_to(head[...], (16, 16)), r16)
    w_head[...] = jnp.where(iota((16, 256), 1) // 16 == iota((16, 256), 0), row, 0.0).astype(BF)
    for copy in copies[4:]:
        copy.wait()


def mid_weights_kernel(middle, after, w_mid_skip, w_mid_up, tiled):
    r32 = repeat_matrix(32)
    for tap in range(27):
        tiled[tap] = dot_tn(middle[tap], r32) * 0.5
    taps = [[tiled[dz * 9 + xy, 64:96, :].astype(BF) for xy in range(9)] for dz in range(3)]
    banded(w_mid_skip, taps, 32, [0, 2, 4, 6, 1, 3, 5, 7], natural(32))
    folded(w_mid_up, lambda dz, dx, dy: tiled[dz * 9 + dx * 3 + dy, 0:64, :], 64, 4, natural(32))


def fine_weights_kernel(fine, after, w_fine_skip, w_fine_up, tiled):
    r16 = repeat_matrix(16)
    for tap in range(27):
        tiled[tap] = dot_tn(fine[tap], r16) * 0.5
    taps = [[tiled[dz * 9 + xy, 32:48, :].astype(BF) for xy in range(9)] for dz in range(3)]
    banded(w_fine_skip, taps, 16, list(range(0, 16, 2)) + list(range(1, 16, 2)), natural(16))
    folded(w_fine_up, lambda dz, dx, dy: tiled[dz * 9 + dx * 3 + dy, 0:32, :], 32, 8, natural(16))


def join_kernel(own, high, low, after, out):
    near = iota((128, 128), 1) < 64
    mine = own[...].astype(F32).reshape(128, 128)
    rim = jnp.where(
        near, high[...].astype(F32).reshape(128, 128), low[...].astype(F32).reshape(128, 128)
    )
    both = jnp.concatenate([mine, rim], axis=1).astype(BF)
    row, col = iota((128, 128), 0), iota((128, 128), 1)
    swap = (col == (row % 16) * 8 + row // 16).astype(BF)
    out[...] = dot(swap, both).astype(BF)


def chip_edge_kernel(own, twin, after, out):
    odd = lax.axis_index("gx") % 2 == 1
    for_high = jnp.concatenate([twin[80:], own[...]], axis=0)
    for_low = jnp.concatenate([own[...], twin[:48]], axis=0)
    out[...] = jnp.where(odd, for_high, for_low)


def twin_edge_kernel(edge, after, also_after, out):
    odd = lax.axis_index("gx") % 2 == 1
    out[...] = jnp.where(odd, edge[:48], edge[128:])


def silu_half(h):
    return h + h * jnp.tanh(h)


def row_flag(cell):
    return jnp.where(cell_inside("gx", 2, cell), 1.0, 0.0)


def encode(field, pick, w_first, first_pair, pairs, put_fine, put_pooled):
    wide = field.astype(F32)
    shifted = [pltpu.roll(wide, 1, 1).astype(BF), field, pltpu.roll(wide, 255, 1).astype(BF)]
    for at in range(pairs):
        m = first_pair + at
        window = jnp.concatenate([part[at * 32 : at * 32 + 64] for part in shifted], axis=0)
        flag = row_flag(lax.shift_right_arithmetic(m, 1) if put_fine is None else m // 2)
        lhs = (dot_nt(pick[...], window) * flag).astype(BF)
        pooled = [jnp.zeros((J, 128), F32) for _ in range(2)]
        for even in range(2):
            value = silu_half(dot(lhs, w_first[even])).reshape(4, J, 256)
            for part in range(2):
                both = value[2 * part] + value[2 * part + 1]
                pooled[part] = pooled[part] + both[:, :128] + both[:, 128:]
            if put_fine is not None and -1 <= 2 * m + even <= 8:
                for group in range(4):
                    put_fine(group + 1, 2 * m + even, value[group, :32])
                put_fine(0, 2 * m + even, pltpu.roll(value[3], 1, 0)[:32])
                put_fine(5, 2 * m + even, pltpu.roll(value[0], J - 1, 0)[:32])
        put_pooled(0, at, pltpu.roll(pooled[1], 1, 0))
        put_pooled(1, at, pooled[0])
        put_pooled(2, at, pooled[1])
        put_pooled(3, at, pltpu.roll(pooled[0], J - 1, 0))


def for_each_core(work):
    odd = lax.axis_index("gx") % 2

    @pl.when(odd == 0)
    def _():
        work(0)

    @pl.when(odd == 1)
    def _():
        work(1)


def encode_part(field, pick, w_first, first_pair, first_x, fine, pooled):
    def put_fine(group, x, value):
        fine[group, x - first_x] = value.astype(BF)

    def put_pooled(group, at, value):
        pooled[group, at] = value.astype(BF)

    encode(field, pick, w_first, first_pair, 6, put_fine, put_pooled)


def encode_near_kernel(own, twin, pick, w_first, after, fine, pooled):
    def work(core):
        first, second = (twin, own) if core else (own, twin)
        field = jnp.concatenate([first[16:], second[:112]], axis=0)
        encode_part(field, pick, w_first, -3 if core else 1, -1 if core else 2, fine, pooled)

    for_each_core(work)


def encode_far_kernel(own, edge, pick, w_first, after, fine, pooled):
    def work(core):
        parts = [own[80:], edge[...]] if core else [edge[...], own[:48]]
        field = jnp.concatenate(parts, axis=0)
        encode_part(field, pick, w_first, 3 if core else -5, 6 if core else -1, fine, pooled)

    for_each_core(work)


def net_kernel(
    twin, twin_edge, pick, fine_near, pool_near, fine_far, pool_far,
    w_first, w_down, w_coarse, w_mid_skip, w_mid_up, w_fine_skip, w_fine_up, w_head,
    out,
    fine_s, pool_fine_s, mid_s, pool_mid_s, coarse_s, up_s, last_s,
):
    y_mask = jnp.where(cell_inside("gy", 32, cell_of(iota((J, 256), 0))), 1.0, 0.0)

    def gather(core):
        if core:
            fine_s[:, 0:7], fine_s[:, 7:10] = fine_near[...], fine_far[...]
            pool_fine_s[:, 2:8], pool_fine_s[:, 8:14] = pool_near[...], pool_far[...]
        else:
            fine_s[:, 0:3], fine_s[:, 3:10] = fine_far[...], fine_near[...]
            pool_fine_s[:, 0:6], pool_fine_s[:, 6:12] = pool_far[...], pool_near[...]

    for_each_core(gather)
    odd = lax.axis_index("gx") % 2 == 1
    rest, other = twin_edge[...], twin[...]
    field = jnp.where(
        odd,
        jnp.concatenate([rest, other[:48]], axis=0),
        jnp.concatenate([other[80:], rest], axis=0),
    )
    first_at = jnp.where(odd, 0, 12)

    def put_pooled(group, at, value):
        pool_fine_s[group, first_at + at] = value.astype(BF)

    encode(field, pick, w_first, first_at - 5, 2, None, put_pooled)

    sums = [jnp.zeros((J, 128), F32) for _ in range(6)]
    for py in range(2):
        lhs = jnp.concatenate(
            [
                pool_fine_s[py + dy, dx : dx + 12].reshape(12 * J, 128)
                for dx in range(3)
                for dy in range(3)
            ],
            axis=1,
        )
        value = silu_half(dot(lhs, w_down[...])).reshape(12, J, 256)
        for at in range(12):
            m = at - 4
            masked = value[at] * (y_mask * row_flag(m // 2))
            sums[at // 2] = sums[at // 2] + masked[:, :128] + masked[:, 128:]
            if -2 <= m <= 5:
                mid_s[py + 1, m + 2] = masked.astype(BF)
                shift = 1 if py else J - 1
                mid_s[0 if py else 3, m + 2] = pltpu.roll(masked, shift, 0).astype(BF)
    for at in range(6):
        pool_mid_s[0, at] = pltpu.roll(sums[at], 1, 0).astype(BF)
        pool_mid_s[1, at] = sums[at].astype(BF)
        pool_mid_s[2, at] = pltpu.roll(sums[at], J - 1, 0).astype(BF)

    lhs = jnp.concatenate(
        [
            pool_mid_s[dy, dx : dx + 4].reshape(4 * J, 128)
            for dx in range(3)
            for dy in range(3)
        ],
        axis=1,
    )
    value = silu_half(dot(lhs, w_coarse[...])).reshape(4, J, 256)
    for at in range(4):
        masked = value[at] * (y_mask * row_flag(at - 1))
        coarse_s[0, at] = pltpu.roll(masked, 1, 0).astype(BF)
        coarse_s[1, at] = masked.astype(BF)
        coarse_s[2, at] = pltpu.roll(masked, J - 1, 0).astype(BF)

    lhs = jnp.concatenate(
        [
            mid_s[dy : dy + 2, dx : dx + 6].reshape(12 * J, 256)
            for dx in range(3)
            for dy in range(3)
        ],
        axis=1,
    )
    skip = dot(lhs, w_mid_skip[...]).reshape(2, 6, J, 256)
    for py in range(2):
        lhs = jnp.concatenate(
            [
                coarse_s[py + ty, tx : tx + 3].reshape(3 * J, 256)
                for tx in range(2)
                for ty in range(2)
            ],
            axis=1,
        )
        for px in range(2):
            up = dot(lhs, w_mid_up[px * 2 + py]).reshape(3, J, 256)
            for k in range(3):
                at = 2 * k if px else 2 * k + 1
                value = silu_half(skip[py, at] + up[k])
                masked = value * (y_mask * row_flag((at - 1) // 2))
                up_s[py + 1, at] = masked[:32].astype(BF)
                shift = 1 if py else J - 1
                up_s[0 if py else 3, at] = pltpu.roll(masked, shift, 0)[:32].astype(BF)

    lhs = jnp.concatenate(
        [
            fine_s[dy : dy + 4, dx : dx + 8].reshape(1024, 256)
            for dx in range(3)
            for dy in range(3)
        ],
        axis=1,
    )
    skip = dot(lhs, w_fine_skip[...]).reshape(4, 8, 32, 256)
    for py in range(2):
        for px in range(2):
            lhs = jnp.concatenate(
                [
                    up_s[py + ty : py + ty + 2, px + tx : px + tx + 4].reshape(256, 256)
                    for tx in range(2)
                    for ty in range(2)
                ],
                axis=1,
            )
            up = dot(lhs, w_fine_up[px * 2 + py]).reshape(2, 4, 32, 256)
            for half in range(2):
                group = 2 * half + py
                for k in range(4):
                    x = 2 * k + px
                    value = silu_half(skip[group, x] + up[half, k])
                    last_s[x, pl.ds(group * 32, 32), :] = value.astype(BF)

    heads = jnp.concatenate([dot_nt(w_head[...], last_s[x]) for x in range(8)], axis=0)
    high = heads.astype(BF)
    rest = heads - high.astype(F32)
    low = rest.astype(BF)
    lowest = (rest - low.astype(F32)).astype(BF)
    row, col = iota((128, 128), 0), iota((128, 128), 1)
    order = (col == 4 * (row % 32) + row // 32).astype(BF)
    noise = dot(
        jnp.concatenate([high, low, lowest], axis=1),
        jnp.concatenate([order, order, order], axis=0),
    ).reshape(8, 16, 128)
    for x in range(8):
        out[:, x, :] = noise[x]


def body(
    noisy_field, first_weight, down_weight, coarse_weight, middle_weight, fine_weight, head_weight
):
    def shape(*dims, kind=BF):
        return jax.ShapeDtypeStruct(dims, kind)

    def cost(flops, moved):
        return pl.CostEstimate(flops=flops, bytes_accessed=moved, transcendentals=0)

    def small(limit):
        return pltpu.CompilerParams(vmem_limit_bytes=limit * 2**20)

    w_first, w_down, w_coarse, w_head, middle, fine, pick = pl.pallas_call(
        encoder_weights_kernel,
        out_shape=(
            shape(2, 192, 256),
            shape(1152, 256),
            shape(1152, 256),
            shape(16, 256),
            shape(27, 32, 96),
            shape(27, 16, 48),
            shape(4 * J, 256),
        ),
        in_specs=[ANY] * 6,
        out_specs=(VMEM,) * 7,
        scratch_shapes=[
            pltpu.VMEM((9, 3, 16), BF),
            pltpu.VMEM((27, 16, 32), BF),
            pltpu.VMEM((27, 32, 64), BF),
            pltpu.VMEM((1, 16), BF),
            pltpu.SemaphoreType.DMA((6,)),
        ],
        compiler_params=small(16),
        cost_estimate=cost(10**9, 3 * 10**6),
    )(
        *(
            pltpu.with_memory_space_constraint(weight, pltpu.HBM)
            for weight in (
                first_weight.transpose(1, 2, 3, 4, 0).reshape(9, 3, 16),
                down_weight.transpose(2, 3, 4, 1, 0).reshape(27, 16, 32),
                coarse_weight.transpose(2, 3, 4, 1, 0).reshape(27, 32, 64),
                middle_weight.transpose(2, 3, 4, 0, 1).reshape(27, 32, 96),
                fine_weight.transpose(2, 3, 4, 0, 1).reshape(27, 16, 48),
                head_weight.reshape(1, 16),
            )
        )
    )

    count = lax.axis_size("gy")
    low = lax.ppermute(noisy_field, "gy", [(i, i + 1) for i in range(count - 1)])
    high = lax.ppermute(noisy_field, "gy", [(i + 1, i) for i in range(count - 1)])
    own = pl.pallas_call(
        join_kernel,
        out_shape=shape(128, 256),
        in_specs=[VMEM] * 3 + [ANY],
        out_specs=VMEM,
        compiler_params=small(4),
        cost_estimate=cost(10**7, 2 * 10**5),
    )(noisy_field, high, low, w_head)

    count = lax.axis_size("gx")
    in_chip = [(i, i ^ 1) for i in range(count)]
    between = [(i, ((i + 1) ^ 1) - 1) for i in range(1, count - 1)]
    twin = lax.ppermute(own, "gx", in_chip)
    w_mid_skip, w_mid_up = pl.pallas_call(
        mid_weights_kernel,
        out_shape=(shape(2304, 256), shape(4, 1024, 256)),
        in_specs=[VMEM, ANY],
        out_specs=(VMEM,) * 2,
        scratch_shapes=[pltpu.VMEM((27, 96, 256), F32)],
        compiler_params=small(24),
        cost_estimate=cost(10**9, 4 * 10**6),
    )(middle, own)
    edge = pl.pallas_call(
        chip_edge_kernel,
        out_shape=shape(176, 256),
        in_specs=[VMEM] * 2 + [ANY],
        out_specs=VMEM,
        compiler_params=small(4),
        cost_estimate=cost(10**5, 3 * 10**5),
    )(own, twin, w_mid_skip)
    chip_edge = lax.ppermute(edge, "gx", between)

    def encoder(kernel, x_rows, *operands):
        return pl.pallas_call(
            kernel,
            out_shape=(shape(6, x_rows, 32, 256), shape(4, 6, J, 128)),
            in_specs=[VMEM] * 4 + [ANY],
            out_specs=(VMEM,) * 2,
            compiler_params=small(16),
            cost_estimate=cost(2 * 10**9, 3 * 10**6),
        )(*operands)

    fine_near, pool_near = encoder(encode_near_kernel, 7, own, twin, pick, w_first, edge)
    w_fine_skip, w_fine_up = pl.pallas_call(
        fine_weights_kernel,
        out_shape=(shape(2304, 256), shape(4, 1024, 256)),
        in_specs=[VMEM, ANY],
        out_specs=(VMEM,) * 2,
        scratch_shapes=[pltpu.VMEM((27, 48, 256), F32)],
        compiler_params=small(16),
        cost_estimate=cost(10**9, 4 * 10**6),
    )(fine, edge)
    rest = pl.pallas_call(
        twin_edge_kernel,
        out_shape=shape(48, 256),
        in_specs=[VMEM, ANY, ANY],
        out_specs=VMEM,
        compiler_params=small(4),
        cost_estimate=cost(10**5, 10**5),
    )(chip_edge, w_fine_skip, pool_near)
    twin_edge = lax.ppermute(rest, "gx", in_chip)
    fine_far, pool_far = encoder(encode_far_kernel, 3, own, chip_edge, pick, w_first, rest)

    return pl.pallas_call(
        net_kernel,
        out_shape=shape(16, 8, 128, kind=F32),
        in_specs=[VMEM] * 15,
        out_specs=VMEM,
        scratch_shapes=[
            pltpu.VMEM((6, 10, 32, 256), BF),
            pltpu.VMEM((4, 14, J, 128), BF),
            pltpu.VMEM((4, 8, J, 256), BF),
            pltpu.VMEM((3, 6, J, 128), BF),
            pltpu.VMEM((3, 4, J, 256), BF),
            pltpu.VMEM((4, 6, 32, 256), BF),
            pltpu.VMEM((8, 128, 256), BF),
        ],
        compiler_params=small(40),
        cost_estimate=pl.CostEstimate(
            flops=6 * 10**9, bytes_accessed=9 * 10**6, transcendentals=10**6
        ),
    )(
        twin, twin_edge, pick, fine_near, pool_near, fine_far, pool_far,
        w_first, w_down, w_coarse, w_mid_skip, w_mid_up, w_fine_skip, w_fine_up, w_head,
    )


def solution(mesh):
    placed = (P(None, "gx", "gy"), P(), P(), P(), P(), P(), P())
    return jax.shard_map(
        body, mesh=mesh, in_specs=placed, out_specs=P(None, "gx", "gy"), check_vma=False
    )
```

```python
import jax
import jax.numpy as jnp
from jax import lax
from jax.experimental import pallas as pl
from jax.experimental.pallas import tpu as pltpu
from jax.sharding import PartitionSpec as P

BF = jnp.bfloat16
F32 = jnp.float32
J = 48
VMEM = pl.BlockSpec(memory_space=pltpu.VMEM)
ANY = pl.BlockSpec(memory_space=pl.ANY)


def dot(a, b):
    return jnp.dot(a, b, preferred_element_type=F32)


def dot_nt(a, b):
    return lax.dot_general(a, b, (((1,), (1,)), ((), ())), preferred_element_type=F32)


def dot_tn(a, b):
    return lax.dot_general(a, b, (((0,), (0,)), ((), ())), preferred_element_type=F32)


def iota(shape, axis):
    return lax.broadcasted_iota(jnp.int32, shape, axis)


def natural(channels):
    return lambda lane: lane // channels


def halves(channels):
    return lambda lane: 2 * ((lane // channels) % (128 // channels)) + lane // 128


def repeat_matrix(channels):
    return (iota((channels, 256), 1) % channels == iota((channels, 256), 0)).astype(BF)


def ones_where(cond):
    return jnp.where(cond, 1.0, 0.0).astype(BF)


def tiles(depth_of):
    return [
        (slice(at, at + 128), {depth_of(lane) for lane in range(at, at + 128)})
        for at in (0, 128)
    ]


def place_block(out, index, row, rows, terms, places, held, lanes):
    total = None
    for depths, value in terms:
        depths = [depth for depth in depths if depth in held]
        if depths:
            mask = places[:, lanes] == depths[0]
            for depth in depths[1:]:
                mask = mask | (places[:, lanes] == depth)
            part = ones_where(mask) * value[:, lanes]
            total = part if total is None else total + part
    if total is None:
        total = jnp.zeros((rows, 128), BF)
    out[(*index, pl.ds(row, rows), lanes)] = total


def cell_of(j):
    return jnp.where(j < 40, j, j - J)


def cell_inside(axis, held, cell):
    at = lax.axis_index(axis) * held + cell
    return (at >= 0) & (at < lax.axis_size(axis) * held)


SETS = (((0,), (1, 2)), ((0, 1), (2,)))


def banded(out, taps, channels, row_depths, depth_of):
    size = channels * len(row_depths)
    places = depth_of(iota((channels, 256), 1))
    for lanes, held in tiles(depth_of):
        for at, depth in enumerate(row_depths):
            for xy in range(9):
                terms = [((depth + 1 - dz,), taps[dz][xy]) for dz in range(3)]
                row = xy * size + at * channels
                place_block(out, (), row, channels, terms, places, held, lanes)


def folded(out, get, channels, depths, depth_of):
    size = channels * depths
    places = depth_of(iota((channels, 256), 1))
    even = places % 2 == 0
    for px in range(2):
        for tx in range(2):
            by_y = [
                [sum(get(dz, dx, dy) for dx in SETS[px][tx]) for dy in range(3)]
                for dz in range(3)
            ]
            for py in range(2):
                for ty in range(2):
                    w0, w1, w2 = [
                        sum(by_y[dz][dy] for dy in SETS[py][ty]) for dz in range(3)
                    ]
                    inner = jnp.where(even, w1 + w2, w0 + w1).astype(BF)
                    outer = jnp.where(even, w0, w2).astype(BF)
                    for lanes, held in tiles(depth_of):
                        for depth in range(depths):
                            terms = [
                                ((2 * depth, 2 * depth + 1), inner),
                                ((2 * depth + 2, 2 * depth - 1), outer),
                            ]
                            row = (tx * 2 + ty) * size + depth * channels
                            index = (px * 2 + py,)
                            place_block(out, index, row, channels, terms, places, held, lanes)


def encoder_weights_kernel(
    raw_first, raw_down, raw_coarse, raw_middle, raw_fine, raw_head,
    w_first, w_down, w_coarse, w_head, middle, fine, pick,
    first, down, coarse, head, sems,
):
    copies = [
        pltpu.make_async_copy(source, target, sems.at[at])
        for at, (source, target) in enumerate(
            (
                (raw_first, first),
                (raw_down, down),
                (raw_coarse, coarse),
                (raw_head, head),
                (raw_middle, middle),
                (raw_fine, fine),
            )
        )
    ]
    for copy in copies:
        copy.start()
    r16, r32, r64 = repeat_matrix(16), repeat_matrix(32), repeat_matrix(64)
    row = iota((4 * J, 256), 0)
    cell = cell_of(row % J)
    inside = cell_inside("gy", 32, cell)
    pick[...] = ((iota((4 * J, 256), 1) == (4 * cell + row // J + 256) % 256) & inside).astype(BF)
    for copy in copies[:4]:
        copy.wait()

    w_first[...] = jnp.zeros_like(w_first)
    for dx in range(3):
        rows = [dot(first[dz * 3 + dx], r16) * 0.5 for dz in range(3)]
        place = halves(16)(iota((16, 256), 1))
        depth = iota((16, 256), 0)
        for dy in range(3):
            block = jnp.zeros((16, 256), F32)
            for dz in range(3):
                block = block + jnp.where(place == depth + 1 - dz, rows[dz][dy : dy + 1], 0.0)
            block = block.astype(BF)
            for even in range(2):
                w_first[even, pl.ds(dy * 64 + (even + dx) * 16, 16), :] = block

    flat = down[...].reshape(27 * 16, 32)
    all_taps = (dot(flat, r32) * (1 / 16)).astype(BF)
    taps = [[all_taps[(dz * 9 + xy) * 16 : (dz * 9 + xy + 1) * 16] for xy in range(9)] for dz in range(3)]
    banded(w_down, taps, 16, list(range(8)), halves(32))

    flat = coarse[...].reshape(27 * 32, 64)
    all_taps = (dot(flat, r64) * (1 / 16)).astype(BF)
    taps = [[all_taps[(dz * 9 + xy) * 32 : (dz * 9 + xy + 1) * 32] for xy in range(9)] for dz in range(3)]
    banded(w_coarse, taps, 32, list(range(4)), natural(64))

    row = dot(jnp.broadcast_to(head[...], (16, 16)), r16)
    w_head[...] = jnp.where(iota((16, 256), 1) // 16 == iota((16, 256), 0), row, 0.0).astype(BF)
    for copy in copies[4:]:
        copy.wait()


def mid_weights_kernel(middle, after, w_mid_skip, w_mid_up, tiled):
    r32 = repeat_matrix(32)
    for tap in range(27):
        tiled[tap] = dot_tn(middle[tap], r32) * 0.5
    taps = [[tiled[dz * 9 + xy, 64:96, :].astype(BF) for xy in range(9)] for dz in range(3)]
    banded(w_mid_skip, taps, 32, [0, 2, 4, 6, 1, 3, 5, 7], natural(32))
    folded(w_mid_up, lambda dz, dx, dy: tiled[dz * 9 + dx * 3 + dy, 0:64, :], 64, 4, natural(32))


def fine_weights_kernel(fine, after, w_fine_skip, w_fine_up, tiled):
    r16 = repeat_matrix(16)
    for tap in range(27):
        tiled[tap] = dot_tn(fine[tap], r16) * 0.5
    taps = [[tiled[dz * 9 + xy, 32:48, :].astype(BF) for xy in range(9)] for dz in range(3)]
    banded(w_fine_skip, taps, 16, list(range(0, 16, 2)) + list(range(1, 16, 2)), natural(16))
    folded(w_fine_up, lambda dz, dx, dy: tiled[dz * 9 + dx * 3 + dy, 0:32, :], 32, 8, natural(16))


def join_kernel(own, inner, outer, after, out):
    from_inner = (iota((128, 128), 1) < 64) == (lax.axis_index("gy") % 2 == 0)
    mine = own[...].astype(F32).reshape(128, 128)
    rim = jnp.where(
        from_inner,
        inner[...].astype(F32).reshape(128, 128),
        outer[...].astype(F32).reshape(128, 128),
    )
    both = jnp.concatenate([mine, rim], axis=1).astype(BF)
    row, col = iota((128, 128), 0), iota((128, 128), 1)
    swap = (col == (row % 16) * 8 + row // 16).astype(BF)
    out[...] = dot(swap, both).astype(BF)


def chip_edge_kernel(own, twin, after, out):
    odd = lax.axis_index("gx") % 2 == 1
    for_high = jnp.concatenate([twin[80:], own[...]], axis=0)
    for_low = jnp.concatenate([own[...], twin[:48]], axis=0)
    out[...] = jnp.where(odd, for_high, for_low)


def twin_edge_kernel(edge, after, also_after, out):
    odd = lax.axis_index("gx") % 2 == 1
    out[...] = jnp.where(odd, edge[:48], edge[128:])


def silu_half(h):
    return h + h * jnp.tanh(h)


def row_flag(cell):
    return jnp.where(cell_inside("gx", 2, cell), 1.0, 0.0)


def encode(field, pick, w_first, first_pair, pairs, put_fine, put_pooled):
    wide = field.astype(F32)
    shifted = [pltpu.roll(wide, 1, 1).astype(BF), field, pltpu.roll(wide, 255, 1).astype(BF)]
    for at in range(pairs):
        m = first_pair + at
        window = jnp.concatenate([part[at * 32 : at * 32 + 64] for part in shifted], axis=0)
        flag = row_flag(lax.shift_right_arithmetic(m, 1) if put_fine is None else m // 2)
        lhs = (dot_nt(pick[...], window) * flag).astype(BF)
        pooled = [jnp.zeros((J, 128), F32) for _ in range(2)]
        for even in range(2):
            value = silu_half(dot(lhs, w_first[even])).reshape(4, J, 256)
            for part in range(2):
                both = value[2 * part] + value[2 * part + 1]
                pooled[part] = pooled[part] + both[:, :128] + both[:, 128:]
            if put_fine is not None and -1 <= 2 * m + even <= 8:
                for group in range(4):
                    put_fine(group + 1, 2 * m + even, value[group, :32])
                put_fine(0, 2 * m + even, pltpu.roll(value[3], 1, 0)[:32])
                put_fine(5, 2 * m + even, pltpu.roll(value[0], J - 1, 0)[:32])
        put_pooled(0, at, pltpu.roll(pooled[1], 1, 0))
        put_pooled(1, at, pooled[0])
        put_pooled(2, at, pooled[1])
        put_pooled(3, at, pltpu.roll(pooled[0], J - 1, 0))


def for_each_core(work):
    odd = lax.axis_index("gx") % 2

    @pl.when(odd == 0)
    def _():
        work(0)

    @pl.when(odd == 1)
    def _():
        work(1)


def encode_part(field, pick, w_first, first_pair, first_x, fine, pooled):
    def put_fine(group, x, value):
        fine[group, x - first_x] = value.astype(BF)

    def put_pooled(group, at, value):
        pooled[group, at] = value.astype(BF)

    encode(field, pick, w_first, first_pair, 6, put_fine, put_pooled)


def encode_near_kernel(own, twin, pick, w_first, after, fine, pooled):
    def work(core):
        first, second = (twin, own) if core else (own, twin)
        field = jnp.concatenate([first[16:], second[:112]], axis=0)
        encode_part(field, pick, w_first, -3 if core else 1, -1 if core else 2, fine, pooled)

    for_each_core(work)


def encode_far_kernel(own, edge, pick, w_first, after, fine, pooled):
    def work(core):
        parts = [own[80:], edge[...]] if core else [edge[...], own[:48]]
        field = jnp.concatenate(parts, axis=0)
        encode_part(field, pick, w_first, 3 if core else -5, 6 if core else -1, fine, pooled)

    for_each_core(work)


def net_kernel(
    twin, twin_edge, pick, fine_near, pool_near, fine_far, pool_far,
    w_first, w_down, w_coarse, w_mid_skip, w_mid_up, w_fine_skip, w_fine_up, w_head,
    out,
    fine_s, pool_fine_s, mid_s, pool_mid_s, coarse_s, up_s, last_s,
):
    y_mask = jnp.where(cell_inside("gy", 32, cell_of(iota((J, 256), 0))), 1.0, 0.0)

    def gather(core):
        if core:
            fine_s[:, 0:7], fine_s[:, 7:10] = fine_near[...], fine_far[...]
            pool_fine_s[:, 2:8], pool_fine_s[:, 8:14] = pool_near[...], pool_far[...]
        else:
            fine_s[:, 0:3], fine_s[:, 3:10] = fine_far[...], fine_near[...]
            pool_fine_s[:, 0:6], pool_fine_s[:, 6:12] = pool_far[...], pool_near[...]

    for_each_core(gather)
    odd = lax.axis_index("gx") % 2 == 1
    rest, other = twin_edge[...], twin[...]
    field = jnp.where(
        odd,
        jnp.concatenate([rest, other[:48]], axis=0),
        jnp.concatenate([other[80:], rest], axis=0),
    )
    first_at = jnp.where(odd, 0, 12)

    def put_pooled(group, at, value):
        pool_fine_s[group, first_at + at] = value.astype(BF)

    encode(field, pick, w_first, first_at - 5, 2, None, put_pooled)

    sums = [jnp.zeros((J, 128), F32) for _ in range(6)]
    for py in range(2):
        lhs = jnp.concatenate(
            [
                pool_fine_s[py + dy, dx : dx + 12].reshape(12 * J, 128)
                for dx in range(3)
                for dy in range(3)
            ],
            axis=1,
        )
        value = silu_half(dot(lhs, w_down[...])).reshape(12, J, 256)
        for at in range(12):
            m = at - 4
            masked = value[at] * (y_mask * row_flag(m // 2))
            sums[at // 2] = sums[at // 2] + masked[:, :128] + masked[:, 128:]
            if -2 <= m <= 5:
                mid_s[py + 1, m + 2] = masked.astype(BF)
                shift = 1 if py else J - 1
                mid_s[0 if py else 3, m + 2] = pltpu.roll(masked, shift, 0).astype(BF)
    for at in range(6):
        pool_mid_s[0, at] = pltpu.roll(sums[at], 1, 0).astype(BF)
        pool_mid_s[1, at] = sums[at].astype(BF)
        pool_mid_s[2, at] = pltpu.roll(sums[at], J - 1, 0).astype(BF)

    lhs = jnp.concatenate(
        [
            pool_mid_s[dy, dx : dx + 4].reshape(4 * J, 128)
            for dx in range(3)
            for dy in range(3)
        ],
        axis=1,
    )
    value = silu_half(dot(lhs, w_coarse[...])).reshape(4, J, 256)
    for at in range(4):
        masked = value[at] * (y_mask * row_flag(at - 1))
        coarse_s[0, at] = pltpu.roll(masked, 1, 0).astype(BF)
        coarse_s[1, at] = masked.astype(BF)
        coarse_s[2, at] = pltpu.roll(masked, J - 1, 0).astype(BF)

    lhs = jnp.concatenate(
        [
            mid_s[dy : dy + 2, dx : dx + 6].reshape(12 * J, 256)
            for dx in range(3)
            for dy in range(3)
        ],
        axis=1,
    )
    skip = dot(lhs, w_mid_skip[...]).reshape(2, 6, J, 256)
    for py in range(2):
        lhs = jnp.concatenate(
            [
                coarse_s[py + ty, tx : tx + 3].reshape(3 * J, 256)
                for tx in range(2)
                for ty in range(2)
            ],
            axis=1,
        )
        for px in range(2):
            up = dot(lhs, w_mid_up[px * 2 + py]).reshape(3, J, 256)
            for k in range(3):
                at = 2 * k if px else 2 * k + 1
                value = silu_half(skip[py, at] + up[k])
                masked = value * (y_mask * row_flag((at - 1) // 2))
                up_s[py + 1, at] = masked[:32].astype(BF)
                shift = 1 if py else J - 1
                up_s[0 if py else 3, at] = pltpu.roll(masked, shift, 0)[:32].astype(BF)

    lhs = jnp.concatenate(
        [
            fine_s[dy : dy + 4, dx : dx + 8].reshape(1024, 256)
            for dx in range(3)
            for dy in range(3)
        ],
        axis=1,
    )
    skip = dot(lhs, w_fine_skip[...]).reshape(4, 8, 32, 256)
    for py in range(2):
        for px in range(2):
            lhs = jnp.concatenate(
                [
                    up_s[py + ty : py + ty + 2, px + tx : px + tx + 4].reshape(256, 256)
                    for tx in range(2)
                    for ty in range(2)
                ],
                axis=1,
            )
            up = dot(lhs, w_fine_up[px * 2 + py]).reshape(2, 4, 32, 256)
            for half in range(2):
                group = 2 * half + py
                for k in range(4):
                    x = 2 * k + px
                    value = silu_half(skip[group, x] + up[half, k])
                    last_s[x, pl.ds(group * 32, 32), :] = value.astype(BF)

    heads = jnp.concatenate([dot_nt(w_head[...], last_s[x]) for x in range(8)], axis=0)
    high = heads.astype(BF)
    rest = heads - high.astype(F32)
    low = rest.astype(BF)
    lowest = (rest - low.astype(F32)).astype(BF)
    row, col = iota((128, 128), 0), iota((128, 128), 1)
    order = (col == 4 * (row % 32) + row // 32).astype(BF)
    noise = dot(
        jnp.concatenate([high, low, lowest], axis=1),
        jnp.concatenate([order, order, order], axis=0),
    ).reshape(8, 16, 128)
    for x in range(8):
        out[:, x, :] = noise[x]


def body(
    noisy_field, first_weight, down_weight, coarse_weight, middle_weight, fine_weight, head_weight
):
    def shape(*dims, kind=BF):
        return jax.ShapeDtypeStruct(dims, kind)

    def cost(flops, moved):
        return pl.CostEstimate(flops=flops, bytes_accessed=moved, transcendentals=0)

    def small(limit):
        return pltpu.CompilerParams(vmem_limit_bytes=limit * 2**20)

    w_first, w_down, w_coarse, w_head, middle, fine, pick = pl.pallas_call(
        encoder_weights_kernel,
        out_shape=(
            shape(2, 192, 256),
            shape(1152, 256),
            shape(1152, 256),
            shape(16, 256),
            shape(27, 32, 96),
            shape(27, 16, 48),
            shape(4 * J, 256),
        ),
        in_specs=[ANY] * 6,
        out_specs=(VMEM,) * 7,
        scratch_shapes=[
            pltpu.VMEM((9, 3, 16), BF),
            pltpu.VMEM((27, 16, 32), BF),
            pltpu.VMEM((27, 32, 64), BF),
            pltpu.VMEM((1, 16), BF),
            pltpu.SemaphoreType.DMA((6,)),
        ],
        compiler_params=small(16),
        cost_estimate=cost(10**9, 3 * 10**6),
    )(
        *(
            pltpu.with_memory_space_constraint(weight, pltpu.HBM)
            for weight in (
                first_weight.transpose(1, 2, 3, 4, 0).reshape(9, 3, 16),
                down_weight.transpose(2, 3, 4, 1, 0).reshape(27, 16, 32),
                coarse_weight.transpose(2, 3, 4, 1, 0).reshape(27, 32, 64),
                middle_weight.transpose(2, 3, 4, 0, 1).reshape(27, 32, 96),
                fine_weight.transpose(2, 3, 4, 0, 1).reshape(27, 16, 48),
                head_weight.reshape(1, 16),
            )
        )
    )

    def pairs(axis):
        count = lax.axis_size(axis)
        inner = [(i, i ^ 1) for i in range(count)]
        return inner, [(i, ((i + 1) ^ 1) - 1) for i in range(1, count - 1)]

    swap_in, swap_out = pairs("gy")
    y_inner = lax.ppermute(noisy_field, "gy", swap_in)
    y_outer = lax.ppermute(noisy_field, "gy", swap_out)
    own = pl.pallas_call(
        join_kernel,
        out_shape=shape(128, 256),
        in_specs=[VMEM] * 3 + [ANY],
        out_specs=VMEM,
        compiler_params=small(4),
        cost_estimate=cost(10**7, 2 * 10**5),
    )(noisy_field, y_inner, y_outer, w_head)

    in_chip, between = pairs("gx")
    twin = lax.ppermute(own, "gx", in_chip)
    w_mid_skip, w_mid_up = pl.pallas_call(
        mid_weights_kernel,
        out_shape=(shape(2304, 256), shape(4, 1024, 256)),
        in_specs=[VMEM, ANY],
        out_specs=(VMEM,) * 2,
        scratch_shapes=[pltpu.VMEM((27, 96, 256), F32)],
        compiler_params=small(24),
        cost_estimate=cost(10**9, 4 * 10**6),
    )(middle, own)
    edge = pl.pallas_call(
        chip_edge_kernel,
        out_shape=shape(176, 256),
        in_specs=[VMEM] * 2 + [ANY],
        out_specs=VMEM,
        compiler_params=small(4),
        cost_estimate=cost(10**5, 3 * 10**5),
    )(own, twin, w_mid_skip)
    chip_edge = lax.ppermute(edge, "gx", between)

    def encoder(kernel, x_rows, *operands):
        return pl.pallas_call(
            kernel,
            out_shape=(shape(6, x_rows, 32, 256), shape(4, 6, J, 128)),
            in_specs=[VMEM] * 4 + [ANY],
            out_specs=(VMEM,) * 2,
            compiler_params=small(16),
            cost_estimate=cost(2 * 10**9, 3 * 10**6),
        )(*operands)

    fine_near, pool_near = encoder(encode_near_kernel, 7, own, twin, pick, w_first, edge)
    w_fine_skip, w_fine_up = pl.pallas_call(
        fine_weights_kernel,
        out_shape=(shape(2304, 256), shape(4, 1024, 256)),
        in_specs=[VMEM, ANY],
        out_specs=(VMEM,) * 2,
        scratch_shapes=[pltpu.VMEM((27, 48, 256), F32)],
        compiler_params=small(16),
        cost_estimate=cost(10**9, 4 * 10**6),
    )(fine, edge)
    rest = pl.pallas_call(
        twin_edge_kernel,
        out_shape=shape(48, 256),
        in_specs=[VMEM, ANY, ANY],
        out_specs=VMEM,
        compiler_params=small(4),
        cost_estimate=cost(10**5, 10**5),
    )(chip_edge, w_fine_skip, pool_near)
    twin_edge = lax.ppermute(rest, "gx", in_chip)
    fine_far, pool_far = encoder(encode_far_kernel, 3, own, chip_edge, pick, w_first, rest)

    return pl.pallas_call(
        net_kernel,
        out_shape=shape(16, 8, 128, kind=F32),
        in_specs=[VMEM] * 15,
        out_specs=VMEM,
        scratch_shapes=[
            pltpu.VMEM((6, 10, 32, 256), BF),
            pltpu.VMEM((4, 14, J, 128), BF),
            pltpu.VMEM((4, 8, J, 256), BF),
            pltpu.VMEM((3, 6, J, 128), BF),
            pltpu.VMEM((3, 4, J, 256), BF),
            pltpu.VMEM((4, 6, 32, 256), BF),
            pltpu.VMEM((8, 128, 256), BF),
        ],
        compiler_params=small(40),
        cost_estimate=pl.CostEstimate(
            flops=6 * 10**9, bytes_accessed=9 * 10**6, transcendentals=10**6
        ),
    )(
        twin, twin_edge, pick, fine_near, pool_near, fine_far, pool_far,
        w_first, w_down, w_coarse, w_mid_skip, w_mid_up, w_fine_skip, w_fine_up, w_head,
    )


def solution(mesh):
    placed = (P(None, "gx", "gy"), P(), P(), P(), P(), P(), P())
    return jax.shard_map(
        body, mesh=mesh, in_specs=placed, out_specs=P(None, "gx", "gy"), check_vma=False
    )
```

```python
import jax
import jax.numpy as jnp
from jax import lax
from jax.experimental import pallas as pl
from jax.experimental.pallas import tpu as pltpu
from jax.sharding import PartitionSpec as P

BF = jnp.bfloat16
F32 = jnp.float32
J = 48
VMEM = pl.BlockSpec(memory_space=pltpu.VMEM)
ANY = pl.BlockSpec(memory_space=pl.ANY)


def dot(a, b):
    return jnp.dot(a, b, preferred_element_type=F32)


def dot_nt(a, b):
    return lax.dot_general(a, b, (((1,), (1,)), ((), ())), preferred_element_type=F32)


def dot_tn(a, b):
    return lax.dot_general(a, b, (((0,), (0,)), ((), ())), preferred_element_type=F32)


def iota(shape, axis):
    return lax.broadcasted_iota(jnp.int32, shape, axis)


def natural(channels):
    return lambda lane: lane // channels


def halves(channels):
    return lambda lane: 2 * ((lane // channels) % (128 // channels)) + lane // 128


def repeat_matrix(channels):
    return (iota((channels, 256), 1) % channels == iota((channels, 256), 0)).astype(BF)


def ones_where(cond):
    return jnp.where(cond, 1.0, 0.0).astype(BF)


def tiles(depth_of):
    return [
        (slice(at, at + 128), {depth_of(lane) for lane in range(at, at + 128)})
        for at in (0, 128)
    ]


def place_block(out, index, row, rows, terms, places, held, lanes):
    total = None
    for depths, value in terms:
        depths = [depth for depth in depths if depth in held]
        if depths:
            mask = places[:, lanes] == depths[0]
            for depth in depths[1:]:
                mask = mask | (places[:, lanes] == depth)
            part = ones_where(mask) * value[:, lanes]
            total = part if total is None else total + part
    if total is None:
        total = jnp.zeros((rows, 128), BF)
    out[(*index, pl.ds(row, rows), lanes)] = total


def cell_of(j):
    return jnp.where(j < 40, j, j - J)


def cell_inside(axis, held, cell):
    at = lax.axis_index(axis) * held + cell
    return (at >= 0) & (at < lax.axis_size(axis) * held)


SETS = (((0,), (1, 2)), ((0, 1), (2,)))


def banded(out, taps, channels, row_depths, depth_of):
    size = channels * len(row_depths)
    places = depth_of(iota((channels, 256), 1))
    for lanes, held in tiles(depth_of):
        for at, depth in enumerate(row_depths):
            for xy in range(9):
                terms = [((depth + 1 - dz,), taps[dz][xy]) for dz in range(3)]
                row = xy * size + at * channels
                place_block(out, (), row, channels, terms, places, held, lanes)


def folded(out, get, channels, depths, depth_of):
    size = channels * depths
    places = depth_of(iota((channels, 256), 1))
    even = places % 2 == 0
    for px in range(2):
        for tx in range(2):
            by_y = [
                [sum(get(dz, dx, dy) for dx in SETS[px][tx]) for dy in range(3)]
                for dz in range(3)
            ]
            for py in range(2):
                for ty in range(2):
                    w0, w1, w2 = [
                        sum(by_y[dz][dy] for dy in SETS[py][ty]) for dz in range(3)
                    ]
                    inner = jnp.where(even, w1 + w2, w0 + w1).astype(BF)
                    outer = jnp.where(even, w0, w2).astype(BF)
                    for lanes, held in tiles(depth_of):
                        for depth in range(depths):
                            terms = [
                                ((2 * depth, 2 * depth + 1), inner),
                                ((2 * depth + 2, 2 * depth - 1), outer),
                            ]
                            row = (tx * 2 + ty) * size + depth * channels
                            index = (px * 2 + py,)
                            place_block(out, index, row, channels, terms, places, held, lanes)


def encoder_weights_kernel(
    raw_first, raw_down, raw_coarse, raw_middle, raw_fine, raw_head,
    w_first, w_down, w_coarse, w_head, middle, fine, pick,
    first, down, coarse, head, sems,
):
    copies = [
        pltpu.make_async_copy(source, target, sems.at[at])
        for at, (source, target) in enumerate(
            (
                (raw_first, first),
                (raw_down, down),
                (raw_coarse, coarse),
                (raw_head, head),
                (raw_middle, middle),
                (raw_fine, fine),
            )
        )
    ]
    for copy in copies:
        copy.start()
    r16, r32, r64 = repeat_matrix(16), repeat_matrix(32), repeat_matrix(64)
    row = iota((4 * J, 256), 0)
    cell = cell_of(row % J)
    inside = cell_inside("gy", 32, cell)
    pick[...] = ((iota((4 * J, 256), 1) == (4 * cell + row // J + 256) % 256) & inside).astype(BF)
    for copy in copies[:4]:
        copy.wait()

    w_first[...] = jnp.zeros_like(w_first)
    for dx in range(3):
        rows = [dot(first[dz * 3 + dx], r16) * 0.5 for dz in range(3)]
        place = halves(16)(iota((16, 256), 1))
        depth = iota((16, 256), 0)
        for dy in range(3):
            block = jnp.zeros((16, 256), F32)
            for dz in range(3):
                block = block + jnp.where(place == depth + 1 - dz, rows[dz][dy : dy + 1], 0.0)
            block = block.astype(BF)
            for even in range(2):
                w_first[even, pl.ds(dy * 64 + (even + dx) * 16, 16), :] = block

    flat = down[...].reshape(27 * 16, 32)
    all_taps = (dot(flat, r32) * (1 / 16)).astype(BF)
    taps = [[all_taps[(dz * 9 + xy) * 16 : (dz * 9 + xy + 1) * 16] for xy in range(9)] for dz in range(3)]
    banded(w_down, taps, 16, list(range(8)), halves(32))

    flat = coarse[...].reshape(27 * 32, 64)
    all_taps = (dot(flat, r64) * (1 / 16)).astype(BF)
    taps = [[all_taps[(dz * 9 + xy) * 32 : (dz * 9 + xy + 1) * 32] for xy in range(9)] for dz in range(3)]
    banded(w_coarse, taps, 32, list(range(4)), natural(64))

    row = dot(jnp.broadcast_to(head[...], (16, 16)), r16)
    w_head[...] = jnp.where(iota((16, 256), 1) // 16 == iota((16, 256), 0), row, 0.0).astype(BF)
    for copy in copies[4:]:
        copy.wait()


def mid_weights_kernel(middle, after, w_mid_skip, w_mid_up, tiled):
    r32 = repeat_matrix(32)
    for tap in range(27):
        tiled[tap] = dot_tn(middle[tap], r32) * 0.5
    taps = [[tiled[dz * 9 + xy, 64:96, :].astype(BF) for xy in range(9)] for dz in range(3)]
    banded(w_mid_skip, taps, 32, [0, 2, 4, 6, 1, 3, 5, 7], natural(32))
    folded(w_mid_up, lambda dz, dx, dy: tiled[dz * 9 + dx * 3 + dy, 0:64, :], 64, 4, natural(32))


def fine_weights_kernel(fine, after, w_fine_skip, w_fine_up, tiled):
    r16 = repeat_matrix(16)
    for tap in range(27):
        tiled[tap] = dot_tn(fine[tap], r16) * 0.5
    taps = [[tiled[dz * 9 + xy, 32:48, :].astype(BF) for xy in range(9)] for dz in range(3)]
    banded(w_fine_skip, taps, 16, list(range(0, 16, 2)) + list(range(1, 16, 2)), natural(16))
    folded(w_fine_up, lambda dz, dx, dy: tiled[dz * 9 + dx * 3 + dy, 0:32, :], 32, 8, natural(16))


def join_kernel(own, inner, outer, after, out):
    from_inner = (iota((128, 128), 1) < 64) == (lax.axis_index("gy") % 2 == 0)
    mine = own[...].astype(F32).reshape(128, 128)
    rim = jnp.where(
        from_inner,
        inner[...].astype(F32).reshape(128, 128),
        outer[...].astype(F32).reshape(128, 128),
    )
    both = jnp.concatenate([mine, rim], axis=1).astype(BF)
    row, col = iota((128, 128), 0), iota((128, 128), 1)
    swap = (col == (row % 16) * 8 + row // 16).astype(BF)
    out[...] = dot(swap, both).astype(BF)


def chip_edge_kernel(own, twin, after, out):
    odd = lax.axis_index("gx") % 2 == 1
    for_high = jnp.concatenate([twin[80:], own[...]], axis=0)
    for_low = jnp.concatenate([own[...], twin[:48]], axis=0)
    out[...] = jnp.where(odd, for_high, for_low)


def silu_half(h):
    return h + h * jnp.tanh(h)


def row_flag(cell):
    return jnp.where(cell_inside("gx", 2, cell), 1.0, 0.0)


def put_shifts(out, at, group, value):
    out[group + 1, at] = value.astype(BF)
    out[0 if group else 3, at] = pltpu.roll(value, 1 if group else J - 1, 0).astype(BF)


def put_three(out, at, value):
    out[0, at] = pltpu.roll(value, 1, 0).astype(BF)
    out[1, at] = value.astype(BF)
    out[2, at] = pltpu.roll(value, J - 1, 0).astype(BF)


def encode(field, pick, w_first, pairs, fine, first_x, pooled, pooled_at):
    wide = field.astype(F32)
    shifted = [pltpu.roll(wide, 1, 1).astype(BF), field, pltpu.roll(wide, 255, 1).astype(BF)]
    for at, m in enumerate(pairs):
        window = jnp.concatenate([part[at * 32 : at * 32 + 64] for part in shifted], axis=0)
        lhs = (dot_nt(pick[...], window) * row_flag(m // 2)).astype(BF)
        sums = [jnp.zeros((J, 128), F32) for _ in range(2)]
        for even in range(2):
            value = silu_half(dot(lhs, w_first[even])).reshape(4, J, 256)
            for part in range(2):
                both = value[2 * part] + value[2 * part + 1]
                sums[part] = sums[part] + both[:, :128] + both[:, 128:]
            x = 2 * m + even
            if fine is not None and -1 <= x <= 8:
                for group in range(4):
                    fine[group + 1, x - first_x] = value[group, :32].astype(BF)
                fine[0, x - first_x] = pltpu.roll(value[3], 1, 0)[:32].astype(BF)
                fine[5, x - first_x] = pltpu.roll(value[0], J - 1, 0)[:32].astype(BF)
        for part in range(2):
            put_shifts(pooled, pooled_at + at, part, sums[part])


def for_each_core(work):
    odd = lax.axis_index("gx") % 2

    @pl.when(odd == 0)
    def _():
        work(0)

    @pl.when(odd == 1)
    def _():
        work(1)


def middle_rows(pool_s, w_down, first):
    lhs = jnp.concatenate(
        [
            pool_s[dy : dy + 2, dx : dx + 4].reshape(8 * J, 128)
            for dx in range(3)
            for dy in range(3)
        ],
        axis=1,
    )
    value = silu_half(dot(lhs, w_down[...])).reshape(2, 4, J, 256)
    mask = y_mask()
    rows = [
        [value[py, at] * (mask * row_flag((first + at) // 2)) for at in range(4)]
        for py in range(2)
    ]
    pooled = []
    for at in (0, 2):
        cells = rows[0][at] + rows[0][at + 1] + rows[1][at] + rows[1][at + 1]
        pooled.append(cells[:, :128] + cells[:, 128:])
    return rows, pooled


def y_mask():
    return jnp.where(cell_inside("gy", 32, cell_of(iota((J, 256), 0))), 1.0, 0.0)


def encode_near_kernel(own, twin, pick, w_first, after, fine, pooled):
    def work(core):
        if core:
            field = jnp.concatenate([twin[80:], own[:112]], axis=0)
        else:
            field = jnp.concatenate([own[16:], twin[:48]], axis=0)
        pairs = range(-1, 3) if core else range(1, 5)
        encode(field, pick, w_first, pairs, fine, -1 if core else 2, pooled, 0)

    for_each_core(work)


def skip_near_kernel(fine, w_fine_skip, out):
    lhs = jnp.concatenate(
        [
            fine[dy : dy + 4, dx : dx + 5].reshape(640, 256)
            for dx in range(3)
            for dy in range(3)
        ],
        axis=1,
    )
    out[...] = dot(lhs, w_fine_skip[...]).reshape(4, 5, 32, 256)


def encode_inner_kernel(
    own, edge, pick, w_first, w_down, pool_near, after,
    fine, pool_far, mid, pool_mid, for_twin, pool_s,
):
    def work(core):
        if core:
            field = jnp.concatenate([own[80:], edge[:48]], axis=0)
        else:
            field = jnp.concatenate([edge[128:], own[:48]], axis=0)
        near, far = (0, 4) if core else (2, 0)
        pairs = (3, 4) if core else (-1, 0)
        encode(field, pick, w_first, pairs, fine, 6 if core else -1, pool_s, far)
        pool_far[...] = pool_s[:, far : far + 2]
        pool_s[:, near : near + 4] = pool_near[...]
        rows, pooled = middle_rows(pool_s, w_down, 0)
        for at in range(4):
            for py in range(2):
                put_shifts(mid, at, py, rows[py][at])
        for at in range(2):
            put_three(pool_mid, at, pooled[at])
            for py in range(2):
                sent = rows[py][at if core else at + 2].astype(BF)
                for_twin[pl.ds((at * 2 + py) * J, J), :] = sent
        for_twin[pl.ds(4 * J, J), :] = jnp.concatenate(pooled, axis=1).astype(BF)

    for_each_core(work)


def encode_outer_kernel(
    edge, pick, w_first, w_down, pool_far, after, mid, pool_mid, pool_s
):
    def work(core):
        field = edge[16:] if core else edge[:160]
        far, outer = (0, 2) if core else (4, 0)
        pairs = range(5, 9) if core else range(-5, -1)
        pool_s[:, far : far + 2] = pool_far[...]
        encode(field, pick, w_first, pairs, None, 0, pool_s, outer)
        rows, pooled = middle_rows(pool_s, w_down, 4 if core else -4)
        for at in range(2):
            put_three(pool_mid, at, pooled[at])
            for py in range(2):
                put_shifts(mid, at, py, rows[py][at if core else at + 2])

    for_each_core(work)


def net_kernel(
    from_twin, fine_near, fine_far, skip_near, mid_in, mid_out, pool_mid_in, pool_mid_out,
    w_coarse, w_mid_skip, w_mid_up, w_fine_skip, w_fine_up, w_head,
    out,
    fine_s, mid_s, pool_mid_s, coarse_s, up_s, skip_s, last_s,
):
    mask = y_mask()

    def gather(core):
        first, last = (6, 0) if core else (0, 6)
        mid_s[:, first : first + 2], mid_s[:, 2:6] = mid_out[...], mid_in[...]
        cell = 4 if core else 0
        pool_mid_s[:, cell : cell + 2], pool_mid_s[:, 2:4] = pool_mid_out[...], pool_mid_in[...]
        for at in range(2):
            for py in range(2):
                row = (at * 2 + py) * J
                put_shifts(mid_s, last + at, py, from_twin[row : row + J].astype(F32))
            lanes = slice(at * 128, at * 128 + 128)
            put_three(pool_mid_s, 4 - cell + at, from_twin[4 * J :, lanes].astype(F32))
        if core:
            fine_s[:, 0:2], fine_s[:, 2:5] = fine_near[:, 5:7], fine_far[...]
        else:
            fine_s[:, 0:3], fine_s[:, 3:5] = fine_far[...], fine_near[:, 0:2]
        lhs = jnp.concatenate(
            [
                fine_s[dy : dy + 4, dx : dx + 3].reshape(384, 256)
                for dx in range(3)
                for dy in range(3)
            ],
            axis=1,
        )
        skip = dot(lhs, w_fine_skip[...]).reshape(4, 3, 32, 256)
        if core:
            skip_s[:, 0:5], skip_s[:, 5:8] = skip_near[...], skip
        else:
            skip_s[:, 0:3], skip_s[:, 3:8] = skip, skip_near[...]

    for_each_core(gather)

    lhs = jnp.concatenate(
        [
            pool_mid_s[dy, dx : dx + 4].reshape(4 * J, 128)
            for dx in range(3)
            for dy in range(3)
        ],
        axis=1,
    )
    value = silu_half(dot(lhs, w_coarse[...])).reshape(4, J, 256)
    for at in range(4):
        put_three(coarse_s, at, value[at] * (mask * row_flag(at - 1)))

    lhs = jnp.concatenate(
        [
            mid_s[dy : dy + 2, dx : dx + 6].reshape(12 * J, 256)
            for dx in range(3)
            for dy in range(3)
        ],
        axis=1,
    )
    skip = dot(lhs, w_mid_skip[...]).reshape(2, 6, J, 256)
    for py in range(2):
        lhs = jnp.concatenate(
            [
                coarse_s[py + ty, tx : tx + 3].reshape(3 * J, 256)
                for tx in range(2)
                for ty in range(2)
            ],
            axis=1,
        )
        for px in range(2):
            up = dot(lhs, w_mid_up[px * 2 + py]).reshape(3, J, 256)
            for k in range(3):
                at = 2 * k if px else 2 * k + 1
                value = silu_half(skip[py, at] + up[k])
                masked = value * (mask * row_flag((at - 1) // 2))
                up_s[py + 1, at] = masked[:32].astype(BF)
                shift = 1 if py else J - 1
                up_s[0 if py else 3, at] = pltpu.roll(masked, shift, 0)[:32].astype(BF)

    for py in range(2):
        for px in range(2):
            lhs = jnp.concatenate(
                [
                    up_s[py + ty : py + ty + 2, px + tx : px + tx + 4].reshape(256, 256)
                    for tx in range(2)
                    for ty in range(2)
                ],
                axis=1,
            )
            up = dot(lhs, w_fine_up[px * 2 + py]).reshape(2, 4, 32, 256)
            for half in range(2):
                group = 2 * half + py
                for k in range(4):
                    x = 2 * k + px
                    value = silu_half(skip_s[group, x] + up[half, k])
                    last_s[x, pl.ds(group * 32, 32), :] = value.astype(BF)

    heads = jnp.concatenate([dot_nt(w_head[...], last_s[x]) for x in range(8)], axis=0)
    high = heads.astype(BF)
    rest = heads - high.astype(F32)
    low = rest.astype(BF)
    lowest = (rest - low.astype(F32)).astype(BF)
    row, col = iota((128, 128), 0), iota((128, 128), 1)
    order = (col == 4 * (row % 32) + row // 32).astype(BF)
    noise = dot(
        jnp.concatenate([high, low, lowest], axis=1),
        jnp.concatenate([order, order, order], axis=0),
    ).reshape(8, 16, 128)
    for x in range(8):
        out[:, x, :] = noise[x]


def body(
    noisy_field, first_weight, down_weight, coarse_weight, middle_weight, fine_weight, head_weight
):
    def shape(*dims, kind=BF):
        return jax.ShapeDtypeStruct(dims, kind)

    def cost(flops, moved):
        return pl.CostEstimate(flops=flops, bytes_accessed=moved, transcendentals=0)

    def small(limit):
        return pltpu.CompilerParams(vmem_limit_bytes=limit * 2**20)

    w_first, w_down, w_coarse, w_head, middle, fine, pick = pl.pallas_call(
        encoder_weights_kernel,
        out_shape=(
            shape(2, 192, 256),
            shape(1152, 256),
            shape(1152, 256),
            shape(16, 256),
            shape(27, 32, 96),
            shape(27, 16, 48),
            shape(4 * J, 256),
        ),
        in_specs=[ANY] * 6,
        out_specs=(VMEM,) * 7,
        scratch_shapes=[
            pltpu.VMEM((9, 3, 16), BF),
            pltpu.VMEM((27, 16, 32), BF),
            pltpu.VMEM((27, 32, 64), BF),
            pltpu.VMEM((1, 16), BF),
            pltpu.SemaphoreType.DMA((6,)),
        ],
        compiler_params=small(16),
        cost_estimate=cost(10**9, 3 * 10**6),
    )(
        *(
            pltpu.with_memory_space_constraint(weight, pltpu.HBM)
            for weight in (
                first_weight.transpose(1, 2, 3, 4, 0).reshape(9, 3, 16),
                down_weight.transpose(2, 3, 4, 1, 0).reshape(27, 16, 32),
                coarse_weight.transpose(2, 3, 4, 1, 0).reshape(27, 32, 64),
                middle_weight.transpose(2, 3, 4, 0, 1).reshape(27, 32, 96),
                fine_weight.transpose(2, 3, 4, 0, 1).reshape(27, 16, 48),
                head_weight.reshape(1, 16),
            )
        )
    )

    def pairs(axis):
        count = lax.axis_size(axis)
        inner = [(i, i ^ 1) for i in range(count)]
        return inner, [(i, ((i + 1) ^ 1) - 1) for i in range(1, count - 1)]

    swap_in, swap_out = pairs("gy")
    y_inner = lax.ppermute(noisy_field, "gy", swap_in)
    y_outer = lax.ppermute(noisy_field, "gy", swap_out)
    own = pl.pallas_call(
        join_kernel,
        out_shape=shape(128, 256),
        in_specs=[VMEM] * 3 + [ANY],
        out_specs=VMEM,
        compiler_params=small(4),
        cost_estimate=cost(10**7, 2 * 10**5),
    )(noisy_field, y_inner, y_outer, w_head)

    in_chip, between = pairs("gx")
    twin = lax.ppermute(own, "gx", in_chip)
    w_mid_skip, w_mid_up = pl.pallas_call(
        mid_weights_kernel,
        out_shape=(shape(2304, 256), shape(4, 1024, 256)),
        in_specs=[VMEM, ANY],
        out_specs=(VMEM,) * 2,
        scratch_shapes=[pltpu.VMEM((27, 96, 256), F32)],
        compiler_params=small(24),
        cost_estimate=cost(10**9, 4 * 10**6),
    )(middle, own)
    edge = pl.pallas_call(
        chip_edge_kernel,
        out_shape=shape(176, 256),
        in_specs=[VMEM] * 2 + [ANY],
        out_specs=VMEM,
        compiler_params=small(4),
        cost_estimate=cost(10**5, 3 * 10**5),
    )(own, twin, w_mid_skip)
    chip_edge = lax.ppermute(edge, "gx", between)

    fine_near, pool_near = pl.pallas_call(
        encode_near_kernel,
        out_shape=(shape(6, 7, 32, 256), shape(4, 4, J, 128)),
        in_specs=[VMEM] * 4 + [ANY],
        out_specs=(VMEM,) * 2,
        compiler_params=small(16),
        cost_estimate=cost(10**9, 3 * 10**6),
    )(own, twin, pick, w_first, edge)
    w_fine_skip, w_fine_up = pl.pallas_call(
        fine_weights_kernel,
        out_shape=(shape(2304, 256), shape(4, 1024, 256)),
        in_specs=[VMEM, ANY],
        out_specs=(VMEM,) * 2,
        scratch_shapes=[pltpu.VMEM((27, 48, 256), F32)],
        compiler_params=small(16),
        cost_estimate=cost(10**9, 4 * 10**6),
    )(fine, edge)
    skip_near = pl.pallas_call(
        skip_near_kernel,
        out_shape=shape(4, 5, 32, 256, kind=F32),
        in_specs=[VMEM] * 2,
        out_specs=VMEM,
        compiler_params=small(16),
        cost_estimate=cost(10**9, 2 * 10**6),
    )(fine_near, w_fine_skip)

    fine_far, pool_far, mid_in, pool_mid_in, for_twin = pl.pallas_call(
        encode_inner_kernel,
        out_shape=(
            shape(6, 3, 32, 256),
            shape(4, 2, J, 128),
            shape(4, 4, J, 256),
            shape(3, 2, J, 128),
            shape(5 * J, 256),
        ),
        in_specs=[VMEM] * 6 + [ANY],
        out_specs=(VMEM,) * 5,
        scratch_shapes=[pltpu.VMEM((4, 6, J, 128), BF)],
        compiler_params=small(16),
        cost_estimate=cost(10**9, 3 * 10**6),
    )(own, chip_edge, pick, w_first, w_down, pool_near, skip_near)
    from_twin = lax.ppermute(for_twin, "gx", in_chip)
    mid_out, pool_mid_out = pl.pallas_call(
        encode_outer_kernel,
        out_shape=(shape(4, 2, J, 256), shape(3, 2, J, 128)),
        in_specs=[VMEM] * 5 + [ANY],
        out_specs=(VMEM,) * 2,
        scratch_shapes=[pltpu.VMEM((4, 6, J, 128), BF)],
        compiler_params=small(16),
        cost_estimate=cost(2 * 10**9, 3 * 10**6),
    )(chip_edge, pick, w_first, w_down, pool_far, for_twin)

    return pl.pallas_call(
        net_kernel,
        out_shape=shape(16, 8, 128, kind=F32),
        in_specs=[VMEM] * 14,
        out_specs=VMEM,
        scratch_shapes=[
            pltpu.VMEM((6, 5, 32, 256), BF),
            pltpu.VMEM((4, 8, J, 256), BF),
            pltpu.VMEM((3, 6, J, 128), BF),
            pltpu.VMEM((3, 4, J, 256), BF),
            pltpu.VMEM((4, 6, 32, 256), BF),
            pltpu.VMEM((4, 8, 32, 256), F32),
            pltpu.VMEM((8, 128, 256), BF),
        ],
        compiler_params=small(32),
        cost_estimate=pl.CostEstimate(
            flops=6 * 10**9, bytes_accessed=9 * 10**6, transcendentals=10**6
        ),
    )(
        from_twin, fine_near, fine_far, skip_near, mid_in, mid_out, pool_mid_in, pool_mid_out,
        w_coarse, w_mid_skip, w_mid_up, w_fine_skip, w_fine_up, w_head,
    )


def solution(mesh):
    placed = (P(None, "gx", "gy"), P(), P(), P(), P(), P(), P())
    return jax.shard_map(
        body, mesh=mesh, in_specs=placed, out_specs=P(None, "gx", "gy"), check_vma=False
    )
```

```python
import jax
import jax.numpy as jnp
from jax import lax
from jax.experimental import pallas as pl
from jax.experimental.pallas import tpu as pltpu
from jax.sharding import PartitionSpec as P

BF = jnp.bfloat16
F32 = jnp.float32
J = 48
VMEM = pl.BlockSpec(memory_space=pltpu.VMEM)
ANY = pl.BlockSpec(memory_space=pl.ANY)


def dot(a, b):
    return jnp.dot(a, b, preferred_element_type=F32)


def dot_nt(a, b):
    return lax.dot_general(a, b, (((1,), (1,)), ((), ())), preferred_element_type=F32)


def dot_tn(a, b):
    return lax.dot_general(a, b, (((0,), (0,)), ((), ())), preferred_element_type=F32)


def iota(shape, axis):
    return lax.broadcasted_iota(jnp.int32, shape, axis)


def natural(channels):
    return lambda lane: lane // channels


def halves(channels):
    return lambda lane: 2 * ((lane // channels) % (128 // channels)) + lane // 128


def repeat_matrix(channels):
    return (iota((channels, 256), 1) % channels == iota((channels, 256), 0)).astype(BF)


def ones_where(cond):
    return jnp.where(cond, 1.0, 0.0).astype(BF)


def tiles(depth_of):
    return [
        (slice(at, at + 128), {depth_of(lane) for lane in range(at, at + 128)})
        for at in (0, 128)
    ]


def place_block(out, index, row, rows, terms, places, held, lanes):
    total = None
    for depths, value in terms:
        depths = [depth for depth in depths if depth in held]
        if depths:
            mask = places[:, lanes] == depths[0]
            for depth in depths[1:]:
                mask = mask | (places[:, lanes] == depth)
            part = ones_where(mask) * value[:, lanes]
            total = part if total is None else total + part
    if total is None:
        total = jnp.zeros((rows, 128), BF)
    out[(*index, pl.ds(row, rows), lanes)] = total


def cell_of(j):
    return jnp.where(j < 40, j, j - J)


def cell_inside(axis, held, cell):
    at = lax.axis_index(axis) * held + cell
    return (at >= 0) & (at < lax.axis_size(axis) * held)


SETS = (((0,), (1, 2)), ((0, 1), (2,)))


def banded(out, taps, channels, row_depths, depth_of):
    size = channels * len(row_depths)
    places = depth_of(iota((channels, 256), 1))
    for lanes, held in tiles(depth_of):
        for at, depth in enumerate(row_depths):
            for xy in range(9):
                terms = [((depth + 1 - dz,), taps[dz][xy]) for dz in range(3)]
                row = xy * size + at * channels
                place_block(out, (), row, channels, terms, places, held, lanes)


def folded(out, get, channels, depths, depth_of):
    size = channels * depths
    places = depth_of(iota((channels, 256), 1))
    even = places % 2 == 0
    for px in range(2):
        for tx in range(2):
            by_y = [
                [sum(get(dz, dx, dy) for dx in SETS[px][tx]) for dy in range(3)]
                for dz in range(3)
            ]
            for py in range(2):
                for ty in range(2):
                    w0, w1, w2 = [
                        sum(by_y[dz][dy] for dy in SETS[py][ty]) for dz in range(3)
                    ]
                    inner = jnp.where(even, w1 + w2, w0 + w1).astype(BF)
                    outer = jnp.where(even, w0, w2).astype(BF)
                    for lanes, held in tiles(depth_of):
                        for depth in range(depths):
                            terms = [
                                ((2 * depth, 2 * depth + 1), inner),
                                ((2 * depth + 2, 2 * depth - 1), outer),
                            ]
                            row = (tx * 2 + ty) * size + depth * channels
                            index = (px * 2 + py,)
                            place_block(out, index, row, channels, terms, places, held, lanes)


def encoder_weights_kernel(
    raw_first, raw_down, raw_coarse, raw_middle, raw_fine, raw_head,
    w_first, w_down, w_coarse, w_head, middle, fine, pick,
    first, down, coarse, head, sems,
):
    copies = [
        pltpu.make_async_copy(source, target, sems.at[at])
        for at, (source, target) in enumerate(
            (
                (raw_first, first),
                (raw_down, down),
                (raw_coarse, coarse),
                (raw_head, head),
                (raw_middle, middle),
                (raw_fine, fine),
            )
        )
    ]
    for copy in copies:
        copy.start()
    r16, r32, r64 = repeat_matrix(16), repeat_matrix(32), repeat_matrix(64)
    row = iota((4 * J, 256), 0)
    cell = cell_of(row % J)
    inside = cell_inside("gy", 32, cell)
    pick[...] = ((iota((4 * J, 256), 1) == (4 * cell + row // J + 256) % 256) & inside).astype(BF)
    for copy in copies[:4]:
        copy.wait()

    w_first[...] = jnp.zeros_like(w_first)
    for dx in range(3):
        rows = [dot(first[dz * 3 + dx], r16) * 0.5 for dz in range(3)]
        place = halves(16)(iota((16, 256), 1))
        depth = iota((16, 256), 0)
        for dy in range(3):
            block = jnp.zeros((16, 256), F32)
            for dz in range(3):
                block = block + jnp.where(place == depth + 1 - dz, rows[dz][dy : dy + 1], 0.0)
            block = block.astype(BF)
            for even in range(2):
                w_first[even, pl.ds(dy * 64 + (even + dx) * 16, 16), :] = block

    flat = down[...].reshape(27 * 16, 32)
    all_taps = (dot(flat, r32) * (1 / 16)).astype(BF)
    taps = [[all_taps[(dz * 9 + xy) * 16 : (dz * 9 + xy + 1) * 16] for xy in range(9)] for dz in range(3)]
    banded(w_down, taps, 16, list(range(8)), halves(32))

    flat = coarse[...].reshape(27 * 32, 64)
    all_taps = (dot(flat, r64) * (1 / 16)).astype(BF)
    taps = [[all_taps[(dz * 9 + xy) * 32 : (dz * 9 + xy + 1) * 32] for xy in range(9)] for dz in range(3)]
    banded(w_coarse, taps, 32, list(range(4)), natural(64))

    row = dot(jnp.broadcast_to(head[...], (16, 16)), r16)
    w_head[...] = jnp.where(iota((16, 256), 1) // 16 == iota((16, 256), 0), row, 0.0).astype(BF)
    for copy in copies[4:]:
        copy.wait()


def mid_weights_kernel(middle, after, w_mid_skip, w_mid_up, tiled):
    r32 = repeat_matrix(32)
    for tap in range(27):
        tiled[tap] = dot_tn(middle[tap], r32) * 0.5
    taps = [[tiled[dz * 9 + xy, 64:96, :].astype(BF) for xy in range(9)] for dz in range(3)]
    banded(w_mid_skip, taps, 32, [0, 2, 4, 6, 1, 3, 5, 7], natural(32))
    folded(w_mid_up, lambda dz, dx, dy: tiled[dz * 9 + dx * 3 + dy, 0:64, :], 64, 4, natural(32))


def fine_weights_kernel(fine, after, w_fine_skip):
    r16 = repeat_matrix(16)
    tiled = [(dot_tn(fine[tap], r16)[32:] * 0.5).astype(BF) for tap in range(27)]
    taps = [tiled[dz * 9 : dz * 9 + 9] for dz in range(3)]
    banded(w_fine_skip, taps, 16, list(range(0, 16, 2)) + list(range(1, 16, 2)), natural(16))


def join_kernel(own, inner, outer, after, out):
    from_inner = (iota((128, 128), 1) < 64) == (lax.axis_index("gy") % 2 == 0)
    mine = own[...].astype(F32).reshape(128, 128)
    rim = jnp.where(
        from_inner,
        inner[...].astype(F32).reshape(128, 128),
        outer[...].astype(F32).reshape(128, 128),
    )
    both = jnp.concatenate([mine, rim], axis=1).astype(BF)
    row, col = iota((128, 128), 0), iota((128, 128), 1)
    swap = (col == (row % 16) * 8 + row // 16).astype(BF)
    out[...] = dot(swap, both).astype(BF)


def chip_edge_kernel(own, twin, after, out):
    odd = lax.axis_index("gx") % 2 == 1
    for_high = jnp.concatenate([twin[80:], own[...]], axis=0)
    for_low = jnp.concatenate([own[...], twin[:48]], axis=0)
    out[...] = jnp.where(odd, for_high, for_low)


def silu_half(h):
    return h + h * jnp.tanh(h)


def row_flag(cell):
    return jnp.where(cell_inside("gx", 2, cell), 1.0, 0.0)


def put_shifts(out, at, group, value):
    out[group + 1, at] = value.astype(BF)
    out[0 if group else 3, at] = pltpu.roll(value, 1 if group else J - 1, 0).astype(BF)


def put_three(out, at, value):
    out[0, at] = pltpu.roll(value, 1, 0).astype(BF)
    out[1, at] = value.astype(BF)
    out[2, at] = pltpu.roll(value, J - 1, 0).astype(BF)


def encode(field, pick, w_first, pairs, fine, first_x, pooled, pooled_at):
    wide = field.astype(F32)
    shifted = [pltpu.roll(wide, 1, 1).astype(BF), field, pltpu.roll(wide, 255, 1).astype(BF)]
    windows = []
    for at, m in enumerate(pairs):
        window = jnp.concatenate([part[at * 32 : at * 32 + 64] for part in shifted], axis=0)
        windows.append((dot_nt(pick[...], window) * row_flag(m // 2)).astype(BF))
    lhs = jnp.concatenate(windows, axis=0)
    sums = [[jnp.zeros((J, 128), F32) for _ in range(2)] for _ in pairs]
    for even in range(2):
        values = silu_half(dot(lhs, w_first[even])).reshape(len(pairs), 4, J, 256)
        for at, m in enumerate(pairs):
            value = values[at]
            for part in range(2):
                both = value[2 * part] + value[2 * part + 1]
                sums[at][part] = sums[at][part] + both[:, :128] + both[:, 128:]
            x = 2 * m + even
            if fine is not None and -1 <= x <= 8:
                for group in range(4):
                    fine[group + 1, x - first_x] = value[group, :32].astype(BF)
                fine[0, x - first_x] = pltpu.roll(value[3], 1, 0)[:32].astype(BF)
                fine[5, x - first_x] = pltpu.roll(value[0], J - 1, 0)[:32].astype(BF)
    for at in range(len(pairs)):
        for part in range(2):
            put_shifts(pooled, pooled_at + at, part, sums[at][part])


def for_each_core(work):
    odd = lax.axis_index("gx") % 2

    @pl.when(odd == 0)
    def _():
        work(0)

    @pl.when(odd == 1)
    def _():
        work(1)


def middle_rows(pool_s, w_down, first, count):
    lhs = jnp.concatenate(
        [
            pool_s[dy : dy + 2, dx : dx + count].reshape(2 * count * J, 128)
            for dx in range(3)
            for dy in range(3)
        ],
        axis=1,
    )
    value = silu_half(dot(lhs, w_down[...])).reshape(2, count, J, 256)
    mask = y_mask()
    rows = [
        [value[py, at] * (mask * row_flag((first + at) // 2)) for at in range(count)]
        for py in range(2)
    ]
    pooled = []
    for at in range(0, count, 2):
        cells = rows[0][at] + rows[0][at + 1] + rows[1][at] + rows[1][at + 1]
        pooled.append(cells[:, :128] + cells[:, 128:])
    return rows, pooled


def y_mask():
    return jnp.where(cell_inside("gy", 32, cell_of(iota((J, 256), 0))), 1.0, 0.0)


def encode_near_kernel(
    own, twin, pick, w_first, w_down, after, fine, pooled, mid, pool_mid, for_twin
):
    def work(core):
        if core:
            field = jnp.concatenate([twin[80:], own[:112]], axis=0)
        else:
            field = jnp.concatenate([own[16:], twin[:48]], axis=0)
        pairs = range(-1, 3) if core else range(1, 5)
        encode(field, pick, w_first, pairs, fine, -1 if core else 2, pooled, 0)
        rows, cells = middle_rows(pooled, w_down, 0 if core else 2, 2)
        for at in range(2):
            for py in range(2):
                put_shifts(mid, at, py, rows[py][at])
                for_twin[pl.ds((at * 2 + py) * J, J), :] = rows[py][at].astype(BF)
        pool_mid[...] = cells[0].astype(BF)

    for_each_core(work)


def skip_near_kernel(fine_near, fine, w_fine_skip, out, w_fine_up, tiled):
    lhs = jnp.concatenate(
        [
            fine_near[dy : dy + 4, dx : dx + 5].reshape(640, 256)
            for dx in range(3)
            for dy in range(3)
        ],
        axis=1,
    )
    out[...] = dot(lhs, w_fine_skip[...]).reshape(4, 5, 32, 256)
    r16 = repeat_matrix(16)
    for tap in range(27):
        tiled[tap] = dot_tn(fine[tap], r16)[:32] * 0.5
    folded(w_fine_up, lambda dz, dx, dy: tiled[dz * 9 + dx * 3 + dy], 32, 8, natural(16))


def encode_inner_kernel(
    own, edge, pick, w_first, w_down, pool_near, pool_mid_near, for_twin_near, after,
    fine, pool_far, mid, pool_mid, for_twin, pool_s,
):
    def work(core):
        if core:
            field = jnp.concatenate([own[80:], edge[:48]], axis=0)
            pool_s[:, 0:2] = pool_near[:, 2:4]
        else:
            field = jnp.concatenate([edge[128:], own[:48]], axis=0)
            pool_s[:, 2:4] = pool_near[:, 0:2]
        pairs, far = ((3, 4), 2) if core else ((-1, 0), 0)
        encode(field, pick, w_first, pairs, fine, 6 if core else -1, pool_s, far)
        pool_far[...] = pool_s[:, far : far + 2]
        rows, pooled = middle_rows(pool_s, w_down, 2 if core else 0, 2)
        for at in range(2):
            for py in range(2):
                put_shifts(mid, at, py, rows[py][at])
        near = pool_mid_near[...].astype(F32)
        cells = (near, pooled[0]) if core else (pooled[0], near)
        for at in range(2):
            put_three(pool_mid, at, cells[at])
        for_twin[pl.ds(0, 4 * J), :] = for_twin_near[...]
        for_twin[pl.ds(4 * J, J), :] = jnp.concatenate(cells, axis=1).astype(BF)

    for_each_core(work)


def encode_outer_kernel(
    edge, pick, w_first, w_down, pool_far, after, mid, pool_mid, pool_s
):
    def work(core):
        field = edge[16:] if core else edge[:160]
        far, outer = (0, 2) if core else (4, 0)
        pairs = range(5, 9) if core else range(-5, -1)
        pool_s[:, far : far + 2] = pool_far[...]
        encode(field, pick, w_first, pairs, None, 0, pool_s, outer)
        rows, pooled = middle_rows(pool_s, w_down, 4 if core else -4, 4)
        for at in range(2):
            put_three(pool_mid, at, pooled[at])
            for py in range(2):
                put_shifts(mid, at, py, rows[py][at if core else at + 2])

    for_each_core(work)


def net_kernel(
    from_twin, fine_near, fine_far, skip_near, mid_near, mid_far, mid_out,
    pool_mid_in, pool_mid_out,
    w_coarse, w_mid_skip, w_mid_up, w_fine_skip, w_fine_up, w_head,
    out,
    fine_s, mid_s, pool_mid_s, coarse_s, up_s, skip_s, last_s,
):
    mask = y_mask()

    def gather(core):
        first, last = (6, 0) if core else (0, 6)
        near, far = (2, 4) if core else (4, 2)
        mid_s[:, first : first + 2] = mid_out[...]
        mid_s[:, near : near + 2], mid_s[:, far : far + 2] = mid_near[...], mid_far[...]
        cell = 4 if core else 0
        pool_mid_s[:, cell : cell + 2], pool_mid_s[:, 2:4] = pool_mid_out[...], pool_mid_in[...]
        for at in range(2):
            for py in range(2):
                row = (at * 2 + py) * J
                put_shifts(mid_s, last + at, py, from_twin[row : row + J].astype(F32))
            lanes = slice(at * 128, at * 128 + 128)
            put_three(pool_mid_s, 4 - cell + at, from_twin[4 * J :, lanes].astype(F32))
        if core:
            fine_s[:, 0:2], fine_s[:, 2:5] = fine_near[:, 5:7], fine_far[...]
            skip_s[:, 0:5] = skip_near[...]
        else:
            fine_s[:, 0:3], fine_s[:, 3:5] = fine_far[...], fine_near[:, 0:2]
            skip_s[:, 3:8] = skip_near[...]

    for_each_core(gather)
    lhs = jnp.concatenate(
        [
            fine_s[dy : dy + 4, dx : dx + 3].reshape(384, 256)
            for dx in range(3)
            for dy in range(3)
        ],
        axis=1,
    )
    skip_far = dot(lhs, w_fine_skip[...]).reshape(4, 3, 32, 256)
    skip_s[:, pl.ds(lax.axis_index("gx") % 2 * 5, 3)] = skip_far

    lhs = jnp.concatenate(
        [
            pool_mid_s[dy, dx : dx + 4].reshape(4 * J, 128)
            for dx in range(3)
            for dy in range(3)
        ],
        axis=1,
    )
    value = silu_half(dot(lhs, w_coarse[...])).reshape(4, J, 256)
    for at in range(4):
        put_three(coarse_s, at, value[at] * (mask * row_flag(at - 1)))

    lhs = jnp.concatenate(
        [
            mid_s[dy : dy + 2, dx : dx + 6].reshape(12 * J, 256)
            for dx in range(3)
            for dy in range(3)
        ],
        axis=1,
    )
    skip = dot(lhs, w_mid_skip[...]).reshape(2, 6, J, 256)
    for py in range(2):
        lhs = jnp.concatenate(
            [
                coarse_s[py + ty, tx : tx + 3].reshape(3 * J, 256)
                for tx in range(2)
                for ty in range(2)
            ],
            axis=1,
        )
        for px in range(2):
            up = dot(lhs, w_mid_up[px * 2 + py]).reshape(3, J, 256)
            for k in range(3):
                at = 2 * k if px else 2 * k + 1
                value = silu_half(skip[py, at] + up[k])
                masked = value * (mask * row_flag((at - 1) // 2))
                up_s[py + 1, at] = masked[:32].astype(BF)
                shift = 1 if py else J - 1
                up_s[0 if py else 3, at] = pltpu.roll(masked, shift, 0)[:32].astype(BF)

    row, col = iota((128, 128), 0), iota((128, 128), 1)
    order = (col == 4 * (row % 32) + row // 32).astype(BF)
    orders = jnp.concatenate([order, order, order], axis=0)
    for px in range(2):
        for py in range(2):
            lhs = jnp.concatenate(
                [
                    up_s[py + ty : py + ty + 2, px + tx : px + tx + 4].reshape(256, 256)
                    for tx in range(2)
                    for ty in range(2)
                ],
                axis=1,
            )
            up = dot(lhs, w_fine_up[px * 2 + py]).reshape(2, 4, 32, 256)
            for half in range(2):
                group = 2 * half + py
                for k in range(4):
                    value = silu_half(skip_s[group, 2 * k + px] + up[half, k])
                    last_s[2 * k + px, pl.ds(group * 32, 32), :] = value.astype(BF)
        heads = jnp.concatenate(
            [dot_nt(w_head[...], last_s[2 * k + px]) for k in range(4)], axis=0
        )
        high = heads.astype(BF)
        rest = heads - high.astype(F32)
        low = rest.astype(BF)
        lowest = (rest - low.astype(F32)).astype(BF)
        noise = dot(jnp.concatenate([high, low, lowest], axis=1), orders).reshape(4, 16, 128)
        for k in range(4):
            out[:, 2 * k + px, :] = noise[k]


def body(
    noisy_field, first_weight, down_weight, coarse_weight, middle_weight, fine_weight, head_weight
):
    def shape(*dims, kind=BF):
        return jax.ShapeDtypeStruct(dims, kind)

    def cost(flops, moved):
        return pl.CostEstimate(flops=flops, bytes_accessed=moved, transcendentals=0)

    def small(limit):
        return pltpu.CompilerParams(vmem_limit_bytes=limit * 2**20)

    w_first, w_down, w_coarse, w_head, middle, fine, pick = pl.pallas_call(
        encoder_weights_kernel,
        out_shape=(
            shape(2, 192, 256),
            shape(1152, 256),
            shape(1152, 256),
            shape(16, 256),
            shape(27, 32, 96),
            shape(27, 16, 48),
            shape(4 * J, 256),
        ),
        in_specs=[ANY] * 6,
        out_specs=(VMEM,) * 7,
        scratch_shapes=[
            pltpu.VMEM((9, 3, 16), BF),
            pltpu.VMEM((27, 16, 32), BF),
            pltpu.VMEM((27, 32, 64), BF),
            pltpu.VMEM((1, 16), BF),
            pltpu.SemaphoreType.DMA((6,)),
        ],
        compiler_params=small(16),
        cost_estimate=cost(10**9, 3 * 10**6),
    )(
        *(
            pltpu.with_memory_space_constraint(weight, pltpu.HBM)
            for weight in (
                first_weight.transpose(1, 2, 3, 4, 0).reshape(9, 3, 16),
                down_weight.transpose(2, 3, 4, 1, 0).reshape(27, 16, 32),
                coarse_weight.transpose(2, 3, 4, 1, 0).reshape(27, 32, 64),
                middle_weight.transpose(2, 3, 4, 0, 1).reshape(27, 32, 96),
                fine_weight.transpose(2, 3, 4, 0, 1).reshape(27, 16, 48),
                head_weight.reshape(1, 16),
            )
        )
    )

    def pairs(axis):
        count = lax.axis_size(axis)
        inner = [(i, i ^ 1) for i in range(count)]
        return inner, [(i, ((i + 1) ^ 1) - 1) for i in range(1, count - 1)]

    swap_in, swap_out = pairs("gy")
    y_inner = lax.ppermute(noisy_field, "gy", swap_in)
    y_outer = lax.ppermute(noisy_field, "gy", swap_out)
    own = pl.pallas_call(
        join_kernel,
        out_shape=shape(128, 256),
        in_specs=[VMEM] * 3 + [ANY],
        out_specs=VMEM,
        compiler_params=small(4),
        cost_estimate=cost(10**7, 2 * 10**5),
    )(noisy_field, y_inner, y_outer, w_head)

    in_chip, between = pairs("gx")
    twin = lax.ppermute(own, "gx", in_chip)
    w_mid_skip, w_mid_up = pl.pallas_call(
        mid_weights_kernel,
        out_shape=(shape(2304, 256), shape(4, 1024, 256)),
        in_specs=[VMEM, ANY],
        out_specs=(VMEM,) * 2,
        scratch_shapes=[pltpu.VMEM((27, 96, 256), F32)],
        compiler_params=small(24),
        cost_estimate=cost(10**9, 4 * 10**6),
    )(middle, own)
    edge = pl.pallas_call(
        chip_edge_kernel,
        out_shape=shape(176, 256),
        in_specs=[VMEM] * 2 + [ANY],
        out_specs=VMEM,
        compiler_params=small(4),
        cost_estimate=cost(10**5, 3 * 10**5),
    )(own, twin, w_mid_skip)
    chip_edge = lax.ppermute(edge, "gx", between)

    fine_near, pool_near, mid_near, pool_mid_near, for_twin_near = pl.pallas_call(
        encode_near_kernel,
        out_shape=(
            shape(6, 7, 32, 256),
            shape(4, 4, J, 128),
            shape(4, 2, J, 256),
            shape(J, 128),
            shape(4 * J, 256),
        ),
        in_specs=[VMEM] * 5 + [ANY],
        out_specs=(VMEM,) * 5,
        compiler_params=small(16),
        cost_estimate=cost(10**9, 3 * 10**6),
    )(own, twin, pick, w_first, w_down, edge)
    w_fine_skip = pl.pallas_call(
        fine_weights_kernel,
        out_shape=shape(2304, 256),
        in_specs=[VMEM, ANY],
        out_specs=VMEM,
        compiler_params=small(16),
        cost_estimate=cost(10**9, 2 * 10**6),
    )(fine, edge)
    skip_near, w_fine_up = pl.pallas_call(
        skip_near_kernel,
        out_shape=(shape(4, 5, 32, 256, kind=F32), shape(4, 1024, 256)),
        in_specs=[VMEM] * 3,
        out_specs=(VMEM,) * 2,
        scratch_shapes=[pltpu.VMEM((27, 32, 256), F32)],
        compiler_params=small(16),
        cost_estimate=cost(10**9, 4 * 10**6),
    )(fine_near, fine, w_fine_skip)

    fine_far, pool_far, mid_far, pool_mid_in, for_twin = pl.pallas_call(
        encode_inner_kernel,
        out_shape=(
            shape(6, 3, 32, 256),
            shape(4, 2, J, 128),
            shape(4, 2, J, 256),
            shape(3, 2, J, 128),
            shape(5 * J, 256),
        ),
        in_specs=[VMEM] * 8 + [ANY],
        out_specs=(VMEM,) * 5,
        scratch_shapes=[pltpu.VMEM((4, 4, J, 128), BF)],
        compiler_params=small(16),
        cost_estimate=cost(10**9, 3 * 10**6),
    )(
        own, chip_edge, pick, w_first, w_down, pool_near, pool_mid_near, for_twin_near,
        skip_near,
    )
    from_twin = lax.ppermute(for_twin, "gx", in_chip)
    mid_out, pool_mid_out = pl.pallas_call(
        encode_outer_kernel,
        out_shape=(shape(4, 2, J, 256), shape(3, 2, J, 128)),
        in_specs=[VMEM] * 5 + [ANY],
        out_specs=(VMEM,) * 2,
        scratch_shapes=[pltpu.VMEM((4, 6, J, 128), BF)],
        compiler_params=small(16),
        cost_estimate=cost(2 * 10**9, 3 * 10**6),
    )(chip_edge, pick, w_first, w_down, pool_far, for_twin)

    return pl.pallas_call(
        net_kernel,
        out_shape=shape(16, 8, 128, kind=F32),
        in_specs=[VMEM] * 15,
        out_specs=VMEM,
        scratch_shapes=[
            pltpu.VMEM((6, 5, 32, 256), BF),
            pltpu.VMEM((4, 8, J, 256), BF),
            pltpu.VMEM((3, 6, J, 128), BF),
            pltpu.VMEM((3, 4, J, 256), BF),
            pltpu.VMEM((4, 6, 32, 256), BF),
            pltpu.VMEM((4, 8, 32, 256), F32),
            pltpu.VMEM((8, 128, 256), BF),
        ],
        compiler_params=small(32),
        cost_estimate=pl.CostEstimate(
            flops=6 * 10**9, bytes_accessed=9 * 10**6, transcendentals=10**6
        ),
    )(
        from_twin, fine_near, fine_far, skip_near, mid_near, mid_far, mid_out,
        pool_mid_in, pool_mid_out,
        w_coarse, w_mid_skip, w_mid_up, w_fine_skip, w_fine_up, w_head,
    )


def solution(mesh):
    placed = (P(None, "gx", "gy"), P(), P(), P(), P(), P(), P())
    return jax.shard_map(
        body, mesh=mesh, in_specs=placed, out_specs=P(None, "gx", "gy"), check_vma=False
    )
```

```python
import jax
import jax.numpy as jnp
from jax import lax
from jax.experimental import pallas as pl
from jax.experimental.pallas import tpu as pltpu
from jax.sharding import PartitionSpec as P

BF = jnp.bfloat16
F32 = jnp.float32
J = 48
VMEM = pl.BlockSpec(memory_space=pltpu.VMEM)
ANY = pl.BlockSpec(memory_space=pl.ANY)


def dot(a, b):
    return jnp.dot(a, b, preferred_element_type=F32)


def dot_nt(a, b):
    return lax.dot_general(a, b, (((1,), (1,)), ((), ())), preferred_element_type=F32)


def dot_tn(a, b):
    return lax.dot_general(a, b, (((0,), (0,)), ((), ())), preferred_element_type=F32)


def iota(shape, axis):
    return lax.broadcasted_iota(jnp.int32, shape, axis)


def natural(channels):
    return lambda lane: lane // channels


def halves(channels):
    return lambda lane: 2 * ((lane // channels) % (128 // channels)) + lane // 128


def repeat_matrix(channels):
    return (iota((channels, 256), 1) % channels == iota((channels, 256), 0)).astype(BF)


def ones_where(cond):
    return jnp.where(cond, 1.0, 0.0).astype(BF)


def tiles(depth_of):
    return [
        (slice(at, at + 128), {depth_of(lane) for lane in range(at, at + 128)})
        for at in (0, 128)
    ]


def place_block(out, index, row, rows, terms, places, held, lanes):
    total = None
    for depths, value in terms:
        depths = [depth for depth in depths if depth in held]
        if depths:
            mask = places[:, lanes] == depths[0]
            for depth in depths[1:]:
                mask = mask | (places[:, lanes] == depth)
            part = ones_where(mask) * value[:, lanes]
            total = part if total is None else total + part
    if total is None:
        total = jnp.zeros((rows, 128), BF)
    out[(*index, pl.ds(row, rows), lanes)] = total


def cell_of(j):
    return jnp.where(j < 40, j, j - J)


def cell_inside(axis, held, cell):
    at = lax.axis_index(axis) * held + cell
    return (at >= 0) & (at < lax.axis_size(axis) * held)


SETS = (((0,), (1, 2)), ((0, 1), (2,)))


def banded(out, taps, channels, row_depths, depth_of):
    size = channels * len(row_depths)
    places = depth_of(iota((channels, 256), 1))
    for lanes, held in tiles(depth_of):
        for at, depth in enumerate(row_depths):
            for xy in range(9):
                terms = [((depth + 1 - dz,), taps[dz][xy]) for dz in range(3)]
                row = xy * size + at * channels
                place_block(out, (), row, channels, terms, places, held, lanes)


def folded(out, get, channels, depths, depth_of):
    size = channels * depths
    places = depth_of(iota((channels, 256), 1))
    even = places % 2 == 0
    for px in range(2):
        for tx in range(2):
            by_y = [
                [sum(get(dz, dx, dy) for dx in SETS[px][tx]) for dy in range(3)]
                for dz in range(3)
            ]
            for py in range(2):
                for ty in range(2):
                    w0, w1, w2 = [
                        sum(by_y[dz][dy] for dy in SETS[py][ty]) for dz in range(3)
                    ]
                    inner = jnp.where(even, w1 + w2, w0 + w1).astype(BF)
                    outer = jnp.where(even, w0, w2).astype(BF)
                    for lanes, held in tiles(depth_of):
                        for depth in range(depths):
                            terms = [
                                ((2 * depth, 2 * depth + 1), inner),
                                ((2 * depth + 2, 2 * depth - 1), outer),
                            ]
                            row = (tx * 2 + ty) * size + depth * channels
                            index = (px * 2 + py,)
                            place_block(out, index, row, channels, terms, places, held, lanes)


def encoder_weights_kernel(
    raw_first, raw_down, raw_coarse, raw_middle, raw_fine, raw_head,
    w_first, w_down, w_coarse, w_head, middle, fine, pick,
    first, down, coarse, head, sems,
):
    copies = [
        pltpu.make_async_copy(source, target, sems.at[at])
        for at, (source, target) in enumerate(
            (
                (raw_first, first),
                (raw_down, down),
                (raw_coarse, coarse),
                (raw_head, head),
                (raw_middle, middle),
                (raw_fine, fine),
            )
        )
    ]
    for copy in copies:
        copy.start()
    r16, r32, r64 = repeat_matrix(16), repeat_matrix(32), repeat_matrix(64)
    row = iota((4 * J, 256), 0)
    cell = cell_of(row % J)
    inside = cell_inside("gy", 32, cell)
    pick[...] = ((iota((4 * J, 256), 1) == (4 * cell + row // J + 256) % 256) & inside).astype(BF)
    for copy in copies[:4]:
        copy.wait()

    w_first[...] = jnp.zeros_like(w_first)
    for dx in range(3):
        rows = [dot(first[dz * 3 + dx], r16) for dz in range(3)]
        place = halves(16)(iota((16, 256), 1))
        depth = iota((16, 256), 0)
        for dy in range(3):
            block = jnp.zeros((16, 256), F32)
            for dz in range(3):
                block = block + jnp.where(place == depth + 1 - dz, rows[dz][dy : dy + 1], 0.0)
            block = block.astype(BF)
            for even in range(2):
                w_first[even, pl.ds(dy * 64 + (even + dx) * 16, 16), :] = block

    flat = down[...].reshape(27 * 16, 32)
    all_taps = (dot(flat, r32) * (1 / 8)).astype(BF)
    taps = [[all_taps[(dz * 9 + xy) * 16 : (dz * 9 + xy + 1) * 16] for xy in range(9)] for dz in range(3)]
    banded(w_down, taps, 16, list(range(8)), halves(32))

    flat = coarse[...].reshape(27 * 32, 64)
    all_taps = (dot(flat, r64) * (1 / 8)).astype(BF)
    taps = [[all_taps[(dz * 9 + xy) * 32 : (dz * 9 + xy + 1) * 32] for xy in range(9)] for dz in range(3)]
    banded(w_coarse, taps, 32, list(range(4)), natural(64))

    row = dot(jnp.broadcast_to(head[...], (16, 16)), r16)
    w_head[...] = jnp.where(iota((16, 256), 1) // 16 == iota((16, 256), 0), row, 0.0).astype(BF)
    for copy in copies[4:]:
        copy.wait()


def mid_weights_kernel(middle, after, w_mid_skip, w_mid_up, tiled):
    r32 = repeat_matrix(32)
    for tap in range(27):
        tiled[tap] = dot_tn(middle[tap], r32)
    taps = [[tiled[dz * 9 + xy, 64:96, :].astype(BF) for xy in range(9)] for dz in range(3)]
    banded(w_mid_skip, taps, 32, [0, 2, 4, 6, 1, 3, 5, 7], natural(32))
    folded(w_mid_up, lambda dz, dx, dy: tiled[dz * 9 + dx * 3 + dy, 0:64, :], 64, 4, natural(32))


def fine_weights_kernel(fine, after, w_fine_skip):
    r16 = repeat_matrix(16)
    tiled = [dot_tn(fine[tap], r16)[32:].astype(BF) for tap in range(27)]
    taps = [tiled[dz * 9 : dz * 9 + 9] for dz in range(3)]
    banded(w_fine_skip, taps, 16, list(range(0, 16, 2)) + list(range(1, 16, 2)), natural(16))


def join_kernel(own, inner, outer, after, out):
    from_inner = (iota((128, 128), 1) < 64) == (lax.axis_index("gy") % 2 == 0)
    mine = own[...].astype(F32).reshape(128, 128)
    rim = jnp.where(
        from_inner,
        inner[...].astype(F32).reshape(128, 128),
        outer[...].astype(F32).reshape(128, 128),
    )
    both = jnp.concatenate([mine, rim], axis=1).astype(BF)
    row, col = iota((128, 128), 0), iota((128, 128), 1)
    swap = (col == (row % 16) * 8 + row // 16).astype(BF)
    out[...] = dot(swap, both).astype(BF)


def chip_edge_kernel(own, twin, after, out):
    odd = lax.axis_index("gx") % 2 == 1
    for_high = jnp.concatenate([twin[80:], own[...]], axis=0)
    for_low = jnp.concatenate([own[...], twin[:48]], axis=0)
    out[...] = jnp.where(odd, for_high, for_low)


def silu(u):
    return u * (1.0 / (1.0 + jnp.exp(-u)))


def row_flag(cell):
    return jnp.where(cell_inside("gx", 2, cell), 1.0, 0.0)


def put_shifts(out, at, group, value):
    out[group + 1, at] = value.astype(BF)
    out[0 if group else 3, at] = pltpu.roll(value, 1 if group else J - 1, 0).astype(BF)


def put_three(out, at, value):
    out[0, at] = pltpu.roll(value, 1, 0).astype(BF)
    out[1, at] = value.astype(BF)
    out[2, at] = pltpu.roll(value, J - 1, 0).astype(BF)


def encode(field, pick, w_first, pairs, fine, first_x, pooled, pooled_at):
    wide = field.astype(F32)
    shifted = [pltpu.roll(wide, 1, 1).astype(BF), field, pltpu.roll(wide, 255, 1).astype(BF)]
    for at, m in enumerate(pairs):
        window = jnp.concatenate([part[at * 32 : at * 32 + 64] for part in shifted], axis=0)
        lhs = (dot_nt(pick[...], window) * row_flag(m // 2)).astype(BF)
        sums = [jnp.zeros((J, 128), F32) for _ in range(2)]
        for even in range(2):
            value = silu(dot(lhs, w_first[even])).reshape(4, J, 256)
            for part in range(2):
                both = value[2 * part] + value[2 * part + 1]
                sums[part] = sums[part] + both[:, :128] + both[:, 128:]
            x = 2 * m + even
            if fine is not None and -1 <= x <= 8:
                for group in range(4):
                    fine[group + 1, x - first_x] = value[group, :32].astype(BF)
                fine[0, x - first_x] = pltpu.roll(value[3], 1, 0)[:32].astype(BF)
                fine[5, x - first_x] = pltpu.roll(value[0], J - 1, 0)[:32].astype(BF)
        for part in range(2):
            put_shifts(pooled, pooled_at + at, part, sums[part])


def for_each_core(work):
    odd = lax.axis_index("gx") % 2

    @pl.when(odd == 0)
    def _():
        work(0)

    @pl.when(odd == 1)
    def _():
        work(1)


def middle_rows(pool_s, w_down, first, count):
    lhs = jnp.concatenate(
        [
            pool_s[dy : dy + 2, dx : dx + count].reshape(2 * count * J, 128)
            for dx in range(3)
            for dy in range(3)
        ],
        axis=1,
    )
    value = silu(dot(lhs, w_down[...])).reshape(2, count, J, 256)
    mask = y_mask()
    rows = [
        [value[py, at] * (mask * row_flag((first + at) // 2)) for at in range(count)]
        for py in range(2)
    ]
    pooled = []
    for at in range(0, count, 2):
        cells = rows[0][at] + rows[0][at + 1] + rows[1][at] + rows[1][at + 1]
        pooled.append(cells[:, :128] + cells[:, 128:])
    return rows, pooled


def y_mask():
    return jnp.where(cell_inside("gy", 32, cell_of(iota((J, 256), 0))), 1.0, 0.0)


def encode_near_kernel(
    own, twin, pick, w_first, w_down, after, fine, pooled, mid, pool_mid, for_twin
):
    def work(core):
        if core:
            field = jnp.concatenate([twin[80:], own[:112]], axis=0)
        else:
            field = jnp.concatenate([own[16:], twin[:48]], axis=0)
        pairs = range(-1, 3) if core else range(1, 5)
        encode(field, pick, w_first, pairs, fine, -1 if core else 2, pooled, 0)
        rows, cells = middle_rows(pooled, w_down, 0 if core else 2, 2)
        for at in range(2):
            for py in range(2):
                put_shifts(mid, at, py, rows[py][at])
                for_twin[pl.ds((at * 2 + py) * J, J), :] = rows[py][at].astype(BF)
        pool_mid[...] = cells[0].astype(BF)

    for_each_core(work)


def skip_near_kernel(fine_near, fine, w_fine_skip, out, w_fine_up, tiled):
    lhs = jnp.concatenate(
        [
            fine_near[dy : dy + 4, dx : dx + 5].reshape(640, 256)
            for dx in range(3)
            for dy in range(3)
        ],
        axis=1,
    )
    out[...] = dot(lhs, w_fine_skip[...]).reshape(4, 5, 32, 256)
    r16 = repeat_matrix(16)
    for tap in range(27):
        tiled[tap] = dot_tn(fine[tap], r16)[:32]
    folded(w_fine_up, lambda dz, dx, dy: tiled[dz * 9 + dx * 3 + dy], 32, 8, natural(16))


def encode_inner_kernel(
    own, edge, pick, w_first, w_down, pool_near, pool_mid_near, for_twin_near, after,
    fine, pool_far, mid, pool_mid, for_twin, pool_s,
):
    def work(core):
        if core:
            field = jnp.concatenate([own[80:], edge[:48]], axis=0)
            pool_s[:, 0:2] = pool_near[:, 2:4]
        else:
            field = jnp.concatenate([edge[128:], own[:48]], axis=0)
            pool_s[:, 2:4] = pool_near[:, 0:2]
        pairs, far = ((3, 4), 2) if core else ((-1, 0), 0)
        encode(field, pick, w_first, pairs, fine, 6 if core else -1, pool_s, far)
        pool_far[...] = pool_s[:, far : far + 2]
        rows, pooled = middle_rows(pool_s, w_down, 2 if core else 0, 2)
        for at in range(2):
            for py in range(2):
                put_shifts(mid, at, py, rows[py][at])
        near = pool_mid_near[...].astype(F32)
        cells = (near, pooled[0]) if core else (pooled[0], near)
        for at in range(2):
            put_three(pool_mid, at, cells[at])
        for_twin[pl.ds(0, 4 * J), :] = for_twin_near[...]
        for_twin[pl.ds(4 * J, J), :] = jnp.concatenate(cells, axis=1).astype(BF)

    for_each_core(work)


def encode_outer_kernel(
    edge, pick, w_first, w_down, pool_far, after, mid, pool_mid, pool_s
):
    def work(core):
        field = edge[16:] if core else edge[:160]
        far, outer = (0, 2) if core else (4, 0)
        pairs = range(5, 9) if core else range(-5, -1)
        pool_s[:, far : far + 2] = pool_far[...]
        encode(field, pick, w_first, pairs, None, 0, pool_s, outer)
        rows, pooled = middle_rows(pool_s, w_down, 4 if core else -4, 4)
        for at in range(2):
            put_three(pool_mid, at, pooled[at])
            for py in range(2):
                put_shifts(mid, at, py, rows[py][at if core else at + 2])

    for_each_core(work)


def net_kernel(
    from_twin, fine_near, fine_far, skip_near, mid_near, mid_far, mid_out,
    pool_mid_in, pool_mid_out,
    w_coarse, w_mid_skip, w_mid_up, w_fine_skip, w_fine_up, w_head,
    out,
    fine_s, mid_s, pool_mid_s, coarse_s, up_s, skip_s, last_s,
):
    mask = y_mask()

    def gather(core):
        first, last = (6, 0) if core else (0, 6)
        near, far = (2, 4) if core else (4, 2)
        mid_s[:, first : first + 2] = mid_out[...]
        mid_s[:, near : near + 2], mid_s[:, far : far + 2] = mid_near[...], mid_far[...]
        cell = 4 if core else 0
        pool_mid_s[:, cell : cell + 2], pool_mid_s[:, 2:4] = pool_mid_out[...], pool_mid_in[...]
        for at in range(2):
            for py in range(2):
                row = (at * 2 + py) * J
                put_shifts(mid_s, last + at, py, from_twin[row : row + J].astype(F32))
            lanes = slice(at * 128, at * 128 + 128)
            put_three(pool_mid_s, 4 - cell + at, from_twin[4 * J :, lanes].astype(F32))
        if core:
            fine_s[:, 0:2], fine_s[:, 2:5] = fine_near[:, 5:7], fine_far[...]
        else:
            fine_s[:, 0:3], fine_s[:, 3:5] = fine_far[...], fine_near[:, 0:2]
        lhs = jnp.concatenate(
            [
                fine_s[dy : dy + 4, dx : dx + 3].reshape(384, 256)
                for dx in range(3)
                for dy in range(3)
            ],
            axis=1,
        )
        skip = dot(lhs, w_fine_skip[...]).reshape(4, 3, 32, 256)
        if core:
            skip_s[:, 0:5], skip_s[:, 5:8] = skip_near[...], skip
        else:
            skip_s[:, 0:3], skip_s[:, 3:8] = skip, skip_near[...]

    for_each_core(gather)

    lhs = jnp.concatenate(
        [
            pool_mid_s[dy, dx : dx + 4].reshape(4 * J, 128)
            for dx in range(3)
            for dy in range(3)
        ],
        axis=1,
    )
    value = silu(dot(lhs, w_coarse[...])).reshape(4, J, 256)
    for at in range(4):
        put_three(coarse_s, at, value[at] * (mask * row_flag(at - 1)))

    lhs = jnp.concatenate(
        [
            mid_s[dy : dy + 2, dx : dx + 6].reshape(12 * J, 256)
            for dx in range(3)
            for dy in range(3)
        ],
        axis=1,
    )
    skip = dot(lhs, w_mid_skip[...]).reshape(2, 6, J, 256)
    for py in range(2):
        lhs = jnp.concatenate(
            [
                coarse_s[py + ty, tx : tx + 3].reshape(3 * J, 256)
                for tx in range(2)
                for ty in range(2)
            ],
            axis=1,
        )
        for px in range(2):
            up = dot(lhs, w_mid_up[px * 2 + py]).reshape(3, J, 256)
            for k in range(3):
                at = 2 * k if px else 2 * k + 1
                value = silu(skip[py, at] + up[k])
                masked = value * (mask * row_flag((at - 1) // 2))
                up_s[py + 1, at] = masked[:32].astype(BF)
                shift = 1 if py else J - 1
                up_s[0 if py else 3, at] = pltpu.roll(masked, shift, 0)[:32].astype(BF)

    for py in range(2):
        for px in range(2):
            lhs = jnp.concatenate(
                [
                    up_s[py + ty : py + ty + 2, px + tx : px + tx + 4].reshape(256, 256)
                    for tx in range(2)
                    for ty in range(2)
                ],
                axis=1,
            )
            up = dot(lhs, w_fine_up[px * 2 + py]).reshape(2, 4, 32, 256)
            for half in range(2):
                group = 2 * half + py
                for k in range(4):
                    x = 2 * k + px
                    value = silu(skip_s[group, x] + up[half, k])
                    last_s[x, pl.ds(group * 32, 32), :] = value.astype(BF)

    heads = jnp.concatenate([dot_nt(w_head[...], last_s[x]) for x in range(8)], axis=0)
    high = heads.astype(BF)
    rest = heads - high.astype(F32)
    low = rest.astype(BF)
    lowest = (rest - low.astype(F32)).astype(BF)
    row, col = iota((128, 128), 0), iota((128, 128), 1)
    order = (col == 4 * (row % 32) + row // 32).astype(BF)
    noise = dot(
        jnp.concatenate([high, low, lowest], axis=1),
        jnp.concatenate([order, order, order], axis=0),
    ).reshape(8, 16, 128)
    for x in range(8):
        out[:, x, :] = noise[x]


def body(
    noisy_field, first_weight, down_weight, coarse_weight, middle_weight, fine_weight, head_weight
):
    def shape(*dims, kind=BF):
        return jax.ShapeDtypeStruct(dims, kind)

    def cost(flops, moved):
        return pl.CostEstimate(flops=flops, bytes_accessed=moved, transcendentals=0)

    def small(limit):
        return pltpu.CompilerParams(vmem_limit_bytes=limit * 2**20)

    w_first, w_down, w_coarse, w_head, middle, fine, pick = pl.pallas_call(
        encoder_weights_kernel,
        out_shape=(
            shape(2, 192, 256),
            shape(1152, 256),
            shape(1152, 256),
            shape(16, 256),
            shape(27, 32, 96),
            shape(27, 16, 48),
            shape(4 * J, 256),
        ),
        in_specs=[ANY] * 6,
        out_specs=(VMEM,) * 7,
        scratch_shapes=[
            pltpu.VMEM((9, 3, 16), BF),
            pltpu.VMEM((27, 16, 32), BF),
            pltpu.VMEM((27, 32, 64), BF),
            pltpu.VMEM((1, 16), BF),
            pltpu.SemaphoreType.DMA((6,)),
        ],
        compiler_params=small(16),
        cost_estimate=cost(10**9, 3 * 10**6),
    )(
        *(
            pltpu.with_memory_space_constraint(weight, pltpu.HBM)
            for weight in (
                first_weight.transpose(1, 2, 3, 4, 0).reshape(9, 3, 16),
                down_weight.transpose(2, 3, 4, 1, 0).reshape(27, 16, 32),
                coarse_weight.transpose(2, 3, 4, 1, 0).reshape(27, 32, 64),
                middle_weight.transpose(2, 3, 4, 0, 1).reshape(27, 32, 96),
                fine_weight.transpose(2, 3, 4, 0, 1).reshape(27, 16, 48),
                head_weight.reshape(1, 16),
            )
        )
    )

    def pairs(axis):
        count = lax.axis_size(axis)
        inner = [(i, i ^ 1) for i in range(count)]
        return inner, [(i, ((i + 1) ^ 1) - 1) for i in range(1, count - 1)]

    swap_in, swap_out = pairs("gy")
    y_inner = lax.ppermute(noisy_field, "gy", swap_in)
    y_outer = lax.ppermute(noisy_field, "gy", swap_out)
    own = pl.pallas_call(
        join_kernel,
        out_shape=shape(128, 256),
        in_specs=[VMEM] * 3 + [ANY],
        out_specs=VMEM,
        compiler_params=small(4),
        cost_estimate=cost(10**7, 2 * 10**5),
    )(noisy_field, y_inner, y_outer, w_head)

    in_chip, between = pairs("gx")
    twin = lax.ppermute(own, "gx", in_chip)
    w_mid_skip, w_mid_up = pl.pallas_call(
        mid_weights_kernel,
        out_shape=(shape(2304, 256), shape(4, 1024, 256)),
        in_specs=[VMEM, ANY],
        out_specs=(VMEM,) * 2,
        scratch_shapes=[pltpu.VMEM((27, 96, 256), F32)],
        compiler_params=small(24),
        cost_estimate=cost(10**9, 4 * 10**6),
    )(middle, own)
    edge = pl.pallas_call(
        chip_edge_kernel,
        out_shape=shape(176, 256),
        in_specs=[VMEM] * 2 + [ANY],
        out_specs=VMEM,
        compiler_params=small(4),
        cost_estimate=cost(10**5, 3 * 10**5),
    )(own, twin, w_mid_skip)
    chip_edge = lax.ppermute(edge, "gx", between)

    fine_near, pool_near, mid_near, pool_mid_near, for_twin_near = pl.pallas_call(
        encode_near_kernel,
        out_shape=(
            shape(6, 7, 32, 256),
            shape(4, 4, J, 128),
            shape(4, 2, J, 256),
            shape(J, 128),
            shape(4 * J, 256),
        ),
        in_specs=[VMEM] * 5 + [ANY],
        out_specs=(VMEM,) * 5,
        compiler_params=small(16),
        cost_estimate=cost(10**9, 3 * 10**6),
    )(own, twin, pick, w_first, w_down, edge)
    w_fine_skip = pl.pallas_call(
        fine_weights_kernel,
        out_shape=shape(2304, 256),
        in_specs=[VMEM, ANY],
        out_specs=VMEM,
        compiler_params=small(16),
        cost_estimate=cost(10**9, 2 * 10**6),
    )(fine, edge)
    skip_near, w_fine_up = pl.pallas_call(
        skip_near_kernel,
        out_shape=(shape(4, 5, 32, 256, kind=F32), shape(4, 1024, 256)),
        in_specs=[VMEM] * 3,
        out_specs=(VMEM,) * 2,
        scratch_shapes=[pltpu.VMEM((27, 32, 256), F32)],
        compiler_params=small(16),
        cost_estimate=cost(10**9, 4 * 10**6),
    )(fine_near, fine, w_fine_skip)

    fine_far, pool_far, mid_far, pool_mid_in, for_twin = pl.pallas_call(
        encode_inner_kernel,
        out_shape=(
            shape(6, 3, 32, 256),
            shape(4, 2, J, 128),
            shape(4, 2, J, 256),
            shape(3, 2, J, 128),
            shape(5 * J, 256),
        ),
        in_specs=[VMEM] * 8 + [ANY],
        out_specs=(VMEM,) * 5,
        scratch_shapes=[pltpu.VMEM((4, 4, J, 128), BF)],
        compiler_params=small(16),
        cost_estimate=cost(10**9, 3 * 10**6),
    )(
        own, chip_edge, pick, w_first, w_down, pool_near, pool_mid_near, for_twin_near,
        skip_near,
    )
    from_twin = lax.ppermute(for_twin, "gx", in_chip)
    mid_out, pool_mid_out = pl.pallas_call(
        encode_outer_kernel,
        out_shape=(shape(4, 2, J, 256), shape(3, 2, J, 128)),
        in_specs=[VMEM] * 5 + [ANY],
        out_specs=(VMEM,) * 2,
        scratch_shapes=[pltpu.VMEM((4, 6, J, 128), BF)],
        compiler_params=small(16),
        cost_estimate=cost(2 * 10**9, 3 * 10**6),
    )(chip_edge, pick, w_first, w_down, pool_far, for_twin)

    return pl.pallas_call(
        net_kernel,
        out_shape=shape(16, 8, 128, kind=F32),
        in_specs=[VMEM] * 15,
        out_specs=VMEM,
        scratch_shapes=[
            pltpu.VMEM((6, 5, 32, 256), BF),
            pltpu.VMEM((4, 8, J, 256), BF),
            pltpu.VMEM((3, 6, J, 128), BF),
            pltpu.VMEM((3, 4, J, 256), BF),
            pltpu.VMEM((4, 6, 32, 256), BF),
            pltpu.VMEM((4, 8, 32, 256), F32),
            pltpu.VMEM((8, 128, 256), BF),
        ],
        compiler_params=small(32),
        cost_estimate=pl.CostEstimate(
            flops=6 * 10**9, bytes_accessed=9 * 10**6, transcendentals=10**6
        ),
    )(
        from_twin, fine_near, fine_far, skip_near, mid_near, mid_far, mid_out,
        pool_mid_in, pool_mid_out,
        w_coarse, w_mid_skip, w_mid_up, w_fine_skip, w_fine_up, w_head,
    )


def solution(mesh):
    placed = (P(None, "gx", "gy"), P(), P(), P(), P(), P(), P())
    return jax.shard_map(
        body, mesh=mesh, in_specs=placed, out_specs=P(None, "gx", "gy"), check_vma=False
    )
```

```python
import jax
import jax.numpy as jnp
from jax import lax
from jax.experimental import pallas as pl
from jax.experimental.pallas import tpu as pltpu
from jax.sharding import PartitionSpec as P

BF = jnp.bfloat16
F32 = jnp.float32
J = 40
VMEM = pl.BlockSpec(memory_space=pltpu.VMEM)
ANY = pl.BlockSpec(memory_space=pl.ANY)


def dot(a, b):
    return jnp.dot(a, b, preferred_element_type=F32)


def dot_nt(a, b):
    return lax.dot_general(a, b, (((1,), (1,)), ((), ())), preferred_element_type=F32)


def dot_tn(a, b):
    return lax.dot_general(a, b, (((0,), (0,)), ((), ())), preferred_element_type=F32)


def iota(shape, axis):
    return lax.broadcasted_iota(jnp.int32, shape, axis)


def natural(channels):
    return lambda lane: lane // channels


def halves(channels):
    return lambda lane: 2 * ((lane // channels) % (128 // channels)) + lane // 128


def repeat_matrix(channels):
    return (iota((channels, 256), 1) % channels == iota((channels, 256), 0)).astype(BF)


def ones_where(cond):
    return jnp.where(cond, 1.0, 0.0).astype(BF)


def tiles(depth_of):
    return [
        (slice(at, at + 128), {depth_of(lane) for lane in range(at, at + 128)})
        for at in (0, 128)
    ]


def place_block(out, index, row, rows, terms, places, held, lanes):
    total = None
    for depths, value in terms:
        depths = [depth for depth in depths if depth in held]
        if depths:
            mask = places[:, lanes] == depths[0]
            for depth in depths[1:]:
                mask = mask | (places[:, lanes] == depth)
            part = ones_where(mask) * value[:, lanes]
            total = part if total is None else total + part
    if total is None:
        total = jnp.zeros((rows, 128), BF)
    out[(*index, pl.ds(row, rows), lanes)] = total


def cell_of(j):
    return jnp.where(j < 36, j, j - J)


def cell_inside(axis, held, cell):
    at = lax.axis_index(axis) * held + cell
    return (at >= 0) & (at < lax.axis_size(axis) * held)


SETS = (((0,), (1, 2)), ((0, 1), (2,)))


def banded(out, taps, channels, row_depths, depth_of):
    size = channels * len(row_depths)
    places = depth_of(iota((channels, 256), 1))
    for lanes, held in tiles(depth_of):
        for at, depth in enumerate(row_depths):
            for xy in range(9):
                terms = [((depth + 1 - dz,), taps[dz][xy]) for dz in range(3)]
                row = xy * size + at * channels
                place_block(out, (), row, channels, terms, places, held, lanes)


def folded(out, get, channels, depths, depth_of):
    size = channels * depths
    places = depth_of(iota((channels, 256), 1))
    even = places % 2 == 0
    for px in range(2):
        for tx in range(2):
            by_y = [
                [sum(get(dz, dx, dy) for dx in SETS[px][tx]) for dy in range(3)]
                for dz in range(3)
            ]
            for py in range(2):
                for ty in range(2):
                    w0, w1, w2 = [
                        sum(by_y[dz][dy] for dy in SETS[py][ty]) for dz in range(3)
                    ]
                    inner = jnp.where(even, w1 + w2, w0 + w1).astype(BF)
                    outer = jnp.where(even, w0, w2).astype(BF)
                    for lanes, held in tiles(depth_of):
                        for depth in range(depths):
                            terms = [
                                ((2 * depth, 2 * depth + 1), inner),
                                ((2 * depth + 2, 2 * depth - 1), outer),
                            ]
                            row = (tx * 2 + ty) * size + depth * channels
                            index = (px * 2 + py,)
                            place_block(out, index, row, channels, terms, places, held, lanes)


def encoder_weights_kernel(
    raw_first, raw_down, raw_coarse, raw_middle, raw_fine, raw_head,
    w_first, w_down, w_coarse, w_head, middle, fine, pick,
    first, down, coarse, head, sems,
):
    copies = [
        pltpu.make_async_copy(source, target, sems.at[at])
        for at, (source, target) in enumerate(
            (
                (raw_first, first),
                (raw_down, down),
                (raw_coarse, coarse),
                (raw_head, head),
                (raw_middle, middle),
                (raw_fine, fine),
            )
        )
    ]
    for copy in copies:
        copy.start()
    r16, r32, r64 = repeat_matrix(16), repeat_matrix(32), repeat_matrix(64)
    row = iota((4 * J, 256), 0)
    cell = cell_of(row % J)
    inside = cell_inside("gy", 32, cell)
    pick[...] = ((iota((4 * J, 256), 1) == (4 * cell + row // J + 256) % 256) & inside).astype(BF)
    for copy in copies[:4]:
        copy.wait()

    w_first[...] = jnp.zeros_like(w_first)
    for dx in range(3):
        rows = [dot(first[dz * 3 + dx], r16) * 0.5 for dz in range(3)]
        place = halves(16)(iota((16, 256), 1))
        depth = iota((16, 256), 0)
        for dy in range(3):
            block = jnp.zeros((16, 256), F32)
            for dz in range(3):
                block = block + jnp.where(place == depth + 1 - dz, rows[dz][dy : dy + 1], 0.0)
            block = block.astype(BF)
            for even in range(2):
                w_first[even, pl.ds(dy * 64 + (even + dx) * 16, 16), :] = block

    flat = down[...].reshape(27 * 16, 32)
    all_taps = (dot(flat, r32) * (1 / 16)).astype(BF)
    taps = [[all_taps[(dz * 9 + xy) * 16 : (dz * 9 + xy + 1) * 16] for xy in range(9)] for dz in range(3)]
    banded(w_down, taps, 16, list(range(8)), halves(32))

    flat = coarse[...].reshape(27 * 32, 64)
    all_taps = (dot(flat, r64) * (1 / 16)).astype(BF)
    taps = [[all_taps[(dz * 9 + xy) * 32 : (dz * 9 + xy + 1) * 32] for xy in range(9)] for dz in range(3)]
    banded(w_coarse, taps, 32, list(range(4)), natural(64))

    row = dot(jnp.broadcast_to(head[...], (16, 16)), r16)
    w_head[...] = jnp.where(iota((16, 256), 1) // 16 == iota((16, 256), 0), row, 0.0).astype(BF)
    for copy in copies[4:]:
        copy.wait()


def mid_weights_kernel(middle, after, w_mid_skip, w_mid_up, tiled):
    r32 = repeat_matrix(32)
    for tap in range(27):
        tiled[tap] = dot_tn(middle[tap], r32) * 0.5
    taps = [[tiled[dz * 9 + xy, 64:96, :].astype(BF) for xy in range(9)] for dz in range(3)]
    banded(w_mid_skip, taps, 32, [0, 2, 4, 6, 1, 3, 5, 7], natural(32))
    folded(w_mid_up, lambda dz, dx, dy: tiled[dz * 9 + dx * 3 + dy, 0:64, :], 64, 4, natural(32))


def fine_weights_kernel(fine, after, w_fine_skip):
    r16 = repeat_matrix(16)
    tiled = [(dot_tn(fine[tap], r16)[32:] * 0.5).astype(BF) for tap in range(27)]
    taps = [tiled[dz * 9 : dz * 9 + 9] for dz in range(3)]
    banded(w_fine_skip, taps, 16, list(range(0, 16, 2)) + list(range(1, 16, 2)), natural(16))


def join_kernel(own, inner, outer, after, out):
    from_inner = (iota((128, 128), 1) < 64) == (lax.axis_index("gy") % 2 == 0)
    mine = own[...].astype(F32).reshape(128, 128)
    rim = jnp.where(
        from_inner,
        inner[...].astype(F32).reshape(128, 128),
        outer[...].astype(F32).reshape(128, 128),
    )
    both = jnp.concatenate([mine, rim], axis=1).astype(BF)
    row, col = iota((128, 128), 0), iota((128, 128), 1)
    swap = (col == (row % 16) * 8 + row // 16).astype(BF)
    out[...] = dot(swap, both).astype(BF)


def chip_edge_kernel(own, twin, after, out):
    odd = lax.axis_index("gx") % 2 == 1
    for_high = jnp.concatenate([twin[80:], own[...]], axis=0)
    for_low = jnp.concatenate([own[...], twin[:48]], axis=0)
    out[...] = jnp.where(odd, for_high, for_low)


def silu_half(h):
    return h + h * jnp.tanh(h)


def row_flag(cell):
    return jnp.where(cell_inside("gx", 2, cell), 1.0, 0.0)


def put_shifts(out, at, group, value):
    out[group + 1, at] = value.astype(BF)
    out[0 if group else 3, at] = pltpu.roll(value, 1 if group else J - 1, 0).astype(BF)


def put_three(out, at, value):
    out[0, at] = pltpu.roll(value, 1, 0).astype(BF)
    out[1, at] = value.astype(BF)
    out[2, at] = pltpu.roll(value, J - 1, 0).astype(BF)


def encode(field, pick, w_first, pairs, fine, first_x, pooled, pooled_at):
    wide = field.astype(F32)
    shifted = [pltpu.roll(wide, 1, 1).astype(BF), field, pltpu.roll(wide, 255, 1).astype(BF)]
    for at, m in enumerate(pairs):
        window = jnp.concatenate([part[at * 32 : at * 32 + 64] for part in shifted], axis=0)
        lhs = (dot_nt(pick[...], window) * row_flag(m // 2)).astype(BF)
        sums = [jnp.zeros((J, 128), F32) for _ in range(2)]
        for even in range(2):
            value = silu_half(dot(lhs, w_first[even])).reshape(4, J, 256)
            for part in range(2):
                both = value[2 * part] + value[2 * part + 1]
                sums[part] = sums[part] + both[:, :128] + both[:, 128:]
            x = 2 * m + even
            if fine is not None and -1 <= x <= 8:
                for group in range(4):
                    fine[group + 1, x - first_x] = value[group, :32].astype(BF)
                fine[0, x - first_x] = pltpu.roll(value[3], 1, 0)[:32].astype(BF)
                fine[5, x - first_x] = pltpu.roll(value[0], J - 1, 0)[:32].astype(BF)
        for part in range(2):
            put_shifts(pooled, pooled_at + at, part, sums[part])


def for_each_core(work):
    odd = lax.axis_index("gx") % 2

    @pl.when(odd == 0)
    def _():
        work(0)

    @pl.when(odd == 1)
    def _():
        work(1)


def middle_rows(pool_s, w_down, first, count):
    lhs = jnp.concatenate(
        [
            pool_s[dy : dy + 2, dx : dx + count].reshape(2 * count * J, 128)
            for dx in range(3)
            for dy in range(3)
        ],
        axis=1,
    )
    value = silu_half(dot(lhs, w_down[...])).reshape(2, count, J, 256)
    mask = y_mask()
    rows = [
        [value[py, at] * (mask * row_flag((first + at) // 2)) for at in range(count)]
        for py in range(2)
    ]
    pooled = []
    for at in range(0, count, 2):
        cells = rows[0][at] + rows[0][at + 1] + rows[1][at] + rows[1][at + 1]
        pooled.append(cells[:, :128] + cells[:, 128:])
    return rows, pooled


def y_mask():
    return jnp.where(cell_inside("gy", 32, cell_of(iota((J, 256), 0))), 1.0, 0.0)


def encode_near_kernel(
    own, twin, pick, w_first, w_down, after, fine, pooled, mid, pool_mid, for_twin
):
    def work(core):
        if core:
            field = jnp.concatenate([twin[80:], own[:112]], axis=0)
        else:
            field = jnp.concatenate([own[16:], twin[:48]], axis=0)
        pairs = range(-1, 3) if core else range(1, 5)
        encode(field, pick, w_first, pairs, fine, -1 if core else 2, pooled, 0)
        rows, cells = middle_rows(pooled, w_down, 0 if core else 2, 2)
        for at in range(2):
            for py in range(2):
                put_shifts(mid, at, py, rows[py][at])
                for_twin[pl.ds((at * 2 + py) * J, J), :] = rows[py][at].astype(BF)
        pool_mid[...] = cells[0].astype(BF)

    for_each_core(work)


def skip_near_kernel(fine_near, fine, w_fine_skip, out, w_fine_up, tiled):
    lhs = jnp.concatenate(
        [
            fine_near[dy : dy + 4, dx : dx + 5].reshape(640, 256)
            for dx in range(3)
            for dy in range(3)
        ],
        axis=1,
    )
    out[...] = dot(lhs, w_fine_skip[...]).reshape(4, 5, 32, 256)
    r16 = repeat_matrix(16)
    for tap in range(27):
        tiled[tap] = dot_tn(fine[tap], r16)[:32] * 0.5
    folded(w_fine_up, lambda dz, dx, dy: tiled[dz * 9 + dx * 3 + dy], 32, 8, natural(16))


def encode_inner_kernel(
    own, edge, pick, w_first, w_down, pool_near, pool_mid_near, for_twin_near, after,
    fine, pool_far, mid, pool_mid, for_twin, pool_s,
):
    def work(core):
        if core:
            field = jnp.concatenate([own[80:], edge[:48]], axis=0)
            pool_s[:, 0:2] = pool_near[:, 2:4]
        else:
            field = jnp.concatenate([edge[128:], own[:48]], axis=0)
            pool_s[:, 2:4] = pool_near[:, 0:2]
        pairs, far = ((3, 4), 2) if core else ((-1, 0), 0)
        encode(field, pick, w_first, pairs, fine, 6 if core else -1, pool_s, far)
        pool_far[...] = pool_s[:, far : far + 2]
        rows, pooled = middle_rows(pool_s, w_down, 2 if core else 0, 2)
        for at in range(2):
            for py in range(2):
                put_shifts(mid, at, py, rows[py][at])
        near = pool_mid_near[...].astype(F32)
        cells = (near, pooled[0]) if core else (pooled[0], near)
        for at in range(2):
            put_three(pool_mid, at, cells[at])
        for_twin[pl.ds(0, 4 * J), :] = for_twin_near[...]
        for_twin[pl.ds(4 * J, J), :] = jnp.concatenate(cells, axis=1).astype(BF)

    for_each_core(work)


def encode_outer_kernel(
    edge, pick, w_first, w_down, pool_far, after, mid, pool_mid, pool_s
):
    def work(core):
        field = edge[16:] if core else edge[:160]
        far, outer = (0, 2) if core else (4, 0)
        pairs = range(5, 9) if core else range(-5, -1)
        pool_s[:, far : far + 2] = pool_far[...]
        encode(field, pick, w_first, pairs, None, 0, pool_s, outer)
        rows, pooled = middle_rows(pool_s, w_down, 4 if core else -4, 4)
        for at in range(2):
            put_three(pool_mid, at, pooled[at])
            for py in range(2):
                put_shifts(mid, at, py, rows[py][at if core else at + 2])

    for_each_core(work)


def net_kernel(
    from_twin, fine_near, fine_far, skip_near, mid_near, mid_far, mid_out,
    pool_mid_in, pool_mid_out,
    w_coarse, w_mid_skip, w_mid_up, w_fine_skip, w_fine_up, w_head,
    out,
    fine_s, mid_s, pool_mid_s, coarse_s, up_s, skip_s, last_s,
):
    mask = y_mask()

    def gather(core):
        first, last = (6, 0) if core else (0, 6)
        near, far = (2, 4) if core else (4, 2)
        mid_s[:, first : first + 2] = mid_out[...]
        mid_s[:, near : near + 2], mid_s[:, far : far + 2] = mid_near[...], mid_far[...]
        cell = 4 if core else 0
        pool_mid_s[:, cell : cell + 2], pool_mid_s[:, 2:4] = pool_mid_out[...], pool_mid_in[...]
        for at in range(2):
            for py in range(2):
                row = (at * 2 + py) * J
                put_shifts(mid_s, last + at, py, from_twin[row : row + J].astype(F32))
            lanes = slice(at * 128, at * 128 + 128)
            put_three(pool_mid_s, 4 - cell + at, from_twin[4 * J :, lanes].astype(F32))
        if core:
            fine_s[:, 0:2], fine_s[:, 2:5] = fine_near[:, 5:7], fine_far[...]
        else:
            fine_s[:, 0:3], fine_s[:, 3:5] = fine_far[...], fine_near[:, 0:2]
        lhs = jnp.concatenate(
            [
                fine_s[dy : dy + 4, dx : dx + 3].reshape(384, 256)
                for dx in range(3)
                for dy in range(3)
            ],
            axis=1,
        )
        skip = dot(lhs, w_fine_skip[...]).reshape(4, 3, 32, 256)
        if core:
            skip_s[:, 0:5], skip_s[:, 5:8] = skip_near[...], skip
        else:
            skip_s[:, 0:3], skip_s[:, 3:8] = skip, skip_near[...]

    for_each_core(gather)

    lhs = jnp.concatenate(
        [
            pool_mid_s[dy, dx : dx + 4].reshape(4 * J, 128)
            for dx in range(3)
            for dy in range(3)
        ],
        axis=1,
    )
    value = silu_half(dot(lhs, w_coarse[...])).reshape(4, J, 256)
    for at in range(4):
        put_three(coarse_s, at, value[at] * (mask * row_flag(at - 1)))

    lhs = jnp.concatenate(
        [
            mid_s[dy : dy + 2, dx : dx + 6].reshape(12 * J, 256)
            for dx in range(3)
            for dy in range(3)
        ],
        axis=1,
    )
    skip = dot(lhs, w_mid_skip[...]).reshape(2, 6, J, 256)
    for py in range(2):
        lhs = jnp.concatenate(
            [
                coarse_s[py + ty, tx : tx + 3].reshape(3 * J, 256)
                for tx in range(2)
                for ty in range(2)
            ],
            axis=1,
        )
        for px in range(2):
            up = dot(lhs, w_mid_up[px * 2 + py]).reshape(3, J, 256)
            for k in range(3):
                at = 2 * k if px else 2 * k + 1
                value = silu_half(skip[py, at] + up[k])
                masked = value * (mask * row_flag((at - 1) // 2))
                up_s[py + 1, at] = masked[:32].astype(BF)
                shift = 1 if py else J - 1
                up_s[0 if py else 3, at] = pltpu.roll(masked, shift, 0)[:32].astype(BF)

    for py in range(2):
        for px in range(2):
            lhs = jnp.concatenate(
                [
                    up_s[py + ty : py + ty + 2, px + tx : px + tx + 4].reshape(256, 256)
                    for tx in range(2)
                    for ty in range(2)
                ],
                axis=1,
            )
            up = dot(lhs, w_fine_up[px * 2 + py]).reshape(2, 4, 32, 256)
            for half in range(2):
                group = 2 * half + py
                for k in range(4):
                    x = 2 * k + px
                    value = silu_half(skip_s[group, x] + up[half, k])
                    last_s[x, pl.ds(group * 32, 32), :] = value.astype(BF)

    heads = jnp.concatenate([dot_nt(w_head[...], last_s[x]) for x in range(8)], axis=0)
    high = heads.astype(BF)
    rest = heads - high.astype(F32)
    low = rest.astype(BF)
    lowest = (rest - low.astype(F32)).astype(BF)
    row, col = iota((128, 128), 0), iota((128, 128), 1)
    order = (col == 4 * (row % 32) + row // 32).astype(BF)
    noise = dot(
        jnp.concatenate([high, low, lowest], axis=1),
        jnp.concatenate([order, order, order], axis=0),
    ).reshape(8, 16, 128)
    for x in range(8):
        out[:, x, :] = noise[x]


def body(
    noisy_field, first_weight, down_weight, coarse_weight, middle_weight, fine_weight, head_weight
):
    def shape(*dims, kind=BF):
        return jax.ShapeDtypeStruct(dims, kind)

    def cost(flops, moved):
        return pl.CostEstimate(flops=flops, bytes_accessed=moved, transcendentals=0)

    def small(limit):
        return pltpu.CompilerParams(vmem_limit_bytes=limit * 2**20)

    w_first, w_down, w_coarse, w_head, middle, fine, pick = pl.pallas_call(
        encoder_weights_kernel,
        out_shape=(
            shape(2, 192, 256),
            shape(1152, 256),
            shape(1152, 256),
            shape(16, 256),
            shape(27, 32, 96),
            shape(27, 16, 48),
            shape(4 * J, 256),
        ),
        in_specs=[ANY] * 6,
        out_specs=(VMEM,) * 7,
        scratch_shapes=[
            pltpu.VMEM((9, 3, 16), BF),
            pltpu.VMEM((27, 16, 32), BF),
            pltpu.VMEM((27, 32, 64), BF),
            pltpu.VMEM((1, 16), BF),
            pltpu.SemaphoreType.DMA((6,)),
        ],
        compiler_params=small(16),
        cost_estimate=cost(10**9, 3 * 10**6),
    )(
        *(
            pltpu.with_memory_space_constraint(weight, pltpu.HBM)
            for weight in (
                first_weight.transpose(1, 2, 3, 4, 0).reshape(9, 3, 16),
                down_weight.transpose(2, 3, 4, 1, 0).reshape(27, 16, 32),
                coarse_weight.transpose(2, 3, 4, 1, 0).reshape(27, 32, 64),
                middle_weight.transpose(2, 3, 4, 0, 1).reshape(27, 32, 96),
                fine_weight.transpose(2, 3, 4, 0, 1).reshape(27, 16, 48),
                head_weight.reshape(1, 16),
            )
        )
    )

    def pairs(axis):
        count = lax.axis_size(axis)
        inner = [(i, i ^ 1) for i in range(count)]
        return inner, [(i, ((i + 1) ^ 1) - 1) for i in range(1, count - 1)]

    swap_in, swap_out = pairs("gy")
    y_inner = lax.ppermute(noisy_field, "gy", swap_in)
    y_outer = lax.ppermute(noisy_field, "gy", swap_out)
    own = pl.pallas_call(
        join_kernel,
        out_shape=shape(128, 256),
        in_specs=[VMEM] * 3 + [ANY],
        out_specs=VMEM,
        compiler_params=small(4),
        cost_estimate=cost(10**7, 2 * 10**5),
    )(noisy_field, y_inner, y_outer, w_head)

    in_chip, between = pairs("gx")
    twin = lax.ppermute(own, "gx", in_chip)
    w_mid_skip, w_mid_up = pl.pallas_call(
        mid_weights_kernel,
        out_shape=(shape(2304, 256), shape(4, 1024, 256)),
        in_specs=[VMEM, ANY],
        out_specs=(VMEM,) * 2,
        scratch_shapes=[pltpu.VMEM((27, 96, 256), F32)],
        compiler_params=small(24),
        cost_estimate=cost(10**9, 4 * 10**6),
    )(middle, own)
    edge = pl.pallas_call(
        chip_edge_kernel,
        out_shape=shape(176, 256),
        in_specs=[VMEM] * 2 + [ANY],
        out_specs=VMEM,
        compiler_params=small(4),
        cost_estimate=cost(10**5, 3 * 10**5),
    )(own, twin, w_mid_skip)
    chip_edge = lax.ppermute(edge, "gx", between)

    fine_near, pool_near, mid_near, pool_mid_near, for_twin_near = pl.pallas_call(
        encode_near_kernel,
        out_shape=(
            shape(6, 7, 32, 256),
            shape(4, 4, J, 128),
            shape(4, 2, J, 256),
            shape(J, 128),
            shape(4 * J, 256),
        ),
        in_specs=[VMEM] * 5 + [ANY],
        out_specs=(VMEM,) * 5,
        compiler_params=small(16),
        cost_estimate=cost(10**9, 3 * 10**6),
    )(own, twin, pick, w_first, w_down, edge)
    w_fine_skip = pl.pallas_call(
        fine_weights_kernel,
        out_shape=shape(2304, 256),
        in_specs=[VMEM, ANY],
        out_specs=VMEM,
        compiler_params=small(16),
        cost_estimate=cost(10**9, 2 * 10**6),
    )(fine, edge)
    skip_near, w_fine_up = pl.pallas_call(
        skip_near_kernel,
        out_shape=(shape(4, 5, 32, 256, kind=F32), shape(4, 1024, 256)),
        in_specs=[VMEM] * 3,
        out_specs=(VMEM,) * 2,
        scratch_shapes=[pltpu.VMEM((27, 32, 256), F32)],
        compiler_params=small(16),
        cost_estimate=cost(10**9, 4 * 10**6),
    )(fine_near, fine, w_fine_skip)

    fine_far, pool_far, mid_far, pool_mid_in, for_twin = pl.pallas_call(
        encode_inner_kernel,
        out_shape=(
            shape(6, 3, 32, 256),
            shape(4, 2, J, 128),
            shape(4, 2, J, 256),
            shape(3, 2, J, 128),
            shape(5 * J, 256),
        ),
        in_specs=[VMEM] * 8 + [ANY],
        out_specs=(VMEM,) * 5,
        scratch_shapes=[pltpu.VMEM((4, 4, J, 128), BF)],
        compiler_params=small(16),
        cost_estimate=cost(10**9, 3 * 10**6),
    )(
        own, chip_edge, pick, w_first, w_down, pool_near, pool_mid_near, for_twin_near,
        skip_near,
    )
    from_twin = lax.ppermute(for_twin, "gx", in_chip)
    mid_out, pool_mid_out = pl.pallas_call(
        encode_outer_kernel,
        out_shape=(shape(4, 2, J, 256), shape(3, 2, J, 128)),
        in_specs=[VMEM] * 5 + [ANY],
        out_specs=(VMEM,) * 2,
        scratch_shapes=[pltpu.VMEM((4, 6, J, 128), BF)],
        compiler_params=small(16),
        cost_estimate=cost(2 * 10**9, 3 * 10**6),
    )(chip_edge, pick, w_first, w_down, pool_far, for_twin)

    return pl.pallas_call(
        net_kernel,
        out_shape=shape(16, 8, 128, kind=F32),
        in_specs=[VMEM] * 15,
        out_specs=VMEM,
        scratch_shapes=[
            pltpu.VMEM((6, 5, 32, 256), BF),
            pltpu.VMEM((4, 8, J, 256), BF),
            pltpu.VMEM((3, 6, J, 128), BF),
            pltpu.VMEM((3, 4, J, 256), BF),
            pltpu.VMEM((4, 6, 32, 256), BF),
            pltpu.VMEM((4, 8, 32, 256), F32),
            pltpu.VMEM((8, 128, 256), BF),
        ],
        compiler_params=small(32),
        cost_estimate=pl.CostEstimate(
            flops=6 * 10**9, bytes_accessed=9 * 10**6, transcendentals=10**6
        ),
    )(
        from_twin, fine_near, fine_far, skip_near, mid_near, mid_far, mid_out,
        pool_mid_in, pool_mid_out,
        w_coarse, w_mid_skip, w_mid_up, w_fine_skip, w_fine_up, w_head,
    )


def solution(mesh):
    placed = (P(None, "gx", "gy"), P(), P(), P(), P(), P(), P())
    return jax.shard_map(
        body, mesh=mesh, in_specs=placed, out_specs=P(None, "gx", "gy"), check_vma=False
    )
```

```python
import jax
import jax.numpy as jnp
from jax import lax
from jax.experimental import pallas as pl
from jax.experimental.pallas import tpu as pltpu
from jax.sharding import PartitionSpec as P

BF = jnp.bfloat16
F32 = jnp.float32
J = 40
VMEM = pl.BlockSpec(memory_space=pltpu.VMEM)
ANY = pl.BlockSpec(memory_space=pl.ANY)


def dot(a, b):
    return jnp.dot(a, b, preferred_element_type=F32)


def dot_nt(a, b):
    return lax.dot_general(a, b, (((1,), (1,)), ((), ())), preferred_element_type=F32)


def dot_tn(a, b):
    return lax.dot_general(a, b, (((0,), (0,)), ((), ())), preferred_element_type=F32)


def iota(shape, axis):
    return lax.broadcasted_iota(jnp.int32, shape, axis)


def natural(channels):
    return lambda lane: lane // channels


def halves(channels):
    return lambda lane: 2 * ((lane // channels) % (128 // channels)) + lane // 128


def repeat_matrix(channels):
    return (iota((channels, 256), 1) % channels == iota((channels, 256), 0)).astype(BF)


def ones_where(cond):
    return jnp.where(cond, 1.0, 0.0).astype(BF)


def tiles(depth_of):
    return [
        (slice(at, at + 128), {depth_of(lane) for lane in range(at, at + 128)})
        for at in (0, 128)
    ]


def place_block(out, index, row, rows, terms, places, held, lanes):
    total = None
    for depths, value in terms:
        depths = [depth for depth in depths if depth in held]
        if depths:
            mask = places[:, lanes] == depths[0]
            for depth in depths[1:]:
                mask = mask | (places[:, lanes] == depth)
            part = ones_where(mask) * value[:, lanes]
            total = part if total is None else total + part
    if total is None:
        total = jnp.zeros((rows, 128), BF)
    out[(*index, pl.ds(row, rows), lanes)] = total


def cell_of(j):
    return jnp.where(j < 36, j, j - J)


def cell_inside(axis, held, cell):
    at = lax.axis_index(axis) * held + cell
    return (at >= 0) & (at < lax.axis_size(axis) * held)


SETS = (((0,), (1, 2)), ((0, 1), (2,)))


def banded(out, taps, channels, row_depths, depth_of):
    size = channels * len(row_depths)
    places = depth_of(iota((channels, 256), 1))

    @pl.loop(0, 9)
    def _(xy):
        values = [taps(dz * 9 + xy) for dz in range(3)]
        for lanes, held in tiles(depth_of):
            for at, depth in enumerate(row_depths):
                terms = [((depth + 1 - dz,), values[dz]) for dz in range(3)]
                row = pl.multiple_of(xy * size + at * channels, 16)
                place_block(out, (), row, channels, terms, places, held, lanes)


def folded(out, get, channels, depths, depth_of):
    size = channels * depths
    places = depth_of(iota((channels, 256), 1))
    even = places % 2 == 0
    for px in range(2):
        for tx in range(2):
            by_y = [
                [sum(get(dz, dx, dy) for dx in SETS[px][tx]) for dy in range(3)]
                for dz in range(3)
            ]
            for py in range(2):
                for ty in range(2):
                    w0, w1, w2 = [
                        sum(by_y[dz][dy] for dy in SETS[py][ty]) for dz in range(3)
                    ]
                    inner = jnp.where(even, w1 + w2, w0 + w1).astype(BF)
                    outer = jnp.where(even, w0, w2).astype(BF)
                    for lanes, held in tiles(depth_of):
                        for depth in range(depths):
                            terms = [
                                ((2 * depth, 2 * depth + 1), inner),
                                ((2 * depth + 2, 2 * depth - 1), outer),
                            ]
                            row = (tx * 2 + ty) * size + depth * channels
                            index = (px * 2 + py,)
                            place_block(out, index, row, channels, terms, places, held, lanes)


def encoder_weights_kernel(
    raw_first, raw_down, raw_coarse, raw_middle, raw_fine, raw_head,
    w_first, w_down, w_coarse, w_head, middle, fine, pick,
    first, down, coarse, head, tiled, sems,
):
    copies = [
        pltpu.make_async_copy(source, target, sems.at[at])
        for at, (source, target) in enumerate(
            (
                (raw_first, first),
                (raw_down, down),
                (raw_coarse, coarse),
                (raw_head, head),
                (raw_middle, middle),
                (raw_fine, fine),
            )
        )
    ]
    for copy in copies:
        copy.start()
    r16, r32, r64 = repeat_matrix(16), repeat_matrix(32), repeat_matrix(64)
    row = iota((4 * J, 256), 0)
    cell = cell_of(row % J)
    inside = cell_inside("gy", 32, cell)
    pick[...] = ((iota((4 * J, 256), 1) == (4 * cell + row // J + 256) % 256) & inside).astype(BF)
    for copy in copies[:4]:
        copy.wait()

    w_first[...] = jnp.zeros_like(w_first)
    for dx in range(3):
        rows = [dot(first[dz * 3 + dx], r16) * 0.5 for dz in range(3)]
        place = halves(16)(iota((16, 256), 1))
        depth = iota((16, 256), 0)
        for dy in range(3):
            block = jnp.zeros((16, 256), F32)
            for dz in range(3):
                block = block + jnp.where(place == depth + 1 - dz, rows[dz][dy : dy + 1], 0.0)
            block = block.astype(BF)
            for even in range(2):
                w_first[even, pl.ds(dy * 64 + (even + dx) * 16, 16), :] = block

    flat = down[...].reshape(27 * 16, 32)
    tiled[pl.ds(0, 27 * 16), :] = (dot(flat, r32) * (1 / 16)).astype(BF)
    banded(w_down, lambda tap: tiled[pl.ds(pl.multiple_of(tap * 16, 16), 16), :], 16, list(range(8)), halves(32))

    flat = coarse[...].reshape(27 * 32, 64)
    tiled[...] = (dot(flat, r64) * (1 / 16)).astype(BF)
    banded(w_coarse, lambda tap: tiled[pl.ds(pl.multiple_of(tap * 32, 32), 32), :], 32, list(range(4)), natural(64))

    row = dot(jnp.broadcast_to(head[...], (16, 16)), r16)
    w_head[...] = jnp.where(iota((16, 256), 1) // 16 == iota((16, 256), 0), row, 0.0).astype(BF)
    for copy in copies[4:]:
        copy.wait()


def mid_weights_kernel(middle, after, w_mid_skip, w_mid_up, tiled):
    r32 = repeat_matrix(32)

    @pl.loop(0, 9)
    def _(xy):
        for dz in range(3):
            tiled[dz * 9 + xy] = dot_tn(middle[dz * 9 + xy], r32) * 0.5

    banded(w_mid_skip, lambda tap: tiled[tap, 64:96, :].astype(BF), 32, [0, 2, 4, 6, 1, 3, 5, 7], natural(32))
    folded(w_mid_up, lambda dz, dx, dy: tiled[dz * 9 + dx * 3 + dy, 0:64, :], 64, 4, natural(32))


def fine_weights_kernel(fine, after, w_fine_skip):
    r16 = repeat_matrix(16)
    banded(w_fine_skip, lambda tap: (dot_tn(fine[tap], r16)[32:] * 0.5).astype(BF), 16, list(range(0, 16, 2)) + list(range(1, 16, 2)), natural(16))


def join_kernel(own, inner, outer, after, out):
    from_inner = (iota((128, 128), 1) < 64) == (lax.axis_index("gy") % 2 == 0)
    mine = own[...].astype(F32).reshape(128, 128)
    rim = jnp.where(
        from_inner,
        inner[...].astype(F32).reshape(128, 128),
        outer[...].astype(F32).reshape(128, 128),
    )
    both = jnp.concatenate([mine, rim], axis=1).astype(BF)
    row, col = iota((128, 128), 0), iota((128, 128), 1)
    swap = (col == (row % 16) * 8 + row // 16).astype(BF)
    out[...] = dot(swap, both).astype(BF)


def chip_edge_kernel(own, twin, after, out):
    odd = lax.axis_index("gx") % 2 == 1
    for_high = jnp.concatenate([twin[80:], own[...]], axis=0)
    for_low = jnp.concatenate([own[...], twin[:48]], axis=0)
    out[...] = jnp.where(odd, for_high, for_low)


def silu_half(h):
    return h + h * jnp.tanh(h)


def row_flag(cell):
    return jnp.where(cell_inside("gx", 2, cell), 1.0, 0.0)


def put_shifts(out, at, group, value):
    out[group + 1, at] = value.astype(BF)
    out[0 if group else 3, at] = pltpu.roll(value, 1 if group else J - 1, 0).astype(BF)


def put_three(out, at, value):
    out[0, at] = pltpu.roll(value, 1, 0).astype(BF)
    out[1, at] = value.astype(BF)
    out[2, at] = pltpu.roll(value, J - 1, 0).astype(BF)


def encode(field, pick, w_first, pairs, fine, first_x, pooled, pooled_at):
    wide = field.astype(F32)
    shifted = [pltpu.roll(wide, 1, 1).astype(BF), field, pltpu.roll(wide, 255, 1).astype(BF)]
    for at, m in enumerate(pairs):
        window = jnp.concatenate([part[at * 32 : at * 32 + 64] for part in shifted], axis=0)
        lhs = (dot_nt(pick[...], window) * row_flag(m // 2)).astype(BF)
        sums = [jnp.zeros((J, 128), F32) for _ in range(2)]
        for even in range(2):
            value = silu_half(dot(lhs, w_first[even])).reshape(4, J, 256)
            for part in range(2):
                both = value[2 * part] + value[2 * part + 1]
                sums[part] = sums[part] + both[:, :128] + both[:, 128:]
            x = 2 * m + even
            if fine is not None and -1 <= x <= 8:
                for group in range(4):
                    fine[group + 1, x - first_x] = value[group, :32].astype(BF)
                fine[0, x - first_x] = pltpu.roll(value[3], 1, 0)[:32].astype(BF)
                fine[5, x - first_x] = pltpu.roll(value[0], J - 1, 0)[:32].astype(BF)
        for part in range(2):
            put_shifts(pooled, pooled_at + at, part, sums[part])


def for_each_core(work):
    odd = lax.axis_index("gx") % 2

    @pl.when(odd == 0)
    def _():
        work(0)

    @pl.when(odd == 1)
    def _():
        work(1)


def middle_rows(pool_s, w_down, first, count):
    lhs = jnp.concatenate(
        [
            pool_s[dy : dy + 2, dx : dx + count].reshape(2 * count * J, 128)
            for dx in range(3)
            for dy in range(3)
        ],
        axis=1,
    )
    value = silu_half(dot(lhs, w_down[...])).reshape(2, count, J, 256)
    mask = y_mask()
    rows = [
        [value[py, at] * (mask * row_flag((first + at) // 2)) for at in range(count)]
        for py in range(2)
    ]
    pooled = []
    for at in range(0, count, 2):
        cells = rows[0][at] + rows[0][at + 1] + rows[1][at] + rows[1][at + 1]
        pooled.append(cells[:, :128] + cells[:, 128:])
    return rows, pooled


def y_mask():
    return jnp.where(cell_inside("gy", 32, cell_of(iota((J, 256), 0))), 1.0, 0.0)


def encode_near_kernel(
    own, twin, pick, w_first, w_down, after, fine, pooled, mid, pool_mid, for_twin
):
    def work(core):
        if core:
            field = jnp.concatenate([twin[80:], own[:112]], axis=0)
        else:
            field = jnp.concatenate([own[16:], twin[:48]], axis=0)
        pairs = range(-1, 3) if core else range(1, 5)
        encode(field, pick, w_first, pairs, fine, -1 if core else 2, pooled, 0)
        rows, cells = middle_rows(pooled, w_down, 0 if core else 2, 2)
        for at in range(2):
            for py in range(2):
                put_shifts(mid, at, py, rows[py][at])
                for_twin[pl.ds((at * 2 + py) * J, J), :] = rows[py][at].astype(BF)
        pool_mid[...] = cells[0].astype(BF)

    for_each_core(work)


def skip_near_kernel(fine_near, fine, w_fine_skip, out, w_fine_up, tiled):
    @pl.loop(0, 4)
    def _(group):
        lhs = jnp.concatenate(
            [
                fine_near[group + dy, dx : dx + 5].reshape(160, 256)
                for dx in range(3)
                for dy in range(3)
            ],
            axis=1,
        )
        out[group] = dot(lhs, w_fine_skip[...]).reshape(5, 32, 256)

    r16 = repeat_matrix(16)
    for tap in range(27):
        tiled[tap] = dot_tn(fine[tap], r16)[:32] * 0.5
    folded(w_fine_up, lambda dz, dx, dy: tiled[dz * 9 + dx * 3 + dy], 32, 8, natural(16))


def encode_inner_kernel(
    own, edge, pick, w_first, w_down, pool_near, pool_mid_near, for_twin_near, after,
    fine, pool_far, mid, pool_mid, for_twin, pool_s,
):
    def work(core):
        if core:
            field = jnp.concatenate([own[80:], edge[:48]], axis=0)
            pool_s[:, 0:2] = pool_near[:, 2:4]
        else:
            field = jnp.concatenate([edge[128:], own[:48]], axis=0)
            pool_s[:, 2:4] = pool_near[:, 0:2]
        pairs, far = ((3, 4), 2) if core else ((-1, 0), 0)
        encode(field, pick, w_first, pairs, fine, 6 if core else -1, pool_s, far)
        pool_far[...] = pool_s[:, far : far + 2]
        rows, pooled = middle_rows(pool_s, w_down, 2 if core else 0, 2)
        for at in range(2):
            for py in range(2):
                put_shifts(mid, at, py, rows[py][at])
        near = pool_mid_near[...].astype(F32)
        cells = (near, pooled[0]) if core else (pooled[0], near)
        for at in range(2):
            put_three(pool_mid, at, cells[at])
        for_twin[pl.ds(0, 4 * J), :] = for_twin_near[...]
        for_twin[pl.ds(4 * J, J), :] = jnp.concatenate(cells, axis=1).astype(BF)

    for_each_core(work)


def encode_outer_kernel(
    edge, pick, w_first, w_down, pool_far, after, mid, pool_mid, pool_s
):
    def work(core):
        field = edge[16:] if core else edge[:160]
        far, outer = (0, 2) if core else (4, 0)
        pairs = range(5, 9) if core else range(-5, -1)
        pool_s[:, far : far + 2] = pool_far[...]
        encode(field, pick, w_first, pairs, None, 0, pool_s, outer)
        rows, pooled = middle_rows(pool_s, w_down, 4 if core else -4, 4)
        for at in range(2):
            put_three(pool_mid, at, pooled[at])
            for py in range(2):
                put_shifts(mid, at, py, rows[py][at if core else at + 2])

    for_each_core(work)


def net_kernel(
    from_twin, fine_near, fine_far, skip_near, mid_near, mid_far, mid_out,
    pool_mid_in, pool_mid_out,
    w_coarse, w_mid_skip, w_mid_up, w_fine_skip, w_fine_up, w_head,
    out,
    fine_s, mid_s, pool_mid_s, coarse_s, up_s, skip_s, last_s,
):
    mask = y_mask()

    def gather(core):
        first, last = (6, 0) if core else (0, 6)
        near, far = (2, 4) if core else (4, 2)
        mid_s[:, first : first + 2] = mid_out[...]
        mid_s[:, near : near + 2], mid_s[:, far : far + 2] = mid_near[...], mid_far[...]
        cell = 4 if core else 0
        pool_mid_s[:, cell : cell + 2], pool_mid_s[:, 2:4] = pool_mid_out[...], pool_mid_in[...]
        for at in range(2):
            for py in range(2):
                row = (at * 2 + py) * J
                put_shifts(mid_s, last + at, py, from_twin[row : row + J].astype(F32))
            lanes = slice(at * 128, at * 128 + 128)
            put_three(pool_mid_s, 4 - cell + at, from_twin[4 * J :, lanes].astype(F32))
        if core:
            fine_s[:, 0:2], fine_s[:, 2:5] = fine_near[:, 5:7], fine_far[...]
        else:
            fine_s[:, 0:3], fine_s[:, 3:5] = fine_far[...], fine_near[:, 0:2]
        lhs = jnp.concatenate(
            [
                fine_s[dy : dy + 4, dx : dx + 3].reshape(384, 256)
                for dx in range(3)
                for dy in range(3)
            ],
            axis=1,
        )
        skip = dot(lhs, w_fine_skip[...]).reshape(4, 3, 32, 256)
        if core:
            skip_s[:, 0:5], skip_s[:, 5:8] = skip_near[...], skip
        else:
            skip_s[:, 0:3], skip_s[:, 3:8] = skip, skip_near[...]

    for_each_core(gather)

    lhs = jnp.concatenate(
        [
            pool_mid_s[dy, dx : dx + 4].reshape(4 * J, 128)
            for dx in range(3)
            for dy in range(3)
        ],
        axis=1,
    )
    value = silu_half(dot(lhs, w_coarse[...])).reshape(4, J, 256)
    for at in range(4):
        put_three(coarse_s, at, value[at] * (mask * row_flag(at - 1)))

    lhs = jnp.concatenate(
        [
            mid_s[dy : dy + 2, dx : dx + 6].reshape(12 * J, 256)
            for dx in range(3)
            for dy in range(3)
        ],
        axis=1,
    )
    skip = dot(lhs, w_mid_skip[...]).reshape(2, 6, J, 256)
    for py in range(2):
        lhs = jnp.concatenate(
            [
                coarse_s[py + ty, tx : tx + 3].reshape(3 * J, 256)
                for tx in range(2)
                for ty in range(2)
            ],
            axis=1,
        )
        for px in range(2):
            up = dot(lhs, w_mid_up[px * 2 + py]).reshape(3, J, 256)
            for k in range(3):
                at = 2 * k if px else 2 * k + 1
                value = silu_half(skip[py, at] + up[k])
                masked = value * (mask * row_flag((at - 1) // 2))
                up_s[py + 1, at] = masked[:32].astype(BF)
                shift = 1 if py else J - 1
                up_s[0 if py else 3, at] = pltpu.roll(masked, shift, 0)[:32].astype(BF)

    @pl.loop(0, 4)
    def _(parity):
        px, py = parity // 2, parity % 2
        lhs = jnp.concatenate(
            [
                up_s[pl.ds(py + ty, 2), pl.ds(px + tx, 4)].reshape(256, 256)
                for tx in range(2)
                for ty in range(2)
            ],
            axis=1,
        )
        up = dot(lhs, w_fine_up[parity]).reshape(2, 4, 32, 256)
        for half in range(2):
            group = 2 * half + py
            for k in range(4):
                value = silu_half(skip_s[group, 2 * k + px] + up[half, k])
                row = pl.multiple_of(group * 32, 32)
                last_s[2 * k + px, pl.ds(row, 32), :] = value.astype(BF)

    heads = jnp.concatenate([dot_nt(w_head[...], last_s[x]) for x in range(8)], axis=0)
    high = heads.astype(BF)
    rest = heads - high.astype(F32)
    low = rest.astype(BF)
    lowest = (rest - low.astype(F32)).astype(BF)
    row, col = iota((128, 128), 0), iota((128, 128), 1)
    order = (col == 4 * (row % 32) + row // 32).astype(BF)
    noise = dot(
        jnp.concatenate([high, low, lowest], axis=1),
        jnp.concatenate([order, order, order], axis=0),
    ).reshape(8, 16, 128)
    for x in range(8):
        out[:, x, :] = noise[x]


def body(
    noisy_field, first_weight, down_weight, coarse_weight, middle_weight, fine_weight, head_weight
):
    def shape(*dims, kind=BF):
        return jax.ShapeDtypeStruct(dims, kind)

    def cost(flops, moved):
        return pl.CostEstimate(flops=flops, bytes_accessed=moved, transcendentals=0)

    def small(limit):
        return pltpu.CompilerParams(vmem_limit_bytes=limit * 2**20)

    w_first, w_down, w_coarse, w_head, middle, fine, pick = pl.pallas_call(
        encoder_weights_kernel,
        out_shape=(
            shape(2, 192, 256),
            shape(1152, 256),
            shape(1152, 256),
            shape(16, 256),
            shape(27, 32, 96),
            shape(27, 16, 48),
            shape(4 * J, 256),
        ),
        in_specs=[ANY] * 6,
        out_specs=(VMEM,) * 7,
        scratch_shapes=[
            pltpu.VMEM((9, 3, 16), BF),
            pltpu.VMEM((27, 16, 32), BF),
            pltpu.VMEM((27, 32, 64), BF),
            pltpu.VMEM((1, 16), BF),
            pltpu.VMEM((27 * 32, 256), BF),
            pltpu.SemaphoreType.DMA((6,)),
        ],
        compiler_params=small(16),
        cost_estimate=cost(10**9, 3 * 10**6),
    )(
        *(
            pltpu.with_memory_space_constraint(weight, pltpu.HBM)
            for weight in (
                first_weight.transpose(1, 2, 3, 4, 0).reshape(9, 3, 16),
                down_weight.transpose(2, 3, 4, 1, 0).reshape(27, 16, 32),
                coarse_weight.transpose(2, 3, 4, 1, 0).reshape(27, 32, 64),
                middle_weight.transpose(2, 3, 4, 0, 1).reshape(27, 32, 96),
                fine_weight.transpose(2, 3, 4, 0, 1).reshape(27, 16, 48),
                head_weight.reshape(1, 16),
            )
        )
    )

    def pairs(axis):
        count = lax.axis_size(axis)
        inner = [(i, i ^ 1) for i in range(count)]
        return inner, [(i, ((i + 1) ^ 1) - 1) for i in range(1, count - 1)]

    swap_in, swap_out = pairs("gy")
    y_inner = lax.ppermute(noisy_field, "gy", swap_in)
    y_outer = lax.ppermute(noisy_field, "gy", swap_out)
    own = pl.pallas_call(
        join_kernel,
        out_shape=shape(128, 256),
        in_specs=[VMEM] * 3 + [ANY],
        out_specs=VMEM,
        compiler_params=small(4),
        cost_estimate=cost(10**7, 2 * 10**5),
    )(noisy_field, y_inner, y_outer, w_head)

    in_chip, between = pairs("gx")
    twin = lax.ppermute(own, "gx", in_chip)
    w_mid_skip, w_mid_up = pl.pallas_call(
        mid_weights_kernel,
        out_shape=(shape(2304, 256), shape(4, 1024, 256)),
        in_specs=[VMEM, ANY],
        out_specs=(VMEM,) * 2,
        scratch_shapes=[pltpu.VMEM((27, 96, 256), F32)],
        compiler_params=small(24),
        cost_estimate=cost(10**9, 4 * 10**6),
    )(middle, own)
    edge = pl.pallas_call(
        chip_edge_kernel,
        out_shape=shape(176, 256),
        in_specs=[VMEM] * 2 + [ANY],
        out_specs=VMEM,
        compiler_params=small(4),
        cost_estimate=cost(10**5, 3 * 10**5),
    )(own, twin, w_mid_skip)
    chip_edge = lax.ppermute(edge, "gx", between)

    fine_near, pool_near, mid_near, pool_mid_near, for_twin_near = pl.pallas_call(
        encode_near_kernel,
        out_shape=(
            shape(6, 7, 32, 256),
            shape(4, 4, J, 128),
            shape(4, 2, J, 256),
            shape(J, 128),
            shape(4 * J, 256),
        ),
        in_specs=[VMEM] * 5 + [ANY],
        out_specs=(VMEM,) * 5,
        compiler_params=small(16),
        cost_estimate=cost(10**9, 3 * 10**6),
    )(own, twin, pick, w_first, w_down, edge)
    w_fine_skip = pl.pallas_call(
        fine_weights_kernel,
        out_shape=shape(2304, 256),
        in_specs=[VMEM, ANY],
        out_specs=VMEM,
        compiler_params=small(16),
        cost_estimate=cost(10**9, 2 * 10**6),
    )(fine, edge)
    skip_near, w_fine_up = pl.pallas_call(
        skip_near_kernel,
        out_shape=(shape(4, 5, 32, 256, kind=F32), shape(4, 1024, 256)),
        in_specs=[VMEM] * 3,
        out_specs=(VMEM,) * 2,
        scratch_shapes=[pltpu.VMEM((27, 32, 256), F32)],
        compiler_params=small(16),
        cost_estimate=cost(10**9, 4 * 10**6),
    )(fine_near, fine, w_fine_skip)

    fine_far, pool_far, mid_far, pool_mid_in, for_twin = pl.pallas_call(
        encode_inner_kernel,
        out_shape=(
            shape(6, 3, 32, 256),
            shape(4, 2, J, 128),
            shape(4, 2, J, 256),
            shape(3, 2, J, 128),
            shape(5 * J, 256),
        ),
        in_specs=[VMEM] * 8 + [ANY],
        out_specs=(VMEM,) * 5,
        scratch_shapes=[pltpu.VMEM((4, 4, J, 128), BF)],
        compiler_params=small(16),
        cost_estimate=cost(10**9, 3 * 10**6),
    )(
        own, chip_edge, pick, w_first, w_down, pool_near, pool_mid_near, for_twin_near,
        skip_near,
    )
    from_twin = lax.ppermute(for_twin, "gx", in_chip)
    mid_out, pool_mid_out = pl.pallas_call(
        encode_outer_kernel,
        out_shape=(shape(4, 2, J, 256), shape(3, 2, J, 128)),
        in_specs=[VMEM] * 5 + [ANY],
        out_specs=(VMEM,) * 2,
        scratch_shapes=[pltpu.VMEM((4, 6, J, 128), BF)],
        compiler_params=small(16),
        cost_estimate=cost(2 * 10**9, 3 * 10**6),
    )(chip_edge, pick, w_first, w_down, pool_far, for_twin)

    return pl.pallas_call(
        net_kernel,
        out_shape=shape(16, 8, 128, kind=F32),
        in_specs=[VMEM] * 15,
        out_specs=VMEM,
        scratch_shapes=[
            pltpu.VMEM((6, 5, 32, 256), BF),
            pltpu.VMEM((4, 8, J, 256), BF),
            pltpu.VMEM((3, 6, J, 128), BF),
            pltpu.VMEM((3, 4, J, 256), BF),
            pltpu.VMEM((4, 6, 32, 256), BF),
            pltpu.VMEM((4, 8, 32, 256), F32),
            pltpu.VMEM((8, 128, 256), BF),
        ],
        compiler_params=small(32),
        cost_estimate=pl.CostEstimate(
            flops=6 * 10**9, bytes_accessed=9 * 10**6, transcendentals=10**6
        ),
    )(
        from_twin, fine_near, fine_far, skip_near, mid_near, mid_far, mid_out,
        pool_mid_in, pool_mid_out,
        w_coarse, w_mid_skip, w_mid_up, w_fine_skip, w_fine_up, w_head,
    )


def solution(mesh):
    placed = (P(None, "gx", "gy"), P(), P(), P(), P(), P(), P())
    return jax.shard_map(
        body, mesh=mesh, in_specs=placed, out_specs=P(None, "gx", "gy"), check_vma=False
    )
```

```python
import jax
import jax.numpy as jnp
from jax import lax
from jax.experimental import pallas as pl
from jax.experimental.pallas import tpu as pltpu
from jax.sharding import PartitionSpec as P

BF = jnp.bfloat16
F32 = jnp.float32
J = 40
VMEM = pl.BlockSpec(memory_space=pltpu.VMEM)
ANY = pl.BlockSpec(memory_space=pl.ANY)


def dot(a, b):
    return jnp.dot(a, b, preferred_element_type=F32)


def dot_nt(a, b):
    return lax.dot_general(a, b, (((1,), (1,)), ((), ())), preferred_element_type=F32)


def dot_tn(a, b):
    return lax.dot_general(a, b, (((0,), (0,)), ((), ())), preferred_element_type=F32)


def iota(shape, axis):
    return lax.broadcasted_iota(jnp.int32, shape, axis)


def natural(channels):
    return lambda lane: lane // channels


def halves(channels):
    return lambda lane: 2 * ((lane // channels) % (128 // channels)) + lane // 128


def repeat_matrix(channels):
    return (iota((channels, 256), 1) % channels == iota((channels, 256), 0)).astype(BF)


def ones_where(cond):
    return jnp.where(cond, 1.0, 0.0).astype(BF)


def tiles(depth_of):
    return [
        (slice(at, at + 128), {depth_of(lane) for lane in range(at, at + 128)})
        for at in (0, 128)
    ]


def place_block(out, index, row, rows, terms, places, held, lanes):
    total = None
    for depths, value in terms:
        depths = [depth for depth in depths if depth in held]
        if depths:
            mask = places[:, lanes] == depths[0]
            for depth in depths[1:]:
                mask = mask | (places[:, lanes] == depth)
            part = ones_where(mask) * value[:, lanes]
            total = part if total is None else total + part
    if total is None:
        total = jnp.zeros((rows, 128), BF)
    out[(*index, pl.ds(row, rows), lanes)] = total


def cell_of(j):
    return jnp.where(j < 36, j, j - J)


def cell_inside(axis, held, cell):
    at = lax.axis_index(axis) * held + cell
    return (at >= 0) & (at < lax.axis_size(axis) * held)


SETS = (((0,), (1, 2)), ((0, 1), (2,)))


def banded(out, taps, channels, row_depths, depth_of):
    size = channels * len(row_depths)
    places = depth_of(iota((channels, 256), 1))
    for lanes, held in tiles(depth_of):
        for at, depth in enumerate(row_depths):
            for xy in range(9):
                terms = [((depth + 1 - dz,), taps[dz][xy]) for dz in range(3)]
                row = xy * size + at * channels
                place_block(out, (), row, channels, terms, places, held, lanes)


def folded(out, get, channels, depths, depth_of):
    size = channels * depths
    places = depth_of(iota((channels, 256), 1))
    even = places % 2 == 0
    for px in range(2):
        for tx in range(2):
            by_y = [
                [sum(get(dz, dx, dy) for dx in SETS[px][tx]) for dy in range(3)]
                for dz in range(3)
            ]
            for py in range(2):
                for ty in range(2):
                    w0, w1, w2 = [
                        sum(by_y[dz][dy] for dy in SETS[py][ty]) for dz in range(3)
                    ]
                    inner = jnp.where(even, w1 + w2, w0 + w1).astype(BF)
                    outer = jnp.where(even, w0, w2).astype(BF)
                    for lanes, held in tiles(depth_of):
                        for depth in range(depths):
                            terms = [
                                ((2 * depth, 2 * depth + 1), inner),
                                ((2 * depth + 2, 2 * depth - 1), outer),
                            ]
                            row = (tx * 2 + ty) * size + depth * channels
                            index = (px * 2 + py,)
                            place_block(out, index, row, channels, terms, places, held, lanes)


def encoder_weights_kernel(
    raw_first, raw_down, raw_coarse, raw_middle, raw_fine, raw_head,
    w_first, w_down, w_coarse, w_head, middle, fine, pick,
    first, down, coarse, head, sems,
):
    copies = [
        pltpu.make_async_copy(source, target, sems.at[at])
        for at, (source, target) in enumerate(
            (
                (raw_first, first),
                (raw_down, down),
                (raw_coarse, coarse),
                (raw_head, head),
                (raw_middle, middle),
                (raw_fine, fine),
            )
        )
    ]
    for copy in copies:
        copy.start()
    r16, r32, r64 = repeat_matrix(16), repeat_matrix(32), repeat_matrix(64)
    row = iota((4 * J, 256), 0)
    cell = cell_of(row % J)
    inside = cell_inside("gy", 32, cell)
    pick[...] = ((iota((4 * J, 256), 1) == (4 * cell + row // J + 256) % 256) & inside).astype(BF)
    for copy in copies[:4]:
        copy.wait()

    w_first[...] = jnp.zeros_like(w_first)
    for dx in range(3):
        rows = [dot(first[dz * 3 + dx], r16) * 0.5 for dz in range(3)]
        place = halves(16)(iota((16, 256), 1))
        depth = iota((16, 256), 0)
        for dy in range(3):
            block = jnp.zeros((16, 256), F32)
            for dz in range(3):
                block = block + jnp.where(place == depth + 1 - dz, rows[dz][dy : dy + 1], 0.0)
            block = block.astype(BF)
            for even in range(2):
                w_first[even, pl.ds(dy * 64 + (even + dx) * 16, 16), :] = block

    flat = down[...].reshape(27 * 16, 32)
    all_taps = (dot(flat, r32) * (1 / 16)).astype(BF)
    taps = [[all_taps[(dz * 9 + xy) * 16 : (dz * 9 + xy + 1) * 16] for xy in range(9)] for dz in range(3)]
    banded(w_down, taps, 16, list(range(8)), halves(32))

    flat = coarse[...].reshape(27 * 32, 64)
    all_taps = (dot(flat, r64) * (1 / 16)).astype(BF)
    taps = [[all_taps[(dz * 9 + xy) * 32 : (dz * 9 + xy + 1) * 32] for xy in range(9)] for dz in range(3)]
    banded(w_coarse, taps, 32, list(range(4)), natural(64))

    row = dot(jnp.broadcast_to(head[...], (16, 16)), r16)
    w_head[...] = jnp.where(iota((16, 256), 1) // 16 == iota((16, 256), 0), row, 0.0).astype(BF)
    for copy in copies[4:]:
        copy.wait()


def mid_weights_kernel(middle, after, w_mid_skip, w_mid_up, tiled):
    r32 = repeat_matrix(32)
    for tap in range(27):
        tiled[tap] = dot_tn(middle[tap], r32) * 0.5
    taps = [[tiled[dz * 9 + xy, 64:96, :].astype(BF) for xy in range(9)] for dz in range(3)]
    banded(w_mid_skip, taps, 32, [0, 2, 4, 6, 1, 3, 5, 7], natural(32))
    folded(w_mid_up, lambda dz, dx, dy: tiled[dz * 9 + dx * 3 + dy, 0:64, :], 64, 4, natural(32))


def fine_weights_kernel(fine, after, w_fine_skip):
    r16 = repeat_matrix(16)
    tiled = [(dot_tn(fine[tap], r16)[32:] * 0.5).astype(BF) for tap in range(27)]
    taps = [tiled[dz * 9 : dz * 9 + 9] for dz in range(3)]
    banded(w_fine_skip, taps, 16, list(range(0, 16, 2)) + list(range(1, 16, 2)), natural(16))


def join_kernel(own, inner, outer, after, out):
    from_inner = (iota((128, 128), 1) < 64) == (lax.axis_index("gy") % 2 == 0)
    mine = own[...].astype(F32).reshape(128, 128)
    rim = jnp.where(
        from_inner,
        inner[...].astype(F32).reshape(128, 128),
        outer[...].astype(F32).reshape(128, 128),
    )
    both = jnp.concatenate([mine, rim], axis=1).astype(BF)
    row, col = iota((128, 128), 0), iota((128, 128), 1)
    swap = (col == (row % 16) * 8 + row // 16).astype(BF)
    out[...] = dot(swap, both).astype(BF)


def chip_edge_kernel(own, twin, after, out):
    odd = lax.axis_index("gx") % 2 == 1
    for_high = jnp.concatenate([twin[80:], own[...]], axis=0)
    for_low = jnp.concatenate([own[...], twin[:48]], axis=0)
    out[...] = jnp.where(odd, for_high, for_low)


def silu_half(h):
    return h + h * jnp.tanh(h)


def row_flag(cell):
    return jnp.where(cell_inside("gx", 2, cell), 1.0, 0.0)


def put_shifts(out, at, group, value):
    out[group + 1, at] = value.astype(BF)
    out[0 if group else 3, at] = pltpu.roll(value, 1 if group else J - 1, 0).astype(BF)


def put_three(out, at, value):
    out[0, at] = pltpu.roll(value, 1, 0).astype(BF)
    out[1, at] = value.astype(BF)
    out[2, at] = pltpu.roll(value, J - 1, 0).astype(BF)


def encode(field, pick, w_first, pairs, fine, first_x, pooled, pooled_at):
    wide = field.astype(F32)
    shifted = [pltpu.roll(wide, 1, 1).astype(BF), field, pltpu.roll(wide, 255, 1).astype(BF)]
    for at, m in enumerate(pairs):
        window = jnp.concatenate([part[at * 32 : at * 32 + 64] for part in shifted], axis=0)
        lhs = (dot_nt(pick[...], window) * row_flag(m // 2)).astype(BF)
        sums = [jnp.zeros((J, 128), F32) for _ in range(2)]
        for even in range(2):
            value = silu_half(dot(lhs, w_first[even])).reshape(4, J, 256)
            for part in range(2):
                both = value[2 * part] + value[2 * part + 1]
                sums[part] = sums[part] + both[:, :128] + both[:, 128:]
            x = 2 * m + even
            if fine is not None and -1 <= x <= 8:
                for group in range(4):
                    fine[group + 1, x - first_x] = value[group, :32].astype(BF)
                fine[0, x - first_x] = pltpu.roll(value[3], 1, 0)[:32].astype(BF)
                fine[5, x - first_x] = pltpu.roll(value[0], J - 1, 0)[:32].astype(BF)
        for part in range(2):
            put_shifts(pooled, pooled_at + at, part, sums[part])


def for_each_core(work):
    odd = lax.axis_index("gx") % 2

    @pl.when(odd == 0)
    def _():
        work(0)

    @pl.when(odd == 1)
    def _():
        work(1)


def middle_rows(pool_s, w_down, first, count):
    lhs = jnp.concatenate(
        [
            pool_s[dy : dy + 2, dx : dx + count].reshape(2 * count * J, 128)
            for dx in range(3)
            for dy in range(3)
        ],
        axis=1,
    )
    value = silu_half(dot(lhs, w_down[...])).reshape(2, count, J, 256)
    mask = y_mask()
    rows = [
        [value[py, at] * (mask * row_flag((first + at) // 2)) for at in range(count)]
        for py in range(2)
    ]
    pooled = []
    for at in range(0, count, 2):
        cells = rows[0][at] + rows[0][at + 1] + rows[1][at] + rows[1][at + 1]
        pooled.append(cells[:, :128] + cells[:, 128:])
    return rows, pooled


def y_mask():
    return jnp.where(cell_inside("gy", 32, cell_of(iota((J, 256), 0))), 1.0, 0.0)


def encode_near_kernel(
    own, twin, pick, w_first, w_down, after, fine, pooled, mid, pool_mid, for_twin
):
    def work(core):
        if core:
            field = jnp.concatenate([twin[80:], own[:112]], axis=0)
        else:
            field = jnp.concatenate([own[16:], twin[:48]], axis=0)
        pairs = range(-1, 3) if core else range(1, 5)
        encode(field, pick, w_first, pairs, fine, -1 if core else 2, pooled, 0)
        rows, cells = middle_rows(pooled, w_down, 0 if core else 2, 2)
        for at in range(2):
            for py in range(2):
                put_shifts(mid, at, py, rows[py][at])
                for_twin[pl.ds((at * 2 + py) * J, J), :] = rows[py][at].astype(BF)
        pool_mid[...] = cells[0].astype(BF)

    for_each_core(work)


def skip_near_kernel(fine_near, fine, w_fine_skip, out, w_fine_up, tiled):
    lhs = jnp.concatenate(
        [
            fine_near[dy : dy + 4, dx : dx + 5].reshape(640, 256)
            for dx in range(3)
            for dy in range(3)
        ],
        axis=1,
    )
    out[...] = dot(lhs, w_fine_skip[...]).reshape(4, 5, 32, 256)
    r16 = repeat_matrix(16)
    for tap in range(27):
        tiled[tap] = dot_tn(fine[tap], r16)[:32] * 0.5
    folded(w_fine_up, lambda dz, dx, dy: tiled[dz * 9 + dx * 3 + dy], 32, 8, natural(16))


def encode_far_kernel(
    own, edge, pick, w_first, w_down, pool_near, pool_mid_near, for_twin_near, after,
    fine, pool_far, mid, pool_mid, for_twin, pool_s,
):
    def work(core):
        parts = [own[80:], edge[...]] if core else [edge[...], own[:48]]
        field = jnp.concatenate(parts, axis=0)
        pairs = range(3, 9) if core else range(-5, 1)
        encode(field, pick, w_first, pairs, fine, 6 if core else -1, pool_far, 0)
        if core:
            pool_s[:, 0:2], pool_s[:, 2:4] = pool_near[:, 2:4], pool_far[:, 0:2]
        else:
            pool_s[:, 0:2], pool_s[:, 2:4] = pool_far[:, 4:6], pool_near[:, 0:2]
        rows, pooled = middle_rows(pool_s, w_down, 2 if core else 0, 2)
        for at in range(2):
            for py in range(2):
                put_shifts(mid, at, py, rows[py][at])
        near = pool_mid_near[...].astype(F32)
        cells = (near, pooled[0]) if core else (pooled[0], near)
        for at in range(2):
            put_three(pool_mid, at, cells[at])
        for_twin[pl.ds(0, 4 * J), :] = for_twin_near[...]
        for_twin[pl.ds(4 * J, J), :] = jnp.concatenate(cells, axis=1).astype(BF)

    for_each_core(work)


def middle_outer_kernel(
    pool_far, w_down, fine_near, fine_far, skip_near, w_fine_skip, after,
    mid, pool_mid, skip, fine_s,
):
    def work(core):
        rows, pooled = middle_rows(pool_far, w_down, 4 if core else -4, 4)
        for at in range(2):
            put_three(pool_mid, at, pooled[at])
            for py in range(2):
                put_shifts(mid, at, py, rows[py][at if core else at + 2])
        if core:
            fine_s[:, 0:2], fine_s[:, 2:5] = fine_near[:, 5:7], fine_far[...]
        else:
            fine_s[:, 0:3], fine_s[:, 3:5] = fine_far[...], fine_near[:, 0:2]
        lhs = jnp.concatenate(
            [
                fine_s[dy : dy + 4, dx : dx + 3].reshape(384, 256)
                for dx in range(3)
                for dy in range(3)
            ],
            axis=1,
        )
        near, far = (0, 5) if core else (3, 0)
        skip[:, far : far + 3] = dot(lhs, w_fine_skip[...]).reshape(4, 3, 32, 256)
        skip[:, near : near + 5] = skip_near[...]

    for_each_core(work)


def net_kernel(
    from_twin, skip_s, mid_near, mid_far, mid_out, pool_mid_in, pool_mid_out,
    w_coarse, w_mid_skip, w_mid_up, w_fine_up, w_head,
    out,
    mid_s, pool_mid_s, coarse_s, up_s, mid_skip_s, last_s,
):
    mask = y_mask()

    def gather(core):
        first, last = (6, 0) if core else (0, 6)
        near, far = (2, 4) if core else (4, 2)
        mid_s[:, first : first + 2] = mid_out[...]
        mid_s[:, near : near + 2], mid_s[:, far : far + 2] = mid_near[...], mid_far[...]
        cell = 4 if core else 0
        pool_mid_s[:, cell : cell + 2], pool_mid_s[:, 2:4] = pool_mid_out[...], pool_mid_in[...]
        for at in range(2):
            for py in range(2):
                row = (at * 2 + py) * J
                put_shifts(mid_s, last + at, py, from_twin[row : row + J].astype(F32))
            lanes = slice(at * 128, at * 128 + 128)
            put_three(pool_mid_s, 4 - cell + at, from_twin[4 * J :, lanes].astype(F32))

    for_each_core(gather)

    lhs = jnp.concatenate(
        [
            pool_mid_s[dy, dx : dx + 4].reshape(4 * J, 128)
            for dx in range(3)
            for dy in range(3)
        ],
        axis=1,
    )
    value = silu_half(dot(lhs, w_coarse[...])).reshape(4, J, 256)
    for at in range(4):
        put_three(coarse_s, at, value[at] * (mask * row_flag(at - 1)))

    lhs = jnp.concatenate(
        [
            mid_s[dy : dy + 2, dx : dx + 6].reshape(12 * J, 256)
            for dx in range(3)
            for dy in range(3)
        ],
        axis=1,
    )
    mid_skip_s[...] = dot(lhs, w_mid_skip[...]).reshape(2, 6, J, 256)

    @pl.loop(0, 2)
    def _(px):
        for py in range(2):
            lhs = jnp.concatenate(
                [
                    coarse_s[py + ty, tx : tx + 3].reshape(3 * J, 256)
                    for tx in range(2)
                    for ty in range(2)
                ],
                axis=1,
            )
            up = dot(lhs, w_mid_up[px * 2 + py]).reshape(3, J, 256)
            for k in range(3):
                at = 2 * k + 1 - px
                value = silu_half(mid_skip_s[py, at] + up[k])
                masked = value * (mask * row_flag(lax.shift_right_arithmetic(at - 1, 1)))
                up_s[py + 1, at] = masked[:32].astype(BF)
                shift = 1 if py else J - 1
                up_s[0 if py else 3, at] = pltpu.roll(masked, shift, 0)[:32].astype(BF)

    @pl.loop(0, 4)
    def _(parity):
        px, py = parity // 2, parity % 2
        lhs = jnp.concatenate(
            [
                up_s[pl.ds(py + ty, 2), pl.ds(px + tx, 4)].reshape(256, 256)
                for tx in range(2)
                for ty in range(2)
            ],
            axis=1,
        )
        up = dot(lhs, w_fine_up[parity]).reshape(2, 4, 32, 256)
        for half in range(2):
            group = 2 * half + py
            for k in range(4):
                value = silu_half(skip_s[group, 2 * k + px] + up[half, k])
                row = pl.multiple_of(group * 32, 32)
                last_s[2 * k + px, pl.ds(row, 32), :] = value.astype(BF)

    heads = jnp.concatenate([dot_nt(w_head[...], last_s[x]) for x in range(8)], axis=0)
    high = heads.astype(BF)
    rest = heads - high.astype(F32)
    low = rest.astype(BF)
    lowest = (rest - low.astype(F32)).astype(BF)
    row, col = iota((128, 128), 0), iota((128, 128), 1)
    order = (col == 4 * (row % 32) + row // 32).astype(BF)
    noise = dot(
        jnp.concatenate([high, low, lowest], axis=1),
        jnp.concatenate([order, order, order], axis=0),
    ).reshape(8, 16, 128)
    for x in range(8):
        out[:, x, :] = noise[x]


def body(
    noisy_field, first_weight, down_weight, coarse_weight, middle_weight, fine_weight, head_weight
):
    def shape(*dims, kind=BF):
        return jax.ShapeDtypeStruct(dims, kind)

    def cost(flops, moved):
        return pl.CostEstimate(flops=flops, bytes_accessed=moved, transcendentals=0)

    def small(limit):
        return pltpu.CompilerParams(vmem_limit_bytes=limit * 2**20)

    w_first, w_down, w_coarse, w_head, middle, fine, pick = pl.pallas_call(
        encoder_weights_kernel,
        out_shape=(
            shape(2, 192, 256),
            shape(1152, 256),
            shape(1152, 256),
            shape(16, 256),
            shape(27, 32, 96),
            shape(27, 16, 48),
            shape(4 * J, 256),
        ),
        in_specs=[ANY] * 6,
        out_specs=(VMEM,) * 7,
        scratch_shapes=[
            pltpu.VMEM((9, 3, 16), BF),
            pltpu.VMEM((27, 16, 32), BF),
            pltpu.VMEM((27, 32, 64), BF),
            pltpu.VMEM((1, 16), BF),
            pltpu.SemaphoreType.DMA((6,)),
        ],
        compiler_params=small(16),
        cost_estimate=cost(10**9, 3 * 10**6),
    )(
        *(
            pltpu.with_memory_space_constraint(weight, pltpu.HBM)
            for weight in (
                first_weight.transpose(1, 2, 3, 4, 0).reshape(9, 3, 16),
                down_weight.transpose(2, 3, 4, 1, 0).reshape(27, 16, 32),
                coarse_weight.transpose(2, 3, 4, 1, 0).reshape(27, 32, 64),
                middle_weight.transpose(2, 3, 4, 0, 1).reshape(27, 32, 96),
                fine_weight.transpose(2, 3, 4, 0, 1).reshape(27, 16, 48),
                head_weight.reshape(1, 16),
            )
        )
    )

    def pairs(axis):
        count = lax.axis_size(axis)
        inner = [(i, i ^ 1) for i in range(count)]
        return inner, [(i, ((i + 1) ^ 1) - 1) for i in range(1, count - 1)]

    swap_in, swap_out = pairs("gy")
    y_inner = lax.ppermute(noisy_field, "gy", swap_in)
    y_outer = lax.ppermute(noisy_field, "gy", swap_out)
    own = pl.pallas_call(
        join_kernel,
        out_shape=shape(128, 256),
        in_specs=[VMEM] * 3 + [ANY],
        out_specs=VMEM,
        compiler_params=small(4),
        cost_estimate=cost(10**7, 2 * 10**5),
    )(noisy_field, y_inner, y_outer, w_head)

    in_chip, between = pairs("gx")
    twin = lax.ppermute(own, "gx", in_chip)
    w_mid_skip, w_mid_up = pl.pallas_call(
        mid_weights_kernel,
        out_shape=(shape(2304, 256), shape(4, 1024, 256)),
        in_specs=[VMEM, ANY],
        out_specs=(VMEM,) * 2,
        scratch_shapes=[pltpu.VMEM((27, 96, 256), F32)],
        compiler_params=small(24),
        cost_estimate=cost(10**9, 4 * 10**6),
    )(middle, own)
    edge = pl.pallas_call(
        chip_edge_kernel,
        out_shape=shape(176, 256),
        in_specs=[VMEM] * 2 + [ANY],
        out_specs=VMEM,
        compiler_params=small(4),
        cost_estimate=cost(10**5, 3 * 10**5),
    )(own, twin, w_mid_skip)
    chip_edge = lax.ppermute(edge, "gx", between)

    fine_near, pool_near, mid_near, pool_mid_near, for_twin_near = pl.pallas_call(
        encode_near_kernel,
        out_shape=(
            shape(6, 7, 32, 256),
            shape(4, 4, J, 128),
            shape(4, 2, J, 256),
            shape(J, 128),
            shape(4 * J, 256),
        ),
        in_specs=[VMEM] * 5 + [ANY],
        out_specs=(VMEM,) * 5,
        compiler_params=small(16),
        cost_estimate=cost(10**9, 3 * 10**6),
    )(own, twin, pick, w_first, w_down, edge)
    w_fine_skip = pl.pallas_call(
        fine_weights_kernel,
        out_shape=shape(2304, 256),
        in_specs=[VMEM, ANY],
        out_specs=VMEM,
        compiler_params=small(16),
        cost_estimate=cost(10**9, 2 * 10**6),
    )(fine, edge)
    skip_near, w_fine_up = pl.pallas_call(
        skip_near_kernel,
        out_shape=(shape(4, 5, 32, 256, kind=F32), shape(4, 1024, 256)),
        in_specs=[VMEM] * 3,
        out_specs=(VMEM,) * 2,
        scratch_shapes=[pltpu.VMEM((27, 32, 256), F32)],
        compiler_params=small(16),
        cost_estimate=cost(10**9, 4 * 10**6),
    )(fine_near, fine, w_fine_skip)

    fine_far, pool_far, mid_far, pool_mid_in, for_twin = pl.pallas_call(
        encode_far_kernel,
        out_shape=(
            shape(6, 3, 32, 256),
            shape(4, 6, J, 128),
            shape(4, 2, J, 256),
            shape(3, 2, J, 128),
            shape(5 * J, 256),
        ),
        in_specs=[VMEM] * 8 + [ANY],
        out_specs=(VMEM,) * 5,
        scratch_shapes=[pltpu.VMEM((4, 4, J, 128), BF)],
        compiler_params=small(16),
        cost_estimate=cost(10**9, 3 * 10**6),
    )(
        own, chip_edge, pick, w_first, w_down, pool_near, pool_mid_near, for_twin_near,
        skip_near,
    )
    from_twin = lax.ppermute(for_twin, "gx", in_chip)
    mid_out, pool_mid_out, skip = pl.pallas_call(
        middle_outer_kernel,
        out_shape=(
            shape(4, 2, J, 256),
            shape(3, 2, J, 128),
            shape(4, 8, 32, 256, kind=F32),
        ),
        in_specs=[VMEM] * 6 + [ANY],
        out_specs=(VMEM,) * 3,
        scratch_shapes=[pltpu.VMEM((6, 5, 32, 256), BF)],
        compiler_params=small(16),
        cost_estimate=cost(2 * 10**9, 3 * 10**6),
    )(pool_far, w_down, fine_near, fine_far, skip_near, w_fine_skip, for_twin)

    return pl.pallas_call(
        net_kernel,
        out_shape=shape(16, 8, 128, kind=F32),
        in_specs=[VMEM] * 12,
        out_specs=VMEM,
        scratch_shapes=[
            pltpu.VMEM((4, 8, J, 256), BF),
            pltpu.VMEM((3, 6, J, 128), BF),
            pltpu.VMEM((3, 4, J, 256), BF),
            pltpu.VMEM((4, 6, 32, 256), BF),
            pltpu.VMEM((2, 6, J, 256), F32),
            pltpu.VMEM((8, 128, 256), BF),
        ],
        compiler_params=small(32),
        cost_estimate=pl.CostEstimate(
            flops=6 * 10**9, bytes_accessed=9 * 10**6, transcendentals=10**6
        ),
    )(
        from_twin, skip, mid_near, mid_far, mid_out, pool_mid_in, pool_mid_out,
        w_coarse, w_mid_skip, w_mid_up, w_fine_up, w_head,
    )


def solution(mesh):
    placed = (P(None, "gx", "gy"), P(), P(), P(), P(), P(), P())
    return jax.shard_map(
        body, mesh=mesh, in_specs=placed, out_specs=P(None, "gx", "gy"), check_vma=False
    )
```

```python
import jax
import jax.numpy as jnp
from jax import lax
from jax.experimental import pallas as pl
from jax.experimental.pallas import tpu as pltpu
from jax.sharding import PartitionSpec as P

BF = jnp.bfloat16
F32 = jnp.float32
J = 40
VMEM = pl.BlockSpec(memory_space=pltpu.VMEM)
ANY = pl.BlockSpec(memory_space=pl.ANY)


def dot(a, b):
    return jnp.dot(a, b, preferred_element_type=F32)


def dot_nt(a, b):
    return lax.dot_general(a, b, (((1,), (1,)), ((), ())), preferred_element_type=F32)


def dot_tn(a, b):
    return lax.dot_general(a, b, (((0,), (0,)), ((), ())), preferred_element_type=F32)


def iota(shape, axis):
    return lax.broadcasted_iota(jnp.int32, shape, axis)


def natural(channels):
    return lambda lane: lane // channels


def halves(channels):
    return lambda lane: 2 * ((lane // channels) % (128 // channels)) + lane // 128


def repeat_matrix(channels):
    return (iota((channels, 256), 1) % channels == iota((channels, 256), 0)).astype(BF)


def ones_where(cond):
    return jnp.where(cond, 1.0, 0.0).astype(BF)


def tiles(depth_of):
    return [
        (slice(at, at + 128), {depth_of(lane) for lane in range(at, at + 128)})
        for at in (0, 128)
    ]


def place_block(out, index, row, rows, terms, places, held, lanes):
    total = None
    for depths, value in terms:
        depths = [depth for depth in depths if depth in held]
        if depths:
            mask = places[:, lanes] == depths[0]
            for depth in depths[1:]:
                mask = mask | (places[:, lanes] == depth)
            part = ones_where(mask) * value[:, lanes]
            total = part if total is None else total + part
    if total is None:
        total = jnp.zeros((rows, 128), BF)
    out[(*index, pl.ds(row, rows), lanes)] = total


def cell_of(j):
    return jnp.where(j < 36, j, j - J)


def cell_inside(axis, held, cell):
    at = lax.axis_index(axis) * held + cell
    return (at >= 0) & (at < lax.axis_size(axis) * held)


SETS = (((0,), (1, 2)), ((0, 1), (2,)))


def banded(out, taps, channels, row_depths, depth_of):
    size = channels * len(row_depths)
    places = depth_of(iota((channels, 256), 1))
    for lanes, held in tiles(depth_of):
        for at, depth in enumerate(row_depths):
            for xy in range(9):
                terms = [((depth + 1 - dz,), taps[dz][xy]) for dz in range(3)]
                row = xy * size + at * channels
                place_block(out, (), row, channels, terms, places, held, lanes)


def folded(out, get, channels, depths, depth_of):
    size = channels * depths
    places = depth_of(iota((channels, 256), 1))
    even = places % 2 == 0
    for px in range(2):
        for tx in range(2):
            by_y = [
                [sum(get(dz, dx, dy) for dx in SETS[px][tx]) for dy in range(3)]
                for dz in range(3)
            ]
            for py in range(2):
                for ty in range(2):
                    w0, w1, w2 = [
                        sum(by_y[dz][dy] for dy in SETS[py][ty]) for dz in range(3)
                    ]
                    inner = jnp.where(even, w1 + w2, w0 + w1).astype(BF)
                    outer = jnp.where(even, w0, w2).astype(BF)
                    for lanes, held in tiles(depth_of):
                        for depth in range(depths):
                            terms = [
                                ((2 * depth, 2 * depth + 1), inner),
                                ((2 * depth + 2, 2 * depth - 1), outer),
                            ]
                            row = (tx * 2 + ty) * size + depth * channels
                            index = (px * 2 + py,)
                            place_block(out, index, row, channels, terms, places, held, lanes)


def encoder_weights_kernel(
    raw_first, raw_down, raw_coarse, raw_middle, raw_fine, raw_head,
    w_first, w_down, w_coarse, w_head, middle, fine, pick,
    first, down, coarse, head, sems,
):
    copies = [
        pltpu.make_async_copy(source, target, sems.at[at])
        for at, (source, target) in enumerate(
            (
                (raw_first, first),
                (raw_down, down),
                (raw_coarse, coarse),
                (raw_head, head),
                (raw_middle, middle),
                (raw_fine, fine),
            )
        )
    ]
    for copy in copies:
        copy.start()
    r16, r32, r64 = repeat_matrix(16), repeat_matrix(32), repeat_matrix(64)
    row = iota((4 * J, 256), 0)
    cell = cell_of(row % J)
    inside = cell_inside("gy", 32, cell)
    pick[...] = ((iota((4 * J, 256), 1) == (4 * cell + row // J + 256) % 256) & inside).astype(BF)
    for copy in copies[:4]:
        copy.wait()

    w_first[...] = jnp.zeros_like(w_first)
    for dx in range(3):
        rows = [dot(first[dz * 3 + dx], r16) * 0.5 for dz in range(3)]
        place = halves(16)(iota((16, 256), 1))
        depth = iota((16, 256), 0)
        for dy in range(3):
            block = jnp.zeros((16, 256), F32)
            for dz in range(3):
                block = block + jnp.where(place == depth + 1 - dz, rows[dz][dy : dy + 1], 0.0)
            block = block.astype(BF)
            for even in range(2):
                w_first[even, pl.ds(dy * 64 + (even + dx) * 16, 16), :] = block

    flat = down[...].reshape(27 * 16, 32)
    all_taps = (dot(flat, r32) * (1 / 16)).astype(BF)
    taps = [[all_taps[(dz * 9 + xy) * 16 : (dz * 9 + xy + 1) * 16] for xy in range(9)] for dz in range(3)]
    banded(w_down, taps, 16, list(range(8)), halves(32))

    flat = coarse[...].reshape(27 * 32, 64)
    all_taps = (dot(flat, r64) * (1 / 16)).astype(BF)
    taps = [[all_taps[(dz * 9 + xy) * 32 : (dz * 9 + xy + 1) * 32] for xy in range(9)] for dz in range(3)]
    banded(w_coarse, taps, 32, list(range(4)), natural(64))

    row = dot(jnp.broadcast_to(head[...], (16, 16)), r16)
    w_head[...] = jnp.where(iota((16, 256), 1) // 16 == iota((16, 256), 0), row, 0.0).astype(BF)
    for copy in copies[4:]:
        copy.wait()


def mid_weights_kernel(middle, after, w_mid_skip, w_mid_up, tiled):
    r32 = repeat_matrix(32)
    for tap in range(27):
        tiled[tap] = dot_tn(middle[tap], r32) * 0.5
    taps = [[tiled[dz * 9 + xy, 64:96, :].astype(BF) for xy in range(9)] for dz in range(3)]
    banded(w_mid_skip, taps, 32, [0, 2, 4, 6, 1, 3, 5, 7], natural(32))
    folded(w_mid_up, lambda dz, dx, dy: tiled[dz * 9 + dx * 3 + dy, 0:64, :], 64, 4, natural(32))


def fine_weights_kernel(fine, after, w_fine_skip):
    r16 = repeat_matrix(16)
    tiled = [(dot_tn(fine[tap], r16)[32:] * 0.5).astype(BF) for tap in range(27)]
    taps = [tiled[dz * 9 : dz * 9 + 9] for dz in range(3)]
    banded(w_fine_skip, taps, 16, list(range(0, 16, 2)) + list(range(1, 16, 2)), natural(16))


def join_kernel(own, outer, inner, after, out):
    from_inner = (iota((128, 128), 1) < 64) == (lax.axis_index("gy") % 2 == 0)
    mine = own[...].astype(F32).reshape(128, 128)
    rim = jnp.where(
        from_inner,
        inner[...].astype(F32).reshape(128, 128),
        outer[...].astype(F32).reshape(128, 128),
    )
    both = jnp.concatenate([mine, rim], axis=1).astype(BF)
    row, col = iota((128, 128), 0), iota((128, 128), 1)
    swap = (col == (row % 16) * 8 + row // 16).astype(BF)
    out[...] = dot(swap, both).astype(BF)


def chip_edge_kernel(own, twin, after, out):
    odd = lax.axis_index("gx") % 2 == 1
    for_high = jnp.concatenate([twin[80:], own[...]], axis=0)
    for_low = jnp.concatenate([own[...], twin[:48]], axis=0)
    out[...] = jnp.where(odd, for_high, for_low)


def silu_half(h):
    return h + h * jnp.tanh(h)


def row_flag(cell):
    return jnp.where(cell_inside("gx", 2, cell), 1.0, 0.0)


def put_shifts(out, at, group, value):
    out[group + 1, at] = value.astype(BF)
    out[0 if group else 3, at] = pltpu.roll(value, 1 if group else J - 1, 0).astype(BF)


def put_three(out, at, value):
    out[0, at] = pltpu.roll(value, 1, 0).astype(BF)
    out[1, at] = value.astype(BF)
    out[2, at] = pltpu.roll(value, J - 1, 0).astype(BF)


def encode(field, pick, w_first, pairs, fine, first_x, pooled, pooled_at):
    wide = field.astype(F32)
    shifted = [pltpu.roll(wide, 1, 1).astype(BF), field, pltpu.roll(wide, 255, 1).astype(BF)]
    for at, m in enumerate(pairs):
        window = jnp.concatenate([part[at * 32 : at * 32 + 64] for part in shifted], axis=0)
        lhs = (dot_nt(pick[...], window) * row_flag(m // 2)).astype(BF)
        sums = [jnp.zeros((J, 128), F32) for _ in range(2)]
        for even in range(2):
            value = silu_half(dot(lhs, w_first[even])).reshape(4, J, 256)
            for part in range(2):
                both = value[2 * part] + value[2 * part + 1]
                sums[part] = sums[part] + both[:, :128] + both[:, 128:]
            x = 2 * m + even
            if fine is not None and -1 <= x <= 8:
                for group in range(4):
                    fine[group + 1, x - first_x] = value[group, :32].astype(BF)
                fine[0, x - first_x] = pltpu.roll(value[3], 1, 0)[:32].astype(BF)
                fine[5, x - first_x] = pltpu.roll(value[0], J - 1, 0)[:32].astype(BF)
        for part in range(2):
            put_shifts(pooled, pooled_at + at, part, sums[part])


def for_each_core(work):
    odd = lax.axis_index("gx") % 2

    @pl.when(odd == 0)
    def _():
        work(0)

    @pl.when(odd == 1)
    def _():
        work(1)


def middle_rows(pool_s, w_down, first, count):
    lhs = jnp.concatenate(
        [
            pool_s[dy : dy + 2, dx : dx + count].reshape(2 * count * J, 128)
            for dx in range(3)
            for dy in range(3)
        ],
        axis=1,
    )
    value = silu_half(dot(lhs, w_down[...])).reshape(2, count, J, 256)
    mask = y_mask()
    rows = [
        [value[py, at] * (mask * row_flag((first + at) // 2)) for at in range(count)]
        for py in range(2)
    ]
    pooled = []
    for at in range(0, count, 2):
        cells = rows[0][at] + rows[0][at + 1] + rows[1][at] + rows[1][at + 1]
        pooled.append(cells[:, :128] + cells[:, 128:])
    return rows, pooled


def y_mask():
    return jnp.where(cell_inside("gy", 32, cell_of(iota((J, 256), 0))), 1.0, 0.0)


def encode_near_kernel(
    own, twin, pick, w_first, w_down, after, fine, pooled, mid, pool_mid, for_twin
):
    def work(core):
        if core:
            field = jnp.concatenate([twin[80:], own[:112]], axis=0)
        else:
            field = jnp.concatenate([own[16:], twin[:48]], axis=0)
        pairs = range(-1, 3) if core else range(1, 5)
        encode(field, pick, w_first, pairs, fine, -1 if core else 2, pooled, 0)
        rows, cells = middle_rows(pooled, w_down, 0 if core else 2, 2)
        for at in range(2):
            for py in range(2):
                put_shifts(mid, at, py, rows[py][at])
                for_twin[pl.ds((at * 2 + py) * J, J), :] = rows[py][at].astype(BF)
        pool_mid[...] = cells[0].astype(BF)

    for_each_core(work)


def skip_near_kernel(fine_near, fine, w_fine_skip, out, w_fine_up, tiled):
    lhs = jnp.concatenate(
        [
            fine_near[dy : dy + 4, dx : dx + 5].reshape(640, 256)
            for dx in range(3)
            for dy in range(3)
        ],
        axis=1,
    )
    out[...] = dot(lhs, w_fine_skip[...]).reshape(4, 5, 32, 256)
    r16 = repeat_matrix(16)
    for tap in range(27):
        tiled[tap] = dot_tn(fine[tap], r16)[:32] * 0.5
    folded(w_fine_up, lambda dz, dx, dy: tiled[dz * 9 + dx * 3 + dy], 32, 8, natural(16))


def encode_inner_kernel(
    own, edge, pick, w_first, w_down, pool_near, pool_mid_near, for_twin_near, after,
    fine, pool_far, mid, pool_mid, for_twin, pool_s,
):
    def work(core):
        if core:
            field = jnp.concatenate([own[80:], edge[:48]], axis=0)
            pool_s[:, 0:2] = pool_near[:, 2:4]
        else:
            field = jnp.concatenate([edge[128:], own[:48]], axis=0)
            pool_s[:, 2:4] = pool_near[:, 0:2]
        pairs, far = ((3, 4), 2) if core else ((-1, 0), 0)
        encode(field, pick, w_first, pairs, fine, 6 if core else -1, pool_s, far)
        pool_far[...] = pool_s[:, far : far + 2]
        rows, pooled = middle_rows(pool_s, w_down, 2 if core else 0, 2)
        for at in range(2):
            for py in range(2):
                put_shifts(mid, at, py, rows[py][at])
        near = pool_mid_near[...].astype(F32)
        cells = (near, pooled[0]) if core else (pooled[0], near)
        for at in range(2):
            put_three(pool_mid, at, cells[at])
        for_twin[pl.ds(0, 4 * J), :] = for_twin_near[...]
        for_twin[pl.ds(4 * J, J), :] = jnp.concatenate(cells, axis=1).astype(BF)

    for_each_core(work)


def encode_outer_kernel(
    edge, pick, w_first, w_down, pool_far, after, mid, pool_mid, pool_s
):
    def work(core):
        field = edge[16:] if core else edge[:160]
        far, outer = (0, 2) if core else (4, 0)
        pairs = range(5, 9) if core else range(-5, -1)
        pool_s[:, far : far + 2] = pool_far[...]
        encode(field, pick, w_first, pairs, None, 0, pool_s, outer)
        rows, pooled = middle_rows(pool_s, w_down, 4 if core else -4, 4)
        for at in range(2):
            put_three(pool_mid, at, pooled[at])
            for py in range(2):
                put_shifts(mid, at, py, rows[py][at if core else at + 2])

    for_each_core(work)


def net_kernel(
    from_twin, fine_near, fine_far, skip_near, mid_near, mid_far, mid_out,
    pool_mid_in, pool_mid_out,
    w_coarse, w_mid_skip, w_mid_up, w_fine_skip, w_fine_up, w_head,
    out,
    fine_s, mid_s, pool_mid_s, coarse_s, up_s, skip_s, last_s,
):
    mask = y_mask()

    def gather(core):
        first, last = (6, 0) if core else (0, 6)
        near, far = (2, 4) if core else (4, 2)
        mid_s[:, first : first + 2] = mid_out[...]
        mid_s[:, near : near + 2], mid_s[:, far : far + 2] = mid_near[...], mid_far[...]
        cell = 4 if core else 0
        pool_mid_s[:, cell : cell + 2], pool_mid_s[:, 2:4] = pool_mid_out[...], pool_mid_in[...]
        for at in range(2):
            for py in range(2):
                row = (at * 2 + py) * J
                put_shifts(mid_s, last + at, py, from_twin[row : row + J].astype(F32))
            lanes = slice(at * 128, at * 128 + 128)
            put_three(pool_mid_s, 4 - cell + at, from_twin[4 * J :, lanes].astype(F32))
        if core:
            fine_s[:, 0:2], fine_s[:, 2:5] = fine_near[:, 5:7], fine_far[...]
        else:
            fine_s[:, 0:3], fine_s[:, 3:5] = fine_far[...], fine_near[:, 0:2]
        lhs = jnp.concatenate(
            [
                fine_s[dy : dy + 4, dx : dx + 3].reshape(384, 256)
                for dx in range(3)
                for dy in range(3)
            ],
            axis=1,
        )
        skip = dot(lhs, w_fine_skip[...]).reshape(4, 3, 32, 256)
        if core:
            skip_s[:, 0:5], skip_s[:, 5:8] = skip_near[...], skip
        else:
            skip_s[:, 0:3], skip_s[:, 3:8] = skip, skip_near[...]

    for_each_core(gather)

    lhs = jnp.concatenate(
        [
            pool_mid_s[dy, dx : dx + 4].reshape(4 * J, 128)
            for dx in range(3)
            for dy in range(3)
        ],
        axis=1,
    )
    value = silu_half(dot(lhs, w_coarse[...])).reshape(4, J, 256)
    for at in range(4):
        put_three(coarse_s, at, value[at] * (mask * row_flag(at - 1)))

    lhs = jnp.concatenate(
        [
            mid_s[dy : dy + 2, dx : dx + 6].reshape(12 * J, 256)
            for dx in range(3)
            for dy in range(3)
        ],
        axis=1,
    )
    skip = dot(lhs, w_mid_skip[...]).reshape(2, 6, J, 256)
    for py in range(2):
        lhs = jnp.concatenate(
            [
                coarse_s[py + ty, tx : tx + 3].reshape(3 * J, 256)
                for tx in range(2)
                for ty in range(2)
            ],
            axis=1,
        )
        for px in range(2):
            up = dot(lhs, w_mid_up[px * 2 + py]).reshape(3, J, 256)
            for k in range(3):
                at = 2 * k if px else 2 * k + 1
                value = silu_half(skip[py, at] + up[k])
                masked = value * (mask * row_flag((at - 1) // 2))
                up_s[py + 1, at] = masked[:32].astype(BF)
                shift = 1 if py else J - 1
                up_s[0 if py else 3, at] = pltpu.roll(masked, shift, 0)[:32].astype(BF)

    @pl.loop(0, 4)
    def _(parity):
        px, py = parity // 2, parity % 2
        lhs = jnp.concatenate(
            [
                up_s[pl.ds(py + ty, 2), pl.ds(px + tx, 4)].reshape(256, 256)
                for tx in range(2)
                for ty in range(2)
            ],
            axis=1,
        )
        up = dot(lhs, w_fine_up[parity]).reshape(2, 4, 32, 256)
        for half in range(2):
            group = 2 * half + py
            for k in range(4):
                value = silu_half(skip_s[group, 2 * k + px] + up[half, k])
                row = pl.multiple_of(group * 32, 32)
                last_s[2 * k + px, pl.ds(row, 32), :] = value.astype(BF)

    heads = jnp.concatenate([dot_nt(w_head[...], last_s[x]) for x in range(8)], axis=0)
    high = heads.astype(BF)
    rest = heads - high.astype(F32)
    low = rest.astype(BF)
    lowest = (rest - low.astype(F32)).astype(BF)
    row, col = iota((128, 128), 0), iota((128, 128), 1)
    order = (col == 4 * (row % 32) + row // 32).astype(BF)
    noise = dot(
        jnp.concatenate([high, low, lowest], axis=1),
        jnp.concatenate([order, order, order], axis=0),
    ).reshape(8, 16, 128)
    for x in range(8):
        out[:, x, :] = noise[x]


def body(
    noisy_field, first_weight, down_weight, coarse_weight, middle_weight, fine_weight, head_weight
):
    def shape(*dims, kind=BF):
        return jax.ShapeDtypeStruct(dims, kind)

    def cost(flops, moved):
        return pl.CostEstimate(flops=flops, bytes_accessed=moved, transcendentals=0)

    def small(limit):
        return pltpu.CompilerParams(vmem_limit_bytes=limit * 2**20)

    w_first, w_down, w_coarse, w_head, middle, fine, pick = pl.pallas_call(
        encoder_weights_kernel,
        out_shape=(
            shape(2, 192, 256),
            shape(1152, 256),
            shape(1152, 256),
            shape(16, 256),
            shape(27, 32, 96),
            shape(27, 16, 48),
            shape(4 * J, 256),
        ),
        in_specs=[ANY] * 6,
        out_specs=(VMEM,) * 7,
        scratch_shapes=[
            pltpu.VMEM((9, 3, 16), BF),
            pltpu.VMEM((27, 16, 32), BF),
            pltpu.VMEM((27, 32, 64), BF),
            pltpu.VMEM((1, 16), BF),
            pltpu.SemaphoreType.DMA((6,)),
        ],
        compiler_params=small(16),
        cost_estimate=cost(10**9, 3 * 10**6),
    )(
        *(
            pltpu.with_memory_space_constraint(weight, pltpu.HBM)
            for weight in (
                first_weight.transpose(1, 2, 3, 4, 0).reshape(9, 3, 16),
                down_weight.transpose(2, 3, 4, 1, 0).reshape(27, 16, 32),
                coarse_weight.transpose(2, 3, 4, 1, 0).reshape(27, 32, 64),
                middle_weight.transpose(2, 3, 4, 0, 1).reshape(27, 32, 96),
                fine_weight.transpose(2, 3, 4, 0, 1).reshape(27, 16, 48),
                head_weight.reshape(1, 16),
            )
        )
    )

    def pairs(axis):
        count = lax.axis_size(axis)
        inner = [(i, i ^ 1) for i in range(count)]
        return inner, [(i, ((i + 1) ^ 1) - 1) for i in range(1, count - 1)]

    swap_in, swap_out = pairs("gy")
    y_outer = lax.ppermute(noisy_field, "gy", swap_out)
    y_inner = lax.ppermute(noisy_field, "gy", swap_in)
    own = pl.pallas_call(
        join_kernel,
        out_shape=shape(128, 256),
        in_specs=[VMEM] * 3 + [ANY],
        out_specs=VMEM,
        compiler_params=small(4),
        cost_estimate=cost(10**7, 2 * 10**5),
    )(noisy_field, y_outer, y_inner, w_head)

    in_chip, between = pairs("gx")
    twin = lax.ppermute(own, "gx", in_chip)
    w_mid_skip, w_mid_up = pl.pallas_call(
        mid_weights_kernel,
        out_shape=(shape(2304, 256), shape(4, 1024, 256)),
        in_specs=[VMEM, ANY],
        out_specs=(VMEM,) * 2,
        scratch_shapes=[pltpu.VMEM((27, 96, 256), F32)],
        compiler_params=small(24),
        cost_estimate=cost(10**9, 4 * 10**6),
    )(middle, own)
    edge = pl.pallas_call(
        chip_edge_kernel,
        out_shape=shape(176, 256),
        in_specs=[VMEM] * 2 + [ANY],
        out_specs=VMEM,
        compiler_params=small(4),
        cost_estimate=cost(10**5, 3 * 10**5),
    )(own, twin, w_mid_skip)
    chip_edge = lax.ppermute(edge, "gx", between)

    fine_near, pool_near, mid_near, pool_mid_near, for_twin_near = pl.pallas_call(
        encode_near_kernel,
        out_shape=(
            shape(6, 7, 32, 256),
            shape(4, 4, J, 128),
            shape(4, 2, J, 256),
            shape(J, 128),
            shape(4 * J, 256),
        ),
        in_specs=[VMEM] * 5 + [ANY],
        out_specs=(VMEM,) * 5,
        compiler_params=small(16),
        cost_estimate=cost(10**9, 3 * 10**6),
    )(own, twin, pick, w_first, w_down, edge)
    w_fine_skip = pl.pallas_call(
        fine_weights_kernel,
        out_shape=shape(2304, 256),
        in_specs=[VMEM, ANY],
        out_specs=VMEM,
        compiler_params=small(16),
        cost_estimate=cost(10**9, 2 * 10**6),
    )(fine, edge)
    skip_near, w_fine_up = pl.pallas_call(
        skip_near_kernel,
        out_shape=(shape(4, 5, 32, 256, kind=F32), shape(4, 1024, 256)),
        in_specs=[VMEM] * 3,
        out_specs=(VMEM,) * 2,
        scratch_shapes=[pltpu.VMEM((27, 32, 256), F32)],
        compiler_params=small(16),
        cost_estimate=cost(10**9, 4 * 10**6),
    )(fine_near, fine, w_fine_skip)

    fine_far, pool_far, mid_far, pool_mid_in, for_twin = pl.pallas_call(
        encode_inner_kernel,
        out_shape=(
            shape(6, 3, 32, 256),
            shape(4, 2, J, 128),
            shape(4, 2, J, 256),
            shape(3, 2, J, 128),
            shape(5 * J, 256),
        ),
        in_specs=[VMEM] * 8 + [ANY],
        out_specs=(VMEM,) * 5,
        scratch_shapes=[pltpu.VMEM((4, 4, J, 128), BF)],
        compiler_params=small(16),
        cost_estimate=cost(10**9, 3 * 10**6),
    )(
        own, chip_edge, pick, w_first, w_down, pool_near, pool_mid_near, for_twin_near,
        skip_near,
    )
    from_twin = lax.ppermute(for_twin, "gx", in_chip)
    mid_out, pool_mid_out = pl.pallas_call(
        encode_outer_kernel,
        out_shape=(shape(4, 2, J, 256), shape(3, 2, J, 128)),
        in_specs=[VMEM] * 5 + [ANY],
        out_specs=(VMEM,) * 2,
        scratch_shapes=[pltpu.VMEM((4, 6, J, 128), BF)],
        compiler_params=small(16),
        cost_estimate=cost(2 * 10**9, 3 * 10**6),
    )(chip_edge, pick, w_first, w_down, pool_far, for_twin)

    return pl.pallas_call(
        net_kernel,
        out_shape=shape(16, 8, 128, kind=F32),
        in_specs=[VMEM] * 15,
        out_specs=VMEM,
        scratch_shapes=[
            pltpu.VMEM((6, 5, 32, 256), BF),
            pltpu.VMEM((4, 8, J, 256), BF),
            pltpu.VMEM((3, 6, J, 128), BF),
            pltpu.VMEM((3, 4, J, 256), BF),
            pltpu.VMEM((4, 6, 32, 256), BF),
            pltpu.VMEM((4, 8, 32, 256), F32),
            pltpu.VMEM((8, 128, 256), BF),
        ],
        compiler_params=small(32),
        cost_estimate=pl.CostEstimate(
            flops=6 * 10**9, bytes_accessed=9 * 10**6, transcendentals=10**6
        ),
    )(
        from_twin, fine_near, fine_far, skip_near, mid_near, mid_far, mid_out,
        pool_mid_in, pool_mid_out,
        w_coarse, w_mid_skip, w_mid_up, w_fine_skip, w_fine_up, w_head,
    )


def solution(mesh):
    placed = (P(None, "gx", "gy"), P(), P(), P(), P(), P(), P())
    return jax.shard_map(
        body, mesh=mesh, in_specs=placed, out_specs=P(None, "gx", "gy"), check_vma=False
    )
```

```python
import jax
import jax.numpy as jnp
from jax import lax
from jax.experimental import pallas as pl
from jax.experimental.pallas import tpu as pltpu
from jax.sharding import PartitionSpec as P

BF = jnp.bfloat16
F32 = jnp.float32
J = 40
VMEM = pl.BlockSpec(memory_space=pltpu.VMEM)
ANY = pl.BlockSpec(memory_space=pl.ANY)


def dot(a, b):
    return jnp.dot(a, b, preferred_element_type=F32)


def dot_nt(a, b):
    return lax.dot_general(a, b, (((1,), (1,)), ((), ())), preferred_element_type=F32)


def dot_tn(a, b):
    return lax.dot_general(a, b, (((0,), (0,)), ((), ())), preferred_element_type=F32)


def iota(shape, axis):
    return lax.broadcasted_iota(jnp.int32, shape, axis)


def natural(channels):
    return lambda lane: lane // channels


def halves(channels):
    return lambda lane: 2 * ((lane // channels) % (128 // channels)) + lane // 128


def repeat_matrix(channels):
    return (iota((channels, 256), 1) % channels == iota((channels, 256), 0)).astype(BF)


def ones_where(cond):
    return jnp.where(cond, 1.0, 0.0).astype(BF)


def tiles(depth_of):
    return [
        (slice(at, at + 128), {depth_of(lane) for lane in range(at, at + 128)})
        for at in (0, 128)
    ]


def place_block(out, index, row, rows, terms, places, held, lanes):
    total = None
    for depths, value in terms:
        depths = [depth for depth in depths if depth in held]
        if depths:
            mask = places[:, lanes] == depths[0]
            for depth in depths[1:]:
                mask = mask | (places[:, lanes] == depth)
            part = ones_where(mask) * value[:, lanes]
            total = part if total is None else total + part
    if total is None:
        total = jnp.zeros((rows, 128), BF)
    out[(*index, pl.ds(row, rows), lanes)] = total


def cell_of(j):
    return jnp.where(j < 36, j, j - J)


def cell_inside(axis, held, cell):
    at = lax.axis_index(axis) * held + cell
    return (at >= 0) & (at < lax.axis_size(axis) * held)


SETS = (((0,), (1, 2)), ((0, 1), (2,)))


def banded(out, taps, channels, row_depths, depth_of):
    size = channels * len(row_depths)
    places = depth_of(iota((channels, 256), 1))
    for lanes, held in tiles(depth_of):
        for at, depth in enumerate(row_depths):
            for xy in range(9):
                terms = [((depth + 1 - dz,), taps[dz][xy]) for dz in range(3)]
                row = xy * size + at * channels
                place_block(out, (), row, channels, terms, places, held, lanes)


def folded(out, get, channels, depths, depth_of):
    size = channels * depths
    places = depth_of(iota((channels, 256), 1))
    even = places % 2 == 0
    for px in range(2):
        for tx in range(2):
            by_y = [
                [sum(get(dz, dx, dy) for dx in SETS[px][tx]) for dy in range(3)]
                for dz in range(3)
            ]
            for py in range(2):
                for ty in range(2):
                    w0, w1, w2 = [
                        sum(by_y[dz][dy] for dy in SETS[py][ty]) for dz in range(3)
                    ]
                    inner = jnp.where(even, w1 + w2, w0 + w1).astype(BF)
                    outer = jnp.where(even, w0, w2).astype(BF)
                    for lanes, held in tiles(depth_of):
                        for depth in range(depths):
                            terms = [
                                ((2 * depth, 2 * depth + 1), inner),
                                ((2 * depth + 2, 2 * depth - 1), outer),
                            ]
                            row = (tx * 2 + ty) * size + depth * channels
                            index = (px * 2 + py,)
                            place_block(out, index, row, channels, terms, places, held, lanes)


def encoder_weights_kernel(
    raw_first, raw_down, raw_coarse, raw_middle, raw_fine, raw_head,
    w_first, w_down, w_coarse, w_head, middle, fine, pick,
    first, down, coarse, head, sems,
):
    copies = [
        pltpu.make_async_copy(source, target, sems.at[at])
        for at, (source, target) in enumerate(
            (
                (raw_first, first),
                (raw_down, down),
                (raw_coarse, coarse),
                (raw_head, head),
                (raw_middle, middle),
                (raw_fine, fine),
            )
        )
    ]
    for copy in copies:
        copy.start()
    r16, r32, r64 = repeat_matrix(16), repeat_matrix(32), repeat_matrix(64)
    row = iota((4 * J, 256), 0)
    cell = cell_of(row % J)
    inside = cell_inside("gy", 32, cell)
    pick[...] = ((iota((4 * J, 256), 1) == (4 * cell + row // J + 256) % 256) & inside).astype(BF)
    for copy in copies[:4]:
        copy.wait()

    w_first[...] = jnp.zeros_like(w_first)
    for dx in range(3):
        rows = [dot(first[dz * 3 + dx], r16) * 0.5 for dz in range(3)]
        place = halves(16)(iota((16, 256), 1))
        depth = iota((16, 256), 0)
        for dy in range(3):
            block = jnp.zeros((16, 256), F32)
            for dz in range(3):
                block = block + jnp.where(place == depth + 1 - dz, rows[dz][dy : dy + 1], 0.0)
            block = block.astype(BF)
            for even in range(2):
                w_first[even, pl.ds(dy * 64 + (even + dx) * 16, 16), :] = block

    flat = down[...].reshape(27 * 16, 32)
    all_taps = (dot(flat, r32) * (1 / 16)).astype(BF)
    taps = [[all_taps[(dz * 9 + xy) * 16 : (dz * 9 + xy + 1) * 16] for xy in range(9)] for dz in range(3)]
    banded(w_down, taps, 16, list(range(8)), halves(32))

    flat = coarse[...].reshape(27 * 32, 64)
    all_taps = (dot(flat, r64) * (1 / 16)).astype(BF)
    taps = [[all_taps[(dz * 9 + xy) * 32 : (dz * 9 + xy + 1) * 32] for xy in range(9)] for dz in range(3)]
    banded(w_coarse, taps, 32, list(range(4)), natural(64))

    row = dot(jnp.broadcast_to(head[...], (16, 16)), r16)
    w_head[...] = jnp.where(iota((16, 256), 1) // 16 == iota((16, 256), 0), row, 0.0).astype(BF)
    for copy in copies[4:]:
        copy.wait()


def mid_skip_weights_kernel(middle, w_mid_skip):
    r32 = repeat_matrix(32)
    tiled = [(dot_tn(middle[tap], r32)[64:] * 0.5).astype(BF) for tap in range(27)]
    taps = [tiled[dz * 9 : dz * 9 + 9] for dz in range(3)]
    banded(w_mid_skip, taps, 32, [0, 2, 4, 6, 1, 3, 5, 7], natural(32))


def mid_up_weights_kernel(middle, after, w_mid_up, tiled):
    r32 = repeat_matrix(32)
    for tap in range(27):
        tiled[tap] = dot_tn(middle[tap], r32)[:64] * 0.5
    folded(w_mid_up, lambda dz, dx, dy: tiled[dz * 9 + dx * 3 + dy], 64, 4, natural(32))


def fine_weights_kernel(fine, after, w_fine_skip):
    r16 = repeat_matrix(16)
    tiled = [(dot_tn(fine[tap], r16)[32:] * 0.5).astype(BF) for tap in range(27)]
    taps = [tiled[dz * 9 : dz * 9 + 9] for dz in range(3)]
    banded(w_fine_skip, taps, 16, list(range(0, 16, 2)) + list(range(1, 16, 2)), natural(16))


def join_kernel(own, outer, inner, after, also_after, out):
    from_inner = (iota((128, 128), 1) < 64) == (lax.axis_index("gy") % 2 == 0)
    mine = own[...].astype(F32).reshape(128, 128)
    rim = jnp.where(
        from_inner,
        inner[...].astype(F32).reshape(128, 128),
        outer[...].astype(F32).reshape(128, 128),
    )
    both = jnp.concatenate([mine, rim], axis=1).astype(BF)
    row, col = iota((128, 128), 0), iota((128, 128), 1)
    swap = (col == (row % 16) * 8 + row // 16).astype(BF)
    out[...] = dot(swap, both).astype(BF)


def chip_edge_kernel(own, twin, after, out):
    odd = lax.axis_index("gx") % 2 == 1
    for_high = jnp.concatenate([twin[80:], own[...]], axis=0)
    for_low = jnp.concatenate([own[...], twin[:48]], axis=0)
    out[...] = jnp.where(odd, for_high, for_low)


def silu_half(h):
    return h + h * jnp.tanh(h)


def row_flag(cell):
    return jnp.where(cell_inside("gx", 2, cell), 1.0, 0.0)


def put_shifts(out, at, group, value):
    out[group + 1, at] = value.astype(BF)
    out[0 if group else 3, at] = pltpu.roll(value, 1 if group else J - 1, 0).astype(BF)


def put_three(out, at, value):
    out[0, at] = pltpu.roll(value, 1, 0).astype(BF)
    out[1, at] = value.astype(BF)
    out[2, at] = pltpu.roll(value, J - 1, 0).astype(BF)


def encode(field, pick, w_first, pairs, fine, first_x, pooled, pooled_at):
    wide = field.astype(F32)
    shifted = [pltpu.roll(wide, 1, 1).astype(BF), field, pltpu.roll(wide, 255, 1).astype(BF)]
    for at, m in enumerate(pairs):
        window = jnp.concatenate([part[at * 32 : at * 32 + 64] for part in shifted], axis=0)
        lhs = (dot_nt(pick[...], window) * row_flag(m // 2)).astype(BF)
        sums = [jnp.zeros((J, 128), F32) for _ in range(2)]
        for even in range(2):
            value = silu_half(dot(lhs, w_first[even])).reshape(4, J, 256)
            for part in range(2):
                both = value[2 * part] + value[2 * part + 1]
                sums[part] = sums[part] + both[:, :128] + both[:, 128:]
            x = 2 * m + even
            if fine is not None and -1 <= x <= 8:
                for group in range(4):
                    fine[group + 1, x - first_x] = value[group, :32].astype(BF)
                fine[0, x - first_x] = pltpu.roll(value[3], 1, 0)[:32].astype(BF)
                fine[5, x - first_x] = pltpu.roll(value[0], J - 1, 0)[:32].astype(BF)
        for part in range(2):
            put_shifts(pooled, pooled_at + at, part, sums[part])


def for_each_core(work):
    odd = lax.axis_index("gx") % 2

    @pl.when(odd == 0)
    def _():
        work(0)

    @pl.when(odd == 1)
    def _():
        work(1)


def middle_rows(pool_s, w_down, first, count):
    lhs = jnp.concatenate(
        [
            pool_s[dy : dy + 2, dx : dx + count].reshape(2 * count * J, 128)
            for dx in range(3)
            for dy in range(3)
        ],
        axis=1,
    )
    value = silu_half(dot(lhs, w_down[...])).reshape(2, count, J, 256)
    mask = y_mask()
    rows = [
        [value[py, at] * (mask * row_flag((first + at) // 2)) for at in range(count)]
        for py in range(2)
    ]
    pooled = []
    for at in range(0, count, 2):
        cells = rows[0][at] + rows[0][at + 1] + rows[1][at] + rows[1][at + 1]
        pooled.append(cells[:, :128] + cells[:, 128:])
    return rows, pooled


def y_mask():
    return jnp.where(cell_inside("gy", 32, cell_of(iota((J, 256), 0))), 1.0, 0.0)


def encode_near_kernel(
    own, twin, pick, w_first, w_down, after, fine, pooled, mid, pool_mid, for_twin
):
    def work(core):
        if core:
            field = jnp.concatenate([twin[80:], own[:112]], axis=0)
        else:
            field = jnp.concatenate([own[16:], twin[:48]], axis=0)
        pairs = range(-1, 3) if core else range(1, 5)
        encode(field, pick, w_first, pairs, fine, -1 if core else 2, pooled, 0)
        rows, cells = middle_rows(pooled, w_down, 0 if core else 2, 2)
        for at in range(2):
            for py in range(2):
                put_shifts(mid, at, py, rows[py][at])
                for_twin[pl.ds((at * 2 + py) * J, J), :] = rows[py][at].astype(BF)
        pool_mid[...] = cells[0].astype(BF)

    for_each_core(work)


def skip_near_kernel(fine_near, fine, w_fine_skip, out, w_fine_up, tiled):
    lhs = jnp.concatenate(
        [
            fine_near[dy : dy + 4, dx : dx + 5].reshape(640, 256)
            for dx in range(3)
            for dy in range(3)
        ],
        axis=1,
    )
    out[...] = dot(lhs, w_fine_skip[...]).reshape(4, 5, 32, 256)
    r16 = repeat_matrix(16)
    for tap in range(27):
        tiled[tap] = dot_tn(fine[tap], r16)[:32] * 0.5
    folded(w_fine_up, lambda dz, dx, dy: tiled[dz * 9 + dx * 3 + dy], 32, 8, natural(16))


def encode_inner_kernel(
    own, edge, pick, w_first, w_down, pool_near, pool_mid_near, for_twin_near, after,
    fine, pool_far, mid, pool_mid, for_twin, pool_s,
):
    def work(core):
        if core:
            field = jnp.concatenate([own[80:], edge[:48]], axis=0)
            pool_s[:, 0:2] = pool_near[:, 2:4]
        else:
            field = jnp.concatenate([edge[128:], own[:48]], axis=0)
            pool_s[:, 2:4] = pool_near[:, 0:2]
        pairs, far = ((3, 4), 2) if core else ((-1, 0), 0)
        encode(field, pick, w_first, pairs, fine, 6 if core else -1, pool_s, far)
        pool_far[...] = pool_s[:, far : far + 2]
        rows, pooled = middle_rows(pool_s, w_down, 2 if core else 0, 2)
        for at in range(2):
            for py in range(2):
                put_shifts(mid, at, py, rows[py][at])
        near = pool_mid_near[...].astype(F32)
        cells = (near, pooled[0]) if core else (pooled[0], near)
        for at in range(2):
            put_three(pool_mid, at, cells[at])
        for_twin[pl.ds(0, 4 * J), :] = for_twin_near[...]
        for_twin[pl.ds(4 * J, J), :] = jnp.concatenate(cells, axis=1).astype(BF)

    for_each_core(work)


def encode_outer_kernel(
    edge, pick, w_first, w_down, pool_far, fine_near, fine_far, skip_near, w_fine_skip, after,
    mid, pool_mid, skip, pool_s, fine_s,
):
    def work(core):
        if core:
            fine_s[:, 0:2], fine_s[:, 2:5] = fine_near[:, 5:7], fine_far[...]
        else:
            fine_s[:, 0:3], fine_s[:, 3:5] = fine_far[...], fine_near[:, 0:2]
        field = edge[16:] if core else edge[:160]
        far, outer = (0, 2) if core else (4, 0)
        pairs = range(5, 9) if core else range(-5, -1)
        pool_s[:, far : far + 2] = pool_far[...]
        encode(field, pick, w_first, pairs, None, 0, pool_s, outer)
        lhs = jnp.concatenate(
            [
                fine_s[dy : dy + 4, dx : dx + 3].reshape(384, 256)
                for dx in range(3)
                for dy in range(3)
            ],
            axis=1,
        )
        near, rest = (0, 5) if core else (3, 0)
        skip[:, rest : rest + 3] = dot(lhs, w_fine_skip[...]).reshape(4, 3, 32, 256)
        skip[:, near : near + 5] = skip_near[...]
        rows, pooled = middle_rows(pool_s, w_down, 4 if core else -4, 4)
        for at in range(2):
            put_three(pool_mid, at, pooled[at])
            for py in range(2):
                put_shifts(mid, at, py, rows[py][at if core else at + 2])

    for_each_core(work)


def net_kernel(
    from_twin, skip_s, mid_near, mid_far, mid_out, pool_mid_in, pool_mid_out,
    w_coarse, w_mid_skip, w_mid_up, w_fine_up, w_head,
    out,
    mid_s, pool_mid_s, coarse_s, up_s, last_s,
):
    mask = y_mask()

    def gather(core):
        first, last = (6, 0) if core else (0, 6)
        near, far = (2, 4) if core else (4, 2)
        mid_s[:, first : first + 2] = mid_out[...]
        mid_s[:, near : near + 2], mid_s[:, far : far + 2] = mid_near[...], mid_far[...]
        cell = 4 if core else 0
        pool_mid_s[:, cell : cell + 2], pool_mid_s[:, 2:4] = pool_mid_out[...], pool_mid_in[...]
        for at in range(2):
            for py in range(2):
                row = (at * 2 + py) * J
                put_shifts(mid_s, last + at, py, from_twin[row : row + J].astype(F32))
            lanes = slice(at * 128, at * 128 + 128)
            put_three(pool_mid_s, 4 - cell + at, from_twin[4 * J :, lanes].astype(F32))

    for_each_core(gather)

    lhs = jnp.concatenate(
        [
            pool_mid_s[dy, dx : dx + 4].reshape(4 * J, 128)
            for dx in range(3)
            for dy in range(3)
        ],
        axis=1,
    )
    value = silu_half(dot(lhs, w_coarse[...])).reshape(4, J, 256)
    for at in range(4):
        put_three(coarse_s, at, value[at] * (mask * row_flag(at - 1)))

    lhs = jnp.concatenate(
        [
            mid_s[dy : dy + 2, dx : dx + 6].reshape(12 * J, 256)
            for dx in range(3)
            for dy in range(3)
        ],
        axis=1,
    )
    skip = dot(lhs, w_mid_skip[...]).reshape(2, 6, J, 256)
    for py in range(2):
        lhs = jnp.concatenate(
            [
                coarse_s[py + ty, tx : tx + 3].reshape(3 * J, 256)
                for tx in range(2)
                for ty in range(2)
            ],
            axis=1,
        )
        for px in range(2):
            up = dot(lhs, w_mid_up[px * 2 + py]).reshape(3, J, 256)
            for k in range(3):
                at = 2 * k if px else 2 * k + 1
                value = silu_half(skip[py, at] + up[k])
                masked = value * (mask * row_flag((at - 1) // 2))
                up_s[py + 1, at] = masked[:32].astype(BF)
                shift = 1 if py else J - 1
                up_s[0 if py else 3, at] = pltpu.roll(masked, shift, 0)[:32].astype(BF)

    @pl.loop(0, 4)
    def _(parity):
        px, py = parity // 2, parity % 2
        lhs = jnp.concatenate(
            [
                up_s[pl.ds(py + ty, 2), pl.ds(px + tx, 4)].reshape(256, 256)
                for tx in range(2)
                for ty in range(2)
            ],
            axis=1,
        )
        up = dot(lhs, w_fine_up[parity]).reshape(2, 4, 32, 256)
        for half in range(2):
            group = 2 * half + py
            for k in range(4):
                value = silu_half(skip_s[group, 2 * k + px] + up[half, k])
                row = pl.multiple_of(group * 32, 32)
                last_s[2 * k + px, pl.ds(row, 32), :] = value.astype(BF)

    heads = jnp.concatenate([dot_nt(w_head[...], last_s[x]) for x in range(8)], axis=0)
    high = heads.astype(BF)
    rest = heads - high.astype(F32)
    low = rest.astype(BF)
    lowest = (rest - low.astype(F32)).astype(BF)
    row, col = iota((128, 128), 0), iota((128, 128), 1)
    order = (col == 4 * (row % 32) + row // 32).astype(BF)
    noise = dot(
        jnp.concatenate([high, low, lowest], axis=1),
        jnp.concatenate([order, order, order], axis=0),
    ).reshape(8, 16, 128)
    for x in range(8):
        out[:, x, :] = noise[x]


def body(
    noisy_field, first_weight, down_weight, coarse_weight, middle_weight, fine_weight, head_weight
):
    def shape(*dims, kind=BF):
        return jax.ShapeDtypeStruct(dims, kind)

    def cost(flops, moved):
        return pl.CostEstimate(flops=flops, bytes_accessed=moved, transcendentals=0)

    def small(limit):
        return pltpu.CompilerParams(vmem_limit_bytes=limit * 2**20)

    w_first, w_down, w_coarse, w_head, middle, fine, pick = pl.pallas_call(
        encoder_weights_kernel,
        out_shape=(
            shape(2, 192, 256),
            shape(1152, 256),
            shape(1152, 256),
            shape(16, 256),
            shape(27, 32, 96),
            shape(27, 16, 48),
            shape(4 * J, 256),
        ),
        in_specs=[ANY] * 6,
        out_specs=(VMEM,) * 7,
        scratch_shapes=[
            pltpu.VMEM((9, 3, 16), BF),
            pltpu.VMEM((27, 16, 32), BF),
            pltpu.VMEM((27, 32, 64), BF),
            pltpu.VMEM((1, 16), BF),
            pltpu.SemaphoreType.DMA((6,)),
        ],
        compiler_params=small(16),
        cost_estimate=cost(10**9, 3 * 10**6),
    )(
        *(
            pltpu.with_memory_space_constraint(weight, pltpu.HBM)
            for weight in (
                first_weight.transpose(1, 2, 3, 4, 0).reshape(9, 3, 16),
                down_weight.transpose(2, 3, 4, 1, 0).reshape(27, 16, 32),
                coarse_weight.transpose(2, 3, 4, 1, 0).reshape(27, 32, 64),
                middle_weight.transpose(2, 3, 4, 0, 1).reshape(27, 32, 96),
                fine_weight.transpose(2, 3, 4, 0, 1).reshape(27, 16, 48),
                head_weight.reshape(1, 16),
            )
        )
    )

    w_mid_skip = pl.pallas_call(
        mid_skip_weights_kernel,
        out_shape=shape(2304, 256),
        in_specs=[VMEM],
        out_specs=VMEM,
        compiler_params=small(16),
        cost_estimate=cost(10**9, 2 * 10**6),
    )(middle)

    def pairs(axis):
        count = lax.axis_size(axis)
        inner = [(i, i ^ 1) for i in range(count)]
        return inner, [(i, ((i + 1) ^ 1) - 1) for i in range(1, count - 1)]

    swap_in, swap_out = pairs("gy")
    y_outer = lax.ppermute(noisy_field, "gy", swap_out)
    y_inner = lax.ppermute(noisy_field, "gy", swap_in)
    own = pl.pallas_call(
        join_kernel,
        out_shape=shape(128, 256),
        in_specs=[VMEM] * 3 + [ANY] * 2,
        out_specs=VMEM,
        compiler_params=small(4),
        cost_estimate=cost(10**7, 2 * 10**5),
    )(noisy_field, y_outer, y_inner, w_head, w_mid_skip)

    in_chip, between = pairs("gx")
    twin = lax.ppermute(own, "gx", in_chip)
    w_mid_up = pl.pallas_call(
        mid_up_weights_kernel,
        out_shape=shape(4, 1024, 256),
        in_specs=[VMEM, ANY],
        out_specs=VMEM,
        scratch_shapes=[pltpu.VMEM((27, 64, 256), F32)],
        compiler_params=small(24),
        cost_estimate=cost(10**9, 4 * 10**6),
    )(middle, own)
    edge = pl.pallas_call(
        chip_edge_kernel,
        out_shape=shape(176, 256),
        in_specs=[VMEM] * 2 + [ANY],
        out_specs=VMEM,
        compiler_params=small(4),
        cost_estimate=cost(10**5, 3 * 10**5),
    )(own, twin, w_mid_up)
    chip_edge = lax.ppermute(edge, "gx", between)

    fine_near, pool_near, mid_near, pool_mid_near, for_twin_near = pl.pallas_call(
        encode_near_kernel,
        out_shape=(
            shape(6, 7, 32, 256),
            shape(4, 4, J, 128),
            shape(4, 2, J, 256),
            shape(J, 128),
            shape(4 * J, 256),
        ),
        in_specs=[VMEM] * 5 + [ANY],
        out_specs=(VMEM,) * 5,
        compiler_params=small(16),
        cost_estimate=cost(10**9, 3 * 10**6),
    )(own, twin, pick, w_first, w_down, edge)
    w_fine_skip = pl.pallas_call(
        fine_weights_kernel,
        out_shape=shape(2304, 256),
        in_specs=[VMEM, ANY],
        out_specs=VMEM,
        compiler_params=small(16),
        cost_estimate=cost(10**9, 2 * 10**6),
    )(fine, edge)
    skip_near, w_fine_up = pl.pallas_call(
        skip_near_kernel,
        out_shape=(shape(4, 5, 32, 256, kind=F32), shape(4, 1024, 256)),
        in_specs=[VMEM] * 3,
        out_specs=(VMEM,) * 2,
        scratch_shapes=[pltpu.VMEM((27, 32, 256), F32)],
        compiler_params=small(16),
        cost_estimate=cost(10**9, 4 * 10**6),
    )(fine_near, fine, w_fine_skip)

    fine_far, pool_far, mid_far, pool_mid_in, for_twin = pl.pallas_call(
        encode_inner_kernel,
        out_shape=(
            shape(6, 3, 32, 256),
            shape(4, 2, J, 128),
            shape(4, 2, J, 256),
            shape(3, 2, J, 128),
            shape(5 * J, 256),
        ),
        in_specs=[VMEM] * 8 + [ANY],
        out_specs=(VMEM,) * 5,
        scratch_shapes=[pltpu.VMEM((4, 4, J, 128), BF)],
        compiler_params=small(16),
        cost_estimate=cost(10**9, 3 * 10**6),
    )(
        own, chip_edge, pick, w_first, w_down, pool_near, pool_mid_near, for_twin_near,
        skip_near,
    )
    from_twin = lax.ppermute(for_twin, "gx", in_chip)
    mid_out, pool_mid_out, skip = pl.pallas_call(
        encode_outer_kernel,
        out_shape=(
            shape(4, 2, J, 256),
            shape(3, 2, J, 128),
            shape(4, 8, 32, 256, kind=F32),
        ),
        in_specs=[VMEM] * 9 + [ANY],
        out_specs=(VMEM,) * 3,
        scratch_shapes=[pltpu.VMEM((4, 6, J, 128), BF), pltpu.VMEM((6, 5, 32, 256), BF)],
        compiler_params=small(16),
        cost_estimate=cost(2 * 10**9, 3 * 10**6),
    )(
        chip_edge, pick, w_first, w_down, pool_far, fine_near, fine_far, skip_near, w_fine_skip,
        for_twin,
    )

    return pl.pallas_call(
        net_kernel,
        out_shape=shape(16, 8, 128, kind=F32),
        in_specs=[VMEM] * 12,
        out_specs=VMEM,
        scratch_shapes=[
            pltpu.VMEM((4, 8, J, 256), BF),
            pltpu.VMEM((3, 6, J, 128), BF),
            pltpu.VMEM((3, 4, J, 256), BF),
            pltpu.VMEM((4, 6, 32, 256), BF),
            pltpu.VMEM((8, 128, 256), BF),
        ],
        compiler_params=small(32),
        cost_estimate=pl.CostEstimate(
            flops=6 * 10**9, bytes_accessed=9 * 10**6, transcendentals=10**6
        ),
    )(
        from_twin, skip, mid_near, mid_far, mid_out, pool_mid_in, pool_mid_out,
        w_coarse, w_mid_skip, w_mid_up, w_fine_up, w_head,
    )


def solution(mesh):
    placed = (P(None, "gx", "gy"), P(), P(), P(), P(), P(), P())
    return jax.shard_map(
        body, mesh=mesh, in_specs=placed, out_specs=P(None, "gx", "gy"), check_vma=False
    )
```

```python
import jax
import jax.numpy as jnp
from jax import lax
from jax.experimental import pallas as pl
from jax.experimental.pallas import tpu as pltpu
from jax.sharding import PartitionSpec as P

BF = jnp.bfloat16
F32 = jnp.float32
J = 40
VMEM = pl.BlockSpec(memory_space=pltpu.VMEM)
ANY = pl.BlockSpec(memory_space=pl.ANY)


def dot(a, b):
    return jnp.dot(a, b, preferred_element_type=F32)


def dot_nt(a, b):
    return lax.dot_general(a, b, (((1,), (1,)), ((), ())), preferred_element_type=F32)


def dot_tn(a, b):
    return lax.dot_general(a, b, (((0,), (0,)), ((), ())), preferred_element_type=F32)


def iota(shape, axis):
    return lax.broadcasted_iota(jnp.int32, shape, axis)


def natural(channels):
    return lambda lane: lane // channels


def halves(channels):
    return lambda lane: 2 * ((lane // channels) % (128 // channels)) + lane // 128


def repeat_matrix(channels):
    return (iota((channels, 256), 1) % channels == iota((channels, 256), 0)).astype(BF)


def ones_where(cond):
    return jnp.where(cond, 1.0, 0.0).astype(BF)


def tiles(depth_of):
    return [
        (slice(at, at + 128), {depth_of(lane) for lane in range(at, at + 128)})
        for at in (0, 128)
    ]


def place_block(out, index, row, rows, terms, places, held, lanes):
    total = None
    for depths, value in terms:
        depths = [depth for depth in depths if depth in held]
        if depths:
            mask = places[:, lanes] == depths[0]
            for depth in depths[1:]:
                mask = mask | (places[:, lanes] == depth)
            part = ones_where(mask) * value[:, lanes]
            total = part if total is None else total + part
    if total is None:
        total = jnp.zeros((rows, 128), BF)
    out[(*index, pl.ds(row, rows), lanes)] = total


def cell_of(j):
    return jnp.where(j < 36, j, j - J)


def cell_inside(axis, held, cell):
    at = lax.axis_index(axis) * held + cell
    return (at >= 0) & (at < lax.axis_size(axis) * held)


SETS = (((0,), (1, 2)), ((0, 1), (2,)))


def banded(out, taps, channels, row_depths, depth_of):
    size = channels * len(row_depths)
    places = depth_of(iota((channels, 256), 1))
    for lanes, held in tiles(depth_of):
        for at, depth in enumerate(row_depths):
            for xy in range(9):
                terms = [((depth + 1 - dz,), taps[dz][xy]) for dz in range(3)]
                row = xy * size + at * channels
                place_block(out, (), row, channels, terms, places, held, lanes)


def folded(out, get, channels, depths, depth_of):
    size = channels * depths
    places = depth_of(iota((channels, 256), 1))
    even = places % 2 == 0
    for px in range(2):
        for tx in range(2):
            by_y = [
                [sum(get(dz, dx, dy) for dx in SETS[px][tx]) for dy in range(3)]
                for dz in range(3)
            ]
            for py in range(2):
                for ty in range(2):
                    w0, w1, w2 = [
                        sum(by_y[dz][dy] for dy in SETS[py][ty]) for dz in range(3)
                    ]
                    inner = jnp.where(even, w1 + w2, w0 + w1).astype(BF)
                    outer = jnp.where(even, w0, w2).astype(BF)
                    for lanes, held in tiles(depth_of):
                        for depth in range(depths):
                            terms = [
                                ((2 * depth, 2 * depth + 1), inner),
                                ((2 * depth + 2, 2 * depth - 1), outer),
                            ]
                            row = (tx * 2 + ty) * size + depth * channels
                            index = (px * 2 + py,)
                            place_block(out, index, row, channels, terms, places, held, lanes)


def encoder_weights_kernel(
    raw_first, raw_down, raw_coarse, raw_middle, raw_fine, raw_head,
    w_first, w_down, w_coarse, w_head, middle, fine, pick,
    first, down, coarse, head, sems,
):
    copies = [
        pltpu.make_async_copy(source, target, sems.at[at])
        for at, (source, target) in enumerate(
            (
                (raw_first, first),
                (raw_down, down),
                (raw_coarse, coarse),
                (raw_head, head),
                (raw_middle, middle),
                (raw_fine, fine),
            )
        )
    ]
    for copy in copies:
        copy.start()
    r16, r32, r64 = repeat_matrix(16), repeat_matrix(32), repeat_matrix(64)
    row = iota((4 * J, 256), 0)
    cell = cell_of(row % J)
    inside = cell_inside("gy", 32, cell)
    pick[...] = ((iota((4 * J, 256), 1) == (4 * cell + row // J + 256) % 256) & inside).astype(BF)
    copies[0].wait()

    w_first[...] = jnp.zeros_like(w_first)
    for dx in range(3):
        rows = [dot(first[dz * 3 + dx], r16) * 0.5 for dz in range(3)]
        place = halves(16)(iota((16, 256), 1))
        depth = iota((16, 256), 0)
        for dy in range(3):
            block = jnp.zeros((16, 256), F32)
            for dz in range(3):
                block = block + jnp.where(place == depth + 1 - dz, rows[dz][dy : dy + 1], 0.0)
            block = block.astype(BF)
            for even in range(2):
                w_first[even, pl.ds(dy * 64 + (even + dx) * 16, 16), :] = block

    copies[1].wait()
    flat = down[...].reshape(27 * 16, 32)
    all_taps = (dot(flat, r32) * (1 / 16)).astype(BF)
    taps = [[all_taps[(dz * 9 + xy) * 16 : (dz * 9 + xy + 1) * 16] for xy in range(9)] for dz in range(3)]
    banded(w_down, taps, 16, list(range(8)), halves(32))

    copies[2].wait()
    flat = coarse[...].reshape(27 * 32, 64)
    all_taps = (dot(flat, r64) * (1 / 16)).astype(BF)
    taps = [[all_taps[(dz * 9 + xy) * 32 : (dz * 9 + xy + 1) * 32] for xy in range(9)] for dz in range(3)]
    banded(w_coarse, taps, 32, list(range(4)), natural(64))

    copies[3].wait()
    row = dot(jnp.broadcast_to(head[...], (16, 16)), r16)
    w_head[...] = jnp.where(iota((16, 256), 1) // 16 == iota((16, 256), 0), row, 0.0).astype(BF)
    for copy in copies[4:]:
        copy.wait()


def mid_skip_weights_kernel(middle, w_mid_skip):
    r32 = repeat_matrix(32)
    tiled = [(dot_tn(middle[tap], r32)[64:] * 0.5).astype(BF) for tap in range(27)]
    taps = [tiled[dz * 9 : dz * 9 + 9] for dz in range(3)]
    banded(w_mid_skip, taps, 32, [0, 2, 4, 6, 1, 3, 5, 7], natural(32))


def mid_up_weights_kernel(middle, after, w_mid_up, tiled):
    r32 = repeat_matrix(32)
    for tap in range(27):
        tiled[tap] = dot_tn(middle[tap], r32)[:64] * 0.5
    folded(w_mid_up, lambda dz, dx, dy: tiled[dz * 9 + dx * 3 + dy], 64, 4, natural(32))


def fine_skip_weights(fine, w_fine_skip):
    r16 = repeat_matrix(16)
    tiled = [(dot_tn(fine[tap], r16)[32:] * 0.5).astype(BF) for tap in range(27)]
    taps = [tiled[dz * 9 : dz * 9 + 9] for dz in range(3)]
    banded(w_fine_skip, taps, 16, list(range(0, 16, 2)) + list(range(1, 16, 2)), natural(16))


def join_kernel(own, outer, inner, after, also_after, out):
    from_inner = (iota((128, 128), 1) < 64) == (lax.axis_index("gy") % 2 == 0)
    mine = own[...].astype(F32).reshape(128, 128)
    rim = jnp.where(
        from_inner,
        inner[...].astype(F32).reshape(128, 128),
        outer[...].astype(F32).reshape(128, 128),
    )
    both = jnp.concatenate([mine, rim], axis=1).astype(BF)
    row, col = iota((128, 128), 0), iota((128, 128), 1)
    swap = (col == (row % 16) * 8 + row // 16).astype(BF)
    out[...] = dot(swap, both).astype(BF)


def chip_edge_kernel(own, twin, after, out):
    odd = lax.axis_index("gx") % 2 == 1
    for_high = jnp.concatenate([twin[80:], own[...]], axis=0)
    for_low = jnp.concatenate([own[...], twin[:48]], axis=0)
    out[...] = jnp.where(odd, for_high, for_low)


def silu_half(h):
    return h + h * jnp.tanh(h)


def row_flag(cell):
    return jnp.where(cell_inside("gx", 2, cell), 1.0, 0.0)


def put_shifts(out, at, group, value):
    out[group + 1, at] = value.astype(BF)
    out[0 if group else 3, at] = pltpu.roll(value, 1 if group else J - 1, 0).astype(BF)


def put_three(out, at, value):
    out[0, at] = pltpu.roll(value, 1, 0).astype(BF)
    out[1, at] = value.astype(BF)
    out[2, at] = pltpu.roll(value, J - 1, 0).astype(BF)


def encode(field, pick, w_first, pairs, fine, first_x, pooled, pooled_at):
    wide = field.astype(F32)
    shifted = [pltpu.roll(wide, 1, 1).astype(BF), field, pltpu.roll(wide, 255, 1).astype(BF)]
    for at, m in enumerate(pairs):
        window = jnp.concatenate([part[at * 32 : at * 32 + 64] for part in shifted], axis=0)
        lhs = (dot_nt(pick[...], window) * row_flag(m // 2)).astype(BF)
        sums = [jnp.zeros((J, 128), F32) for _ in range(2)]
        for even in range(2):
            value = silu_half(dot(lhs, w_first[even])).reshape(4, J, 256)
            for part in range(2):
                both = value[2 * part] + value[2 * part + 1]
                sums[part] = sums[part] + both[:, :128] + both[:, 128:]
            x = 2 * m + even
            if fine is not None and -1 <= x <= 8:
                for group in range(4):
                    fine[group + 1, x - first_x] = value[group, :32].astype(BF)
                fine[0, x - first_x] = pltpu.roll(value[3], 1, 0)[:32].astype(BF)
                fine[5, x - first_x] = pltpu.roll(value[0], J - 1, 0)[:32].astype(BF)
        for part in range(2):
            put_shifts(pooled, pooled_at + at, part, sums[part])


def for_each_core(work):
    odd = lax.axis_index("gx") % 2

    @pl.when(odd == 0)
    def _():
        work(0)

    @pl.when(odd == 1)
    def _():
        work(1)


def middle_rows(pool_s, w_down, first, count):
    lhs = jnp.concatenate(
        [
            pool_s[dy : dy + 2, dx : dx + count].reshape(2 * count * J, 128)
            for dx in range(3)
            for dy in range(3)
        ],
        axis=1,
    )
    value = silu_half(dot(lhs, w_down[...])).reshape(2, count, J, 256)
    mask = y_mask()
    rows = [
        [value[py, at] * (mask * row_flag((first + at) // 2)) for at in range(count)]
        for py in range(2)
    ]
    pooled = []
    for at in range(0, count, 2):
        cells = rows[0][at] + rows[0][at + 1] + rows[1][at] + rows[1][at + 1]
        pooled.append(cells[:, :128] + cells[:, 128:])
    return rows, pooled


def y_mask():
    return jnp.where(cell_inside("gy", 32, cell_of(iota((J, 256), 0))), 1.0, 0.0)


def encode_near_kernel(
    own, twin, pick, w_first, w_down, fine_taps, after,
    fine, pooled, mid, pool_mid, for_twin, w_fine_skip,
):
    def work(core):
        fine_skip_weights(fine_taps, w_fine_skip)
        if core:
            field = jnp.concatenate([twin[80:], own[:112]], axis=0)
        else:
            field = jnp.concatenate([own[16:], twin[:48]], axis=0)
        pairs = range(-1, 3) if core else range(1, 5)
        encode(field, pick, w_first, pairs, fine, -1 if core else 2, pooled, 0)
        rows, cells = middle_rows(pooled, w_down, 0 if core else 2, 2)
        for at in range(2):
            for py in range(2):
                put_shifts(mid, at, py, rows[py][at])
                for_twin[pl.ds((at * 2 + py) * J, J), :] = rows[py][at].astype(BF)
        pool_mid[...] = cells[0].astype(BF)

    for_each_core(work)


def skip_near_kernel(fine_near, fine, w_fine_skip, out, w_fine_up, tiled):
    lhs = jnp.concatenate(
        [
            fine_near[dy : dy + 4, dx : dx + 5].reshape(640, 256)
            for dx in range(3)
            for dy in range(3)
        ],
        axis=1,
    )
    out[...] = dot(lhs, w_fine_skip[...]).reshape(4, 5, 32, 256)
    r16 = repeat_matrix(16)
    for tap in range(27):
        tiled[tap] = dot_tn(fine[tap], r16)[:32] * 0.5
    folded(w_fine_up, lambda dz, dx, dy: tiled[dz * 9 + dx * 3 + dy], 32, 8, natural(16))


def encode_inner_kernel(
    own, edge, pick, w_first, w_down, pool_near, pool_mid_near, for_twin_near, after,
    fine, pool_far, mid, pool_mid, for_twin, pool_s,
):
    def work(core):
        if core:
            field = jnp.concatenate([own[80:], edge[:48]], axis=0)
            pool_s[:, 0:2] = pool_near[:, 2:4]
        else:
            field = jnp.concatenate([edge[128:], own[:48]], axis=0)
            pool_s[:, 2:4] = pool_near[:, 0:2]
        pairs, far = ((3, 4), 2) if core else ((-1, 0), 0)
        encode(field, pick, w_first, pairs, fine, 6 if core else -1, pool_s, far)
        pool_far[...] = pool_s[:, far : far + 2]
        rows, pooled = middle_rows(pool_s, w_down, 2 if core else 0, 2)
        for at in range(2):
            for py in range(2):
                put_shifts(mid, at, py, rows[py][at])
        near = pool_mid_near[...].astype(F32)
        cells = (near, pooled[0]) if core else (pooled[0], near)
        for at in range(2):
            put_three(pool_mid, at, cells[at])
        for_twin[pl.ds(0, 4 * J), :] = for_twin_near[...]
        for_twin[pl.ds(4 * J, J), :] = jnp.concatenate(cells, axis=1).astype(BF)

    for_each_core(work)


def encode_outer_kernel(
    edge, pick, w_first, w_down, pool_far, fine_near, fine_far, skip_near, w_fine_skip, after,
    mid, pool_mid, skip, pool_s, fine_s,
):
    def work(core):
        if core:
            fine_s[:, 0:2], fine_s[:, 2:5] = fine_near[:, 5:7], fine_far[...]
        else:
            fine_s[:, 0:3], fine_s[:, 3:5] = fine_far[...], fine_near[:, 0:2]
        field = edge[16:] if core else edge[:160]
        far, outer = (0, 2) if core else (4, 0)
        pairs = range(5, 9) if core else range(-5, -1)
        pool_s[:, far : far + 2] = pool_far[...]
        encode(field, pick, w_first, pairs, None, 0, pool_s, outer)
        lhs = jnp.concatenate(
            [
                fine_s[dy : dy + 4, dx : dx + 3].reshape(384, 256)
                for dx in range(3)
                for dy in range(3)
            ],
            axis=1,
        )
        near, rest = (0, 5) if core else (3, 0)
        skip[:, rest : rest + 3] = dot(lhs, w_fine_skip[...]).reshape(4, 3, 32, 256)
        skip[:, near : near + 5] = skip_near[...]
        rows, pooled = middle_rows(pool_s, w_down, 4 if core else -4, 4)
        for at in range(2):
            put_three(pool_mid, at, pooled[at])
            for py in range(2):
                put_shifts(mid, at, py, rows[py][at if core else at + 2])

    for_each_core(work)


def net_kernel(
    from_twin, skip_s, mid_near, mid_far, mid_out, pool_mid_in, pool_mid_out,
    w_coarse, w_mid_skip, w_mid_up, w_fine_up, w_head,
    out,
    mid_s, pool_mid_s, coarse_s, up_s, last_s,
):
    mask = y_mask()

    def gather(core):
        first, last = (6, 0) if core else (0, 6)
        near, far = (2, 4) if core else (4, 2)
        mid_s[:, first : first + 2] = mid_out[...]
        mid_s[:, near : near + 2], mid_s[:, far : far + 2] = mid_near[...], mid_far[...]
        cell = 4 if core else 0
        pool_mid_s[:, cell : cell + 2], pool_mid_s[:, 2:4] = pool_mid_out[...], pool_mid_in[...]
        for at in range(2):
            for py in range(2):
                row = (at * 2 + py) * J
                put_shifts(mid_s, last + at, py, from_twin[row : row + J].astype(F32))
            lanes = slice(at * 128, at * 128 + 128)
            put_three(pool_mid_s, 4 - cell + at, from_twin[4 * J :, lanes].astype(F32))

    for_each_core(gather)

    lhs = jnp.concatenate(
        [
            pool_mid_s[dy, dx : dx + 4].reshape(4 * J, 128)
            for dx in range(3)
            for dy in range(3)
        ],
        axis=1,
    )
    value = silu_half(dot(lhs, w_coarse[...])).reshape(4, J, 256)
    for at in range(4):
        put_three(coarse_s, at, value[at] * (mask * row_flag(at - 1)))

    lhs = jnp.concatenate(
        [
            mid_s[dy : dy + 2, dx : dx + 6].reshape(12 * J, 256)
            for dx in range(3)
            for dy in range(3)
        ],
        axis=1,
    )
    skip = dot(lhs, w_mid_skip[...]).reshape(2, 6, J, 256)
    for py in range(2):
        lhs = jnp.concatenate(
            [
                coarse_s[py + ty, tx : tx + 3].reshape(3 * J, 256)
                for tx in range(2)
                for ty in range(2)
            ],
            axis=1,
        )
        for px in range(2):
            up = dot(lhs, w_mid_up[px * 2 + py]).reshape(3, J, 256)
            for k in range(3):
                at = 2 * k if px else 2 * k + 1
                value = silu_half(skip[py, at] + up[k])
                masked = value * (mask * row_flag((at - 1) // 2))
                up_s[py + 1, at] = masked[:32].astype(BF)
                shift = 1 if py else J - 1
                up_s[0 if py else 3, at] = pltpu.roll(masked, shift, 0)[:32].astype(BF)

    @pl.loop(0, 2)
    def _(py):
        for px in range(2):
            lhs = jnp.concatenate(
                [
                    up_s[pl.ds(py + ty, 2), px + tx : px + tx + 4].reshape(256, 256)
                    for tx in range(2)
                    for ty in range(2)
                ],
                axis=1,
            )
            up = dot(lhs, w_fine_up[px * 2 + py]).reshape(2, 4, 32, 256)
            for half in range(2):
                group = 2 * half + py
                for k in range(4):
                    value = silu_half(skip_s[group, 2 * k + px] + up[half, k])
                    row = pl.multiple_of(group * 32, 32)
                    last_s[2 * k + px, pl.ds(row, 32), :] = value.astype(BF)

    heads = jnp.concatenate([dot_nt(w_head[...], last_s[x]) for x in range(8)], axis=0)
    high = heads.astype(BF)
    rest = heads - high.astype(F32)
    low = rest.astype(BF)
    lowest = (rest - low.astype(F32)).astype(BF)
    row, col = iota((128, 128), 0), iota((128, 128), 1)
    order = (col == 4 * (row % 32) + row // 32).astype(BF)
    noise = dot(
        jnp.concatenate([high, low, lowest], axis=1),
        jnp.concatenate([order, order, order], axis=0),
    ).reshape(8, 16, 128)
    for x in range(8):
        out[:, x, :] = noise[x]


def body(
    noisy_field, first_weight, down_weight, coarse_weight, middle_weight, fine_weight, head_weight
):
    def shape(*dims, kind=BF):
        return jax.ShapeDtypeStruct(dims, kind)

    def cost(flops, moved):
        return pl.CostEstimate(flops=flops, bytes_accessed=moved, transcendentals=0)

    def small(limit):
        return pltpu.CompilerParams(vmem_limit_bytes=limit * 2**20)

    w_first, w_down, w_coarse, w_head, middle, fine, pick = pl.pallas_call(
        encoder_weights_kernel,
        out_shape=(
            shape(2, 192, 256),
            shape(1152, 256),
            shape(1152, 256),
            shape(16, 256),
            shape(27, 32, 96),
            shape(27, 16, 48),
            shape(4 * J, 256),
        ),
        in_specs=[ANY] * 6,
        out_specs=(VMEM,) * 7,
        scratch_shapes=[
            pltpu.VMEM((9, 3, 16), BF),
            pltpu.VMEM((27, 16, 32), BF),
            pltpu.VMEM((27, 32, 64), BF),
            pltpu.VMEM((1, 16), BF),
            pltpu.SemaphoreType.DMA((6,)),
        ],
        compiler_params=small(16),
        cost_estimate=cost(10**9, 3 * 10**6),
    )(
        *(
            pltpu.with_memory_space_constraint(weight, pltpu.HBM)
            for weight in (
                first_weight.transpose(1, 2, 3, 4, 0).reshape(9, 3, 16),
                down_weight.transpose(2, 3, 4, 1, 0).reshape(27, 16, 32),
                coarse_weight.transpose(2, 3, 4, 1, 0).reshape(27, 32, 64),
                middle_weight.transpose(2, 3, 4, 0, 1).reshape(27, 32, 96),
                fine_weight.transpose(2, 3, 4, 0, 1).reshape(27, 16, 48),
                head_weight.reshape(1, 16),
            )
        )
    )

    w_mid_skip = pl.pallas_call(
        mid_skip_weights_kernel,
        out_shape=shape(2304, 256),
        in_specs=[VMEM],
        out_specs=VMEM,
        compiler_params=small(16),
        cost_estimate=cost(10**9, 2 * 10**6),
    )(middle)

    def pairs(axis):
        count = lax.axis_size(axis)
        inner = [(i, i ^ 1) for i in range(count)]
        return inner, [(i, ((i + 1) ^ 1) - 1) for i in range(1, count - 1)]

    swap_in, swap_out = pairs("gy")
    y_outer = lax.ppermute(noisy_field, "gy", swap_out)
    y_inner = lax.ppermute(noisy_field, "gy", swap_in)
    own = pl.pallas_call(
        join_kernel,
        out_shape=shape(128, 256),
        in_specs=[VMEM] * 3 + [ANY] * 2,
        out_specs=VMEM,
        compiler_params=small(4),
        cost_estimate=cost(10**7, 2 * 10**5),
    )(noisy_field, y_outer, y_inner, w_head, w_mid_skip)

    in_chip, between = pairs("gx")
    twin = lax.ppermute(own, "gx", in_chip)
    w_mid_up = pl.pallas_call(
        mid_up_weights_kernel,
        out_shape=shape(4, 1024, 256),
        in_specs=[VMEM, ANY],
        out_specs=VMEM,
        scratch_shapes=[pltpu.VMEM((27, 64, 256), F32)],
        compiler_params=small(24),
        cost_estimate=cost(10**9, 4 * 10**6),
    )(middle, own)
    edge = pl.pallas_call(
        chip_edge_kernel,
        out_shape=shape(176, 256),
        in_specs=[VMEM] * 2 + [ANY],
        out_specs=VMEM,
        compiler_params=small(4),
        cost_estimate=cost(10**5, 3 * 10**5),
    )(own, twin, w_mid_up)
    chip_edge = lax.ppermute(edge, "gx", between)

    fine_near, pool_near, mid_near, pool_mid_near, for_twin_near, w_fine_skip = pl.pallas_call(
        encode_near_kernel,
        out_shape=(
            shape(6, 7, 32, 256),
            shape(4, 4, J, 128),
            shape(4, 2, J, 256),
            shape(J, 128),
            shape(4 * J, 256),
            shape(2304, 256),
        ),
        in_specs=[VMEM] * 6 + [ANY],
        out_specs=(VMEM,) * 6,
        compiler_params=small(16),
        cost_estimate=cost(10**9, 3 * 10**6),
    )(own, twin, pick, w_first, w_down, fine, edge)
    skip_near, w_fine_up = pl.pallas_call(
        skip_near_kernel,
        out_shape=(shape(4, 5, 32, 256, kind=F32), shape(4, 1024, 256)),
        in_specs=[VMEM] * 3,
        out_specs=(VMEM,) * 2,
        scratch_shapes=[pltpu.VMEM((27, 32, 256), F32)],
        compiler_params=small(16),
        cost_estimate=cost(10**9, 4 * 10**6),
    )(fine_near, fine, w_fine_skip)

    fine_far, pool_far, mid_far, pool_mid_in, for_twin = pl.pallas_call(
        encode_inner_kernel,
        out_shape=(
            shape(6, 3, 32, 256),
            shape(4, 2, J, 128),
            shape(4, 2, J, 256),
            shape(3, 2, J, 128),
            shape(5 * J, 256),
        ),
        in_specs=[VMEM] * 8 + [ANY],
        out_specs=(VMEM,) * 5,
        scratch_shapes=[pltpu.VMEM((4, 4, J, 128), BF)],
        compiler_params=small(16),
        cost_estimate=cost(10**9, 3 * 10**6),
    )(
        own, chip_edge, pick, w_first, w_down, pool_near, pool_mid_near, for_twin_near,
        skip_near,
    )
    from_twin = lax.ppermute(for_twin, "gx", in_chip)
    mid_out, pool_mid_out, skip = pl.pallas_call(
        encode_outer_kernel,
        out_shape=(
            shape(4, 2, J, 256),
            shape(3, 2, J, 128),
            shape(4, 8, 32, 256, kind=F32),
        ),
        in_specs=[VMEM] * 9 + [ANY],
        out_specs=(VMEM,) * 3,
        scratch_shapes=[pltpu.VMEM((4, 6, J, 128), BF), pltpu.VMEM((6, 5, 32, 256), BF)],
        compiler_params=small(16),
        cost_estimate=cost(2 * 10**9, 3 * 10**6),
    )(
        chip_edge, pick, w_first, w_down, pool_far, fine_near, fine_far, skip_near, w_fine_skip,
        for_twin,
    )

    return pl.pallas_call(
        net_kernel,
        out_shape=shape(16, 8, 128, kind=F32),
        in_specs=[VMEM] * 12,
        out_specs=VMEM,
        scratch_shapes=[
            pltpu.VMEM((4, 8, J, 256), BF),
            pltpu.VMEM((3, 6, J, 128), BF),
            pltpu.VMEM((3, 4, J, 256), BF),
            pltpu.VMEM((4, 6, 32, 256), BF),
            pltpu.VMEM((8, 128, 256), BF),
        ],
        compiler_params=small(32),
        cost_estimate=pl.CostEstimate(
            flops=6 * 10**9, bytes_accessed=9 * 10**6, transcendentals=10**6
        ),
    )(
        from_twin, skip, mid_near, mid_far, mid_out, pool_mid_in, pool_mid_out,
        w_coarse, w_mid_skip, w_mid_up, w_fine_up, w_head,
    )


def solution(mesh):
    placed = (P(None, "gx", "gy"), P(), P(), P(), P(), P(), P())
    return jax.shard_map(
        body, mesh=mesh, in_specs=placed, out_specs=P(None, "gx", "gy"), check_vma=False
    )
```

```python
import jax
import jax.numpy as jnp
from jax import lax
from jax.experimental import pallas as pl
from jax.experimental.pallas import tpu as pltpu
from jax.sharding import PartitionSpec as P

BF = jnp.bfloat16
F32 = jnp.float32
J = 40
VMEM = pl.BlockSpec(memory_space=pltpu.VMEM)
ANY = pl.BlockSpec(memory_space=pl.ANY)


def dot(a, b):
    return jnp.dot(a, b, preferred_element_type=F32)


def dot_nt(a, b):
    return lax.dot_general(a, b, (((1,), (1,)), ((), ())), preferred_element_type=F32)


def dot_tn(a, b):
    return lax.dot_general(a, b, (((0,), (0,)), ((), ())), preferred_element_type=F32)


def iota(shape, axis):
    return lax.broadcasted_iota(jnp.int32, shape, axis)


def natural(channels):
    return lambda lane: lane // channels


def halves(channels):
    return lambda lane: 2 * ((lane // channels) % (128 // channels)) + lane // 128


def repeat_matrix(channels):
    return (iota((channels, 256), 1) % channels == iota((channels, 256), 0)).astype(BF)


def ones_where(cond):
    return jnp.where(cond, 1.0, 0.0).astype(BF)


def tiles(depth_of):
    return [
        (slice(at, at + 128), {depth_of(lane) for lane in range(at, at + 128)})
        for at in (0, 128)
    ]


def place_block(out, index, row, rows, terms, places, held, lanes):
    total = None
    for depths, value in terms:
        depths = [depth for depth in depths if depth in held]
        if depths:
            mask = places[:, lanes] == depths[0]
            for depth in depths[1:]:
                mask = mask | (places[:, lanes] == depth)
            part = ones_where(mask) * value[:, lanes]
            total = part if total is None else total + part
    if total is None:
        total = jnp.zeros((rows, 128), BF)
    out[(*index, pl.ds(row, rows), lanes)] = total


def cell_of(j):
    return jnp.where(j < 36, j, j - J)


def cell_inside(axis, held, cell):
    at = lax.axis_index(axis) * held + cell
    return (at >= 0) & (at < lax.axis_size(axis) * held)


SETS = (((0,), (1, 2)), ((0, 1), (2,)))


def banded(out, taps, channels, row_depths, depth_of):
    size = channels * len(row_depths)
    places = depth_of(iota((channels, 256), 1))
    for lanes, held in tiles(depth_of):
        for at, depth in enumerate(row_depths):
            for xy in range(9):
                terms = [((depth + 1 - dz,), taps[dz][xy]) for dz in range(3)]
                row = xy * size + at * channels
                place_block(out, (), row, channels, terms, places, held, lanes)


def folded(out, get, channels, depths, depth_of):
    size = channels * depths
    places = depth_of(iota((channels, 256), 1))
    even = places % 2 == 0
    for px in range(2):
        for tx in range(2):
            by_y = [
                [sum(get(dz, dx, dy) for dx in SETS[px][tx]) for dy in range(3)]
                for dz in range(3)
            ]
            for py in range(2):
                for ty in range(2):
                    w0, w1, w2 = [
                        sum(by_y[dz][dy] for dy in SETS[py][ty]) for dz in range(3)
                    ]
                    inner = jnp.where(even, w1 + w2, w0 + w1).astype(BF)
                    outer = jnp.where(even, w0, w2).astype(BF)
                    for lanes, held in tiles(depth_of):
                        for depth in range(depths):
                            terms = [
                                ((2 * depth, 2 * depth + 1), inner),
                                ((2 * depth + 2, 2 * depth - 1), outer),
                            ]
                            row = (tx * 2 + ty) * size + depth * channels
                            index = (px * 2 + py,)
                            place_block(out, index, row, channels, terms, places, held, lanes)


def encoder_weights_kernel(
    raw_first, raw_down, raw_coarse, raw_middle, raw_fine, raw_head,
    w_first, w_down, w_coarse, w_head, middle, fine, pick,
    first, down, coarse, head, sems,
):
    copies = [
        pltpu.make_async_copy(source, target, sems.at[at])
        for at, (source, target) in enumerate(
            (
                (raw_first, first),
                (raw_down, down),
                (raw_coarse, coarse),
                (raw_head, head),
                (raw_middle, middle),
                (raw_fine, fine),
            )
        )
    ]
    for copy in copies:
        copy.start()
    r16, r32, r64 = repeat_matrix(16), repeat_matrix(32), repeat_matrix(64)
    row = iota((4 * J, 256), 0)
    cell = cell_of(row % J)
    inside = cell_inside("gy", 32, cell)
    pick[...] = ((iota((4 * J, 256), 1) == (4 * cell + row // J + 256) % 256) & inside).astype(BF)
    for copy in copies[:4]:
        copy.wait()

    w_first[...] = jnp.zeros_like(w_first)
    for dx in range(3):
        rows = [dot(first[dz * 3 + dx], r16) * 0.5 for dz in range(3)]
        place = halves(16)(iota((16, 256), 1))
        depth = iota((16, 256), 0)
        for dy in range(3):
            block = jnp.zeros((16, 256), F32)
            for dz in range(3):
                block = block + jnp.where(place == depth + 1 - dz, rows[dz][dy : dy + 1], 0.0)
            block = block.astype(BF)
            for even in range(2):
                w_first[even, pl.ds(dy * 64 + (even + dx) * 16, 16), :] = block

    flat = down[...].reshape(27 * 16, 32)
    all_taps = (dot(flat, r32) * (1 / 16)).astype(BF)
    taps = [[all_taps[(dz * 9 + xy) * 16 : (dz * 9 + xy + 1) * 16] for xy in range(9)] for dz in range(3)]
    banded(w_down, taps, 16, list(range(8)), halves(32))

    flat = coarse[...].reshape(27 * 32, 64)
    all_taps = (dot(flat, r64) * (1 / 16)).astype(BF)
    taps = [[all_taps[(dz * 9 + xy) * 32 : (dz * 9 + xy + 1) * 32] for xy in range(9)] for dz in range(3)]
    banded(w_coarse, taps, 32, list(range(4)), natural(64))

    row = dot(jnp.broadcast_to(head[...], (16, 16)), r16)
    w_head[...] = jnp.where(iota((16, 256), 1) // 16 == iota((16, 256), 0), row, 0.0).astype(BF)
    for copy in copies[4:]:
        copy.wait()


def mid_skip_weights_kernel(middle, w_mid_skip):
    r32 = repeat_matrix(32)
    tiled = [(dot_tn(middle[tap, :, 64:96], r32) * 0.5).astype(BF) for tap in range(27)]
    taps = [tiled[dz * 9 : dz * 9 + 9] for dz in range(3)]
    banded(w_mid_skip, taps, 32, [0, 2, 4, 6, 1, 3, 5, 7], natural(32))


def mid_up_weights_kernel(middle, after, w_mid_up, tiled):
    r32 = repeat_matrix(32)
    for tap in range(27):
        tiled[tap] = dot_tn(middle[tap, :, 0:64], r32) * 0.5
    folded(w_mid_up, lambda dz, dx, dy: tiled[dz * 9 + dx * 3 + dy], 64, 4, natural(32))


def fine_skip_weights(fine, w_fine_skip):
    r16 = repeat_matrix(16)
    tiled = [(dot_tn(fine[tap, :, 32:48], r16) * 0.5).astype(BF) for tap in range(27)]
    taps = [tiled[dz * 9 : dz * 9 + 9] for dz in range(3)]
    banded(w_fine_skip, taps, 16, list(range(0, 16, 2)) + list(range(1, 16, 2)), natural(16))


def join_kernel(own, outer, inner, after, also_after, out):
    from_inner = (iota((128, 128), 1) < 64) == (lax.axis_index("gy") % 2 == 0)
    mine = own[...].astype(F32).reshape(128, 128)
    rim = jnp.where(
        from_inner,
        inner[...].astype(F32).reshape(128, 128),
        outer[...].astype(F32).reshape(128, 128),
    )
    both = jnp.concatenate([mine, rim], axis=1).astype(BF)
    row, col = iota((128, 128), 0), iota((128, 128), 1)
    swap = (col == (row % 16) * 8 + row // 16).astype(BF)
    out[...] = dot(swap, both).astype(BF)


def chip_edge_kernel(own, twin, after, out):
    odd = lax.axis_index("gx") % 2 == 1
    for_high = jnp.concatenate([twin[80:], own[...]], axis=0)
    for_low = jnp.concatenate([own[...], twin[:48]], axis=0)
    out[...] = jnp.where(odd, for_high, for_low)


def silu_half(h):
    return h + h * jnp.tanh(h)


def row_flag(cell):
    return jnp.where(cell_inside("gx", 2, cell), 1.0, 0.0)


def put_shifts(out, at, group, value):
    out[group + 1, at] = value.astype(BF)
    out[0 if group else 3, at] = pltpu.roll(value, 1 if group else J - 1, 0).astype(BF)


def put_three(out, at, value):
    out[0, at] = pltpu.roll(value, 1, 0).astype(BF)
    out[1, at] = value.astype(BF)
    out[2, at] = pltpu.roll(value, J - 1, 0).astype(BF)


def encode(field, pick, w_first, pairs, fine, first_x, pooled, pooled_at):
    wide = field.astype(F32)
    shifted = [pltpu.roll(wide, 1, 1).astype(BF), field, pltpu.roll(wide, 255, 1).astype(BF)]
    for at, m in enumerate(pairs):
        window = jnp.concatenate([part[at * 32 : at * 32 + 64] for part in shifted], axis=0)
        lhs = (dot_nt(pick[...], window) * row_flag(m // 2)).astype(BF)
        sums = [jnp.zeros((J, 128), F32) for _ in range(2)]
        for even in range(2):
            value = silu_half(dot(lhs, w_first[even])).reshape(4, J, 256)
            for part in range(2):
                both = value[2 * part] + value[2 * part + 1]
                sums[part] = sums[part] + both[:, :128] + both[:, 128:]
            x = 2 * m + even
            if fine is not None and -1 <= x <= 8:
                for group in range(4):
                    fine[group + 1, x - first_x] = value[group, :32].astype(BF)
                fine[0, x - first_x] = pltpu.roll(value[3], 1, 0)[:32].astype(BF)
                fine[5, x - first_x] = pltpu.roll(value[0], J - 1, 0)[:32].astype(BF)
        for part in range(2):
            put_shifts(pooled, pooled_at + at, part, sums[part])


def for_each_core(work):
    odd = lax.axis_index("gx") % 2

    @pl.when(odd == 0)
    def _():
        work(0)

    @pl.when(odd == 1)
    def _():
        work(1)


def middle_rows(pool_s, w_down, first, count):
    lhs = jnp.concatenate(
        [
            pool_s[dy : dy + 2, dx : dx + count].reshape(2 * count * J, 128)
            for dx in range(3)
            for dy in range(3)
        ],
        axis=1,
    )
    value = silu_half(dot(lhs, w_down[...])).reshape(2, count, J, 256)
    mask = y_mask()
    rows = [
        [value[py, at] * (mask * row_flag((first + at) // 2)) for at in range(count)]
        for py in range(2)
    ]
    pooled = []
    for at in range(0, count, 2):
        cells = rows[0][at] + rows[0][at + 1] + rows[1][at] + rows[1][at + 1]
        pooled.append(cells[:, :128] + cells[:, 128:])
    return rows, pooled


def y_mask():
    return jnp.where(cell_inside("gy", 32, cell_of(iota((J, 256), 0))), 1.0, 0.0)


def encode_near_kernel(
    own, twin, pick, w_first, w_down, fine_taps, after,
    fine, pooled, mid, pool_mid, for_twin, w_fine_skip,
):
    def work(core):
        fine_skip_weights(fine_taps, w_fine_skip)
        if core:
            field = jnp.concatenate([twin[80:], own[:112]], axis=0)
        else:
            field = jnp.concatenate([own[16:], twin[:48]], axis=0)
        pairs = range(-1, 3) if core else range(1, 5)
        encode(field, pick, w_first, pairs, fine, -1 if core else 2, pooled, 0)
        rows, cells = middle_rows(pooled, w_down, 0 if core else 2, 2)
        for at in range(2):
            for py in range(2):
                put_shifts(mid, at, py, rows[py][at])
                for_twin[pl.ds((at * 2 + py) * J, J), :] = rows[py][at].astype(BF)
        pool_mid[...] = cells[0].astype(BF)

    for_each_core(work)


def skip_near_kernel(fine_near, fine, w_fine_skip, out, w_fine_up, tiled):
    lhs = jnp.concatenate(
        [
            fine_near[dy : dy + 4, dx : dx + 5].reshape(640, 256)
            for dx in range(3)
            for dy in range(3)
        ],
        axis=1,
    )
    out[...] = dot(lhs, w_fine_skip[...]).reshape(4, 5, 32, 256)
    r16 = repeat_matrix(16)
    for tap in range(27):
        tiled[tap] = dot_tn(fine[tap, :, 0:32], r16) * 0.5
    folded(w_fine_up, lambda dz, dx, dy: tiled[dz * 9 + dx * 3 + dy], 32, 8, natural(16))


def encode_inner_kernel(
    own, edge, pick, w_first, w_down, pool_near, pool_mid_near, for_twin_near, after,
    fine, pool_far, mid, pool_mid, for_twin, pool_s,
):
    def work(core):
        if core:
            field = jnp.concatenate([own[80:], edge[:48]], axis=0)
            pool_s[:, 0:2] = pool_near[:, 2:4]
        else:
            field = jnp.concatenate([edge[128:], own[:48]], axis=0)
            pool_s[:, 2:4] = pool_near[:, 0:2]
        pairs, far = ((3, 4), 2) if core else ((-1, 0), 0)
        encode(field, pick, w_first, pairs, fine, 6 if core else -1, pool_s, far)
        pool_far[...] = pool_s[:, far : far + 2]
        rows, pooled = middle_rows(pool_s, w_down, 2 if core else 0, 2)
        for at in range(2):
            for py in range(2):
                put_shifts(mid, at, py, rows[py][at])
        near = pool_mid_near[...].astype(F32)
        cells = (near, pooled[0]) if core else (pooled[0], near)
        for at in range(2):
            put_three(pool_mid, at, cells[at])
        for_twin[pl.ds(0, 4 * J), :] = for_twin_near[...]
        for_twin[pl.ds(4 * J, J), :] = jnp.concatenate(cells, axis=1).astype(BF)

    for_each_core(work)


def encode_outer_kernel(
    edge, pick, w_first, w_down, pool_far, fine_near, fine_far, skip_near, w_fine_skip, after,
    mid, pool_mid, skip, pool_s, fine_s,
):
    def work(core):
        if core:
            fine_s[:, 0:2], fine_s[:, 2:5] = fine_near[:, 5:7], fine_far[...]
        else:
            fine_s[:, 0:3], fine_s[:, 3:5] = fine_far[...], fine_near[:, 0:2]
        field = edge[16:] if core else edge[:160]
        far, outer = (0, 2) if core else (4, 0)
        pairs = range(5, 9) if core else range(-5, -1)
        pool_s[:, far : far + 2] = pool_far[...]
        encode(field, pick, w_first, pairs, None, 0, pool_s, outer)
        lhs = jnp.concatenate(
            [
                fine_s[dy : dy + 4, dx : dx + 3].reshape(384, 256)
                for dx in range(3)
                for dy in range(3)
            ],
            axis=1,
        )
        near, rest = (0, 5) if core else (3, 0)
        skip[:, rest : rest + 3] = dot(lhs, w_fine_skip[...]).reshape(4, 3, 32, 256)
        skip[:, near : near + 5] = skip_near[...]
        rows, pooled = middle_rows(pool_s, w_down, 4 if core else -4, 4)
        for at in range(2):
            put_three(pool_mid, at, pooled[at])
            for py in range(2):
                put_shifts(mid, at, py, rows[py][at if core else at + 2])

    for_each_core(work)


def net_kernel(
    from_twin, skip_s, mid_near, mid_far, mid_out, pool_mid_in, pool_mid_out,
    w_coarse, w_mid_skip, w_mid_up, w_fine_up, w_head,
    out,
    mid_s, pool_mid_s, coarse_s, up_s, last_s,
):
    mask = y_mask()

    def gather(core):
        first, last = (6, 0) if core else (0, 6)
        near, far = (2, 4) if core else (4, 2)
        mid_s[:, first : first + 2] = mid_out[...]
        mid_s[:, near : near + 2], mid_s[:, far : far + 2] = mid_near[...], mid_far[...]
        cell = 4 if core else 0
        pool_mid_s[:, cell : cell + 2], pool_mid_s[:, 2:4] = pool_mid_out[...], pool_mid_in[...]
        for at in range(2):
            for py in range(2):
                row = (at * 2 + py) * J
                put_shifts(mid_s, last + at, py, from_twin[row : row + J].astype(F32))
            lanes = slice(at * 128, at * 128 + 128)
            put_three(pool_mid_s, 4 - cell + at, from_twin[4 * J :, lanes].astype(F32))

    for_each_core(gather)

    lhs = jnp.concatenate(
        [
            pool_mid_s[dy, dx : dx + 4].reshape(4 * J, 128)
            for dx in range(3)
            for dy in range(3)
        ],
        axis=1,
    )
    value = silu_half(dot(lhs, w_coarse[...])).reshape(4, J, 256)
    for at in range(4):
        put_three(coarse_s, at, value[at] * (mask * row_flag(at - 1)))

    lhs = jnp.concatenate(
        [
            mid_s[dy : dy + 2, dx : dx + 6].reshape(12 * J, 256)
            for dx in range(3)
            for dy in range(3)
        ],
        axis=1,
    )
    skip = dot(lhs, w_mid_skip[...]).reshape(2, 6, J, 256)
    for py in range(2):
        lhs = jnp.concatenate(
            [
                coarse_s[py + ty, tx : tx + 3].reshape(3 * J, 256)
                for tx in range(2)
                for ty in range(2)
            ],
            axis=1,
        )
        for px in range(2):
            up = dot(lhs, w_mid_up[px * 2 + py]).reshape(3, J, 256)
            for k in range(3):
                at = 2 * k if px else 2 * k + 1
                value = silu_half(skip[py, at] + up[k])
                masked = value * (mask * row_flag((at - 1) // 2))
                up_s[py + 1, at] = masked[:32].astype(BF)
                shift = 1 if py else J - 1
                up_s[0 if py else 3, at] = pltpu.roll(masked, shift, 0)[:32].astype(BF)

    @pl.loop(0, 2)
    def _(py):
        for px in range(2):
            lhs = jnp.concatenate(
                [
                    up_s[pl.ds(py + ty, 2), px + tx : px + tx + 4].reshape(256, 256)
                    for tx in range(2)
                    for ty in range(2)
                ],
                axis=1,
            )
            up = dot(lhs, w_fine_up[px * 2 + py]).reshape(2, 4, 32, 256)
            for half in range(2):
                group = 2 * half + py
                for k in range(4):
                    value = silu_half(skip_s[group, 2 * k + px] + up[half, k])
                    row = pl.multiple_of(group * 32, 32)
                    last_s[2 * k + px, pl.ds(row, 32), :] = value.astype(BF)

    heads = jnp.concatenate([dot_nt(w_head[...], last_s[x]) for x in range(8)], axis=0)
    high = heads.astype(BF)
    rest = heads - high.astype(F32)
    low = rest.astype(BF)
    lowest = (rest - low.astype(F32)).astype(BF)
    row, col = iota((128, 128), 0), iota((128, 128), 1)
    order = (col == 4 * (row % 32) + row // 32).astype(BF)
    noise = dot(
        jnp.concatenate([high, low, lowest], axis=1),
        jnp.concatenate([order, order, order], axis=0),
    ).reshape(8, 16, 128)
    for x in range(8):
        out[:, x, :] = noise[x]


def body(
    noisy_field, first_weight, down_weight, coarse_weight, middle_weight, fine_weight, head_weight
):
    def shape(*dims, kind=BF):
        return jax.ShapeDtypeStruct(dims, kind)

    def cost(flops, moved):
        return pl.CostEstimate(flops=flops, bytes_accessed=moved, transcendentals=0)

    def small(limit):
        return pltpu.CompilerParams(vmem_limit_bytes=limit * 2**20)

    w_first, w_down, w_coarse, w_head, middle, fine, pick = pl.pallas_call(
        encoder_weights_kernel,
        out_shape=(
            shape(2, 192, 256),
            shape(1152, 256),
            shape(1152, 256),
            shape(16, 256),
            shape(27, 32, 96),
            shape(27, 16, 48),
            shape(4 * J, 256),
        ),
        in_specs=[ANY] * 6,
        out_specs=(VMEM,) * 7,
        scratch_shapes=[
            pltpu.VMEM((9, 3, 16), BF),
            pltpu.VMEM((27, 16, 32), BF),
            pltpu.VMEM((27, 32, 64), BF),
            pltpu.VMEM((1, 16), BF),
            pltpu.SemaphoreType.DMA((6,)),
        ],
        compiler_params=small(16),
        cost_estimate=cost(10**9, 3 * 10**6),
    )(
        *(
            pltpu.with_memory_space_constraint(weight, pltpu.HBM)
            for weight in (
                first_weight.transpose(1, 2, 3, 4, 0).reshape(9, 3, 16),
                down_weight.transpose(2, 3, 4, 1, 0).reshape(27, 16, 32),
                coarse_weight.transpose(2, 3, 4, 1, 0).reshape(27, 32, 64),
                middle_weight.transpose(2, 3, 4, 0, 1).reshape(27, 32, 96),
                fine_weight.transpose(2, 3, 4, 0, 1).reshape(27, 16, 48),
                head_weight.reshape(1, 16),
            )
        )
    )

    w_mid_skip = pl.pallas_call(
        mid_skip_weights_kernel,
        out_shape=shape(2304, 256),
        in_specs=[VMEM],
        out_specs=VMEM,
        compiler_params=small(16),
        cost_estimate=cost(10**9, 2 * 10**6),
    )(middle)

    def pairs(axis):
        count = lax.axis_size(axis)
        inner = [(i, i ^ 1) for i in range(count)]
        return inner, [(i, ((i + 1) ^ 1) - 1) for i in range(1, count - 1)]

    swap_in, swap_out = pairs("gy")
    y_outer = lax.ppermute(noisy_field, "gy", swap_out)
    y_inner = lax.ppermute(noisy_field, "gy", swap_in)
    own = pl.pallas_call(
        join_kernel,
        out_shape=shape(128, 256),
        in_specs=[VMEM] * 3 + [ANY] * 2,
        out_specs=VMEM,
        compiler_params=small(4),
        cost_estimate=cost(10**7, 2 * 10**5),
    )(noisy_field, y_outer, y_inner, w_head, w_mid_skip)

    in_chip, between = pairs("gx")
    twin = lax.ppermute(own, "gx", in_chip)
    w_mid_up = pl.pallas_call(
        mid_up_weights_kernel,
        out_shape=shape(4, 1024, 256),
        in_specs=[VMEM, ANY],
        out_specs=VMEM,
        scratch_shapes=[pltpu.VMEM((27, 64, 256), F32)],
        compiler_params=small(24),
        cost_estimate=cost(10**9, 4 * 10**6),
    )(middle, own)
    edge = pl.pallas_call(
        chip_edge_kernel,
        out_shape=shape(176, 256),
        in_specs=[VMEM] * 2 + [ANY],
        out_specs=VMEM,
        compiler_params=small(4),
        cost_estimate=cost(10**5, 3 * 10**5),
    )(own, twin, w_mid_up)
    chip_edge = lax.ppermute(edge, "gx", between)

    fine_near, pool_near, mid_near, pool_mid_near, for_twin_near, w_fine_skip = pl.pallas_call(
        encode_near_kernel,
        out_shape=(
            shape(6, 7, 32, 256),
            shape(4, 4, J, 128),
            shape(4, 2, J, 256),
            shape(J, 128),
            shape(4 * J, 256),
            shape(2304, 256),
        ),
        in_specs=[VMEM] * 6 + [ANY],
        out_specs=(VMEM,) * 6,
        compiler_params=small(16),
        cost_estimate=cost(10**9, 3 * 10**6),
    )(own, twin, pick, w_first, w_down, fine, edge)
    skip_near, w_fine_up = pl.pallas_call(
        skip_near_kernel,
        out_shape=(shape(4, 5, 32, 256, kind=F32), shape(4, 1024, 256)),
        in_specs=[VMEM] * 3,
        out_specs=(VMEM,) * 2,
        scratch_shapes=[pltpu.VMEM((27, 32, 256), F32)],
        compiler_params=small(16),
        cost_estimate=cost(10**9, 4 * 10**6),
    )(fine_near, fine, w_fine_skip)

    fine_far, pool_far, mid_far, pool_mid_in, for_twin = pl.pallas_call(
        encode_inner_kernel,
        out_shape=(
            shape(6, 3, 32, 256),
            shape(4, 2, J, 128),
            shape(4, 2, J, 256),
            shape(3, 2, J, 128),
            shape(5 * J, 256),
        ),
        in_specs=[VMEM] * 8 + [ANY],
        out_specs=(VMEM,) * 5,
        scratch_shapes=[pltpu.VMEM((4, 4, J, 128), BF)],
        compiler_params=small(16),
        cost_estimate=cost(10**9, 3 * 10**6),
    )(
        own, chip_edge, pick, w_first, w_down, pool_near, pool_mid_near, for_twin_near,
        skip_near,
    )
    from_twin = lax.ppermute(for_twin, "gx", in_chip)
    mid_out, pool_mid_out, skip = pl.pallas_call(
        encode_outer_kernel,
        out_shape=(
            shape(4, 2, J, 256),
            shape(3, 2, J, 128),
            shape(4, 8, 32, 256, kind=F32),
        ),
        in_specs=[VMEM] * 9 + [ANY],
        out_specs=(VMEM,) * 3,
        scratch_shapes=[pltpu.VMEM((4, 6, J, 128), BF), pltpu.VMEM((6, 5, 32, 256), BF)],
        compiler_params=small(16),
        cost_estimate=cost(2 * 10**9, 3 * 10**6),
    )(
        chip_edge, pick, w_first, w_down, pool_far, fine_near, fine_far, skip_near, w_fine_skip,
        for_twin,
    )

    return pl.pallas_call(
        net_kernel,
        out_shape=shape(16, 8, 128, kind=F32),
        in_specs=[VMEM] * 12,
        out_specs=VMEM,
        scratch_shapes=[
            pltpu.VMEM((4, 8, J, 256), BF),
            pltpu.VMEM((3, 6, J, 128), BF),
            pltpu.VMEM((3, 4, J, 256), BF),
            pltpu.VMEM((4, 6, 32, 256), BF),
            pltpu.VMEM((8, 128, 256), BF),
        ],
        compiler_params=small(32),
        cost_estimate=pl.CostEstimate(
            flops=6 * 10**9, bytes_accessed=9 * 10**6, transcendentals=10**6
        ),
    )(
        from_twin, skip, mid_near, mid_far, mid_out, pool_mid_in, pool_mid_out,
        w_coarse, w_mid_skip, w_mid_up, w_fine_up, w_head,
    )


def solution(mesh):
    placed = (P(None, "gx", "gy"), P(), P(), P(), P(), P(), P())
    return jax.shard_map(
        body, mesh=mesh, in_specs=placed, out_specs=P(None, "gx", "gy"), check_vma=False
    )
```

```python
import jax
import jax.numpy as jnp
from jax import lax
from jax.experimental import pallas as pl
from jax.experimental.pallas import tpu as pltpu
from jax.sharding import PartitionSpec as P

BF = jnp.bfloat16
F32 = jnp.float32
J = 40
VMEM = pl.BlockSpec(memory_space=pltpu.VMEM)
ANY = pl.BlockSpec(memory_space=pl.ANY)


def dot(a, b):
    return jnp.dot(a, b, preferred_element_type=F32)


def dot_nt(a, b):
    return lax.dot_general(a, b, (((1,), (1,)), ((), ())), preferred_element_type=F32)


def dot_tn(a, b):
    return lax.dot_general(a, b, (((0,), (0,)), ((), ())), preferred_element_type=F32)


def iota(shape, axis):
    return lax.broadcasted_iota(jnp.int32, shape, axis)


def natural(channels):
    return lambda lane: lane // channels


def halves(channels):
    return lambda lane: 2 * ((lane // channels) % (128 // channels)) + lane // 128


def repeat_matrix(channels):
    return (iota((channels, 256), 1) % channels == iota((channels, 256), 0)).astype(BF)


def ones_where(cond):
    return jnp.where(cond, 1.0, 0.0).astype(BF)


def tiles(depth_of):
    return [
        (slice(at, at + 128), {depth_of(lane) for lane in range(at, at + 128)})
        for at in (0, 128)
    ]


def place_block(out, index, row, rows, terms, places, held, lanes):
    total = None
    for depths, value in terms:
        depths = [depth for depth in depths if depth in held]
        if depths:
            mask = places[:, lanes] == depths[0]
            for depth in depths[1:]:
                mask = mask | (places[:, lanes] == depth)
            part = ones_where(mask) * value[:, lanes]
            total = part if total is None else total + part
    if total is None:
        total = jnp.zeros((rows, 128), BF)
    out[(*index, pl.ds(row, rows), lanes)] = total


def cell_of(j):
    return jnp.where(j < 36, j, j - J)


def cell_inside(axis, held, cell):
    at = lax.axis_index(axis) * held + cell
    return (at >= 0) & (at < lax.axis_size(axis) * held)


SETS = (((0,), (1, 2)), ((0, 1), (2,)))


def banded(out, taps, channels, row_depths, depth_of):
    size = channels * len(row_depths)
    places = depth_of(iota((channels, 256), 1))
    for lanes, held in tiles(depth_of):
        for at, depth in enumerate(row_depths):
            for xy in range(9):
                terms = [((depth + 1 - dz,), taps[dz][xy]) for dz in range(3)]
                row = xy * size + at * channels
                place_block(out, (), row, channels, terms, places, held, lanes)


def folded(out, get, channels, depths, depth_of):
    size = channels * depths
    places = depth_of(iota((channels, 256), 1))
    even = places % 2 == 0
    for px in range(2):
        for tx in range(2):
            by_y = [
                [sum(get(dz, dx, dy) for dx in SETS[px][tx]) for dy in range(3)]
                for dz in range(3)
            ]
            for py in range(2):
                for ty in range(2):
                    w0, w1, w2 = [
                        sum(by_y[dz][dy] for dy in SETS[py][ty]) for dz in range(3)
                    ]
                    inner = jnp.where(even, w1 + w2, w0 + w1).astype(BF)
                    outer = jnp.where(even, w0, w2).astype(BF)
                    for lanes, held in tiles(depth_of):
                        for depth in range(depths):
                            terms = [
                                ((2 * depth, 2 * depth + 1), inner),
                                ((2 * depth + 2, 2 * depth - 1), outer),
                            ]
                            row = (tx * 2 + ty) * size + depth * channels
                            index = (px * 2 + py,)
                            place_block(out, index, row, channels, terms, places, held, lanes)


def encoder_weights_kernel(
    raw_first, raw_down, raw_coarse, raw_middle, raw_fine, raw_head,
    w_first, w_down, w_coarse, w_head, middle, fine, pick,
    first, down, coarse, head, sems,
):
    copies = [
        pltpu.make_async_copy(source, target, sems.at[at])
        for at, (source, target) in enumerate(
            (
                (raw_first, first),
                (raw_down, down),
                (raw_coarse, coarse),
                (raw_head, head),
                (raw_middle, middle),
                (raw_fine, fine),
            )
        )
    ]
    for copy in copies:
        copy.start()
    r16, r32, r64 = repeat_matrix(16), repeat_matrix(32), repeat_matrix(64)
    row = iota((4 * J, 256), 0)
    cell = cell_of(row % J)
    inside = cell_inside("gy", 32, cell)
    pick[...] = ((iota((4 * J, 256), 1) == (4 * cell + row // J + 256) % 256) & inside).astype(BF)
    for copy in copies[:4]:
        copy.wait()

    w_first[...] = jnp.zeros_like(w_first)
    for dx in range(3):
        rows = [dot(first[dz * 3 + dx], r16) * 0.5 for dz in range(3)]
        place = halves(16)(iota((16, 256), 1))
        depth = iota((16, 256), 0)
        for dy in range(3):
            block = jnp.zeros((16, 256), F32)
            for dz in range(3):
                block = block + jnp.where(place == depth + 1 - dz, rows[dz][dy : dy + 1], 0.0)
            block = block.astype(BF)
            for even in range(2):
                w_first[even, pl.ds(dy * 64 + (even + dx) * 16, 16), :] = block

    flat = down[...].reshape(27 * 16, 32)
    all_taps = (dot(flat, r32) * (1 / 16)).astype(BF)
    taps = [[all_taps[(dz * 9 + xy) * 16 : (dz * 9 + xy + 1) * 16] for xy in range(9)] for dz in range(3)]
    banded(w_down, taps, 16, list(range(8)), halves(32))

    flat = coarse[...].reshape(27 * 32, 64)
    all_taps = (dot(flat, r64) * (1 / 16)).astype(BF)
    taps = [[all_taps[(dz * 9 + xy) * 32 : (dz * 9 + xy + 1) * 32] for xy in range(9)] for dz in range(3)]
    banded(w_coarse, taps, 32, list(range(4)), natural(64))

    row = dot(jnp.broadcast_to(head[...], (16, 16)), r16)
    w_head[...] = jnp.where(iota((16, 256), 1) // 16 == iota((16, 256), 0), row, 0.0).astype(BF)
    for copy in copies[4:]:
        copy.wait()


def mid_skip_weights_kernel(middle, w_mid_skip):
    r32 = repeat_matrix(32)
    tiled = [(dot_tn(middle[tap, :, 64:96], r32) * 0.5).astype(BF) for tap in range(27)]
    taps = [tiled[dz * 9 : dz * 9 + 9] for dz in range(3)]
    banded(w_mid_skip, taps, 32, [0, 2, 4, 6, 1, 3, 5, 7], natural(32))


def mid_up_weights_kernel(middle, after, w_mid_up, tiled):
    r32 = repeat_matrix(32)
    for tap in range(27):
        tiled[tap] = dot_tn(middle[tap, :, 0:64], r32) * 0.5
    folded(w_mid_up, lambda dz, dx, dy: tiled[dz * 9 + dx * 3 + dy], 64, 4, natural(32))


def fine_skip_weights(fine, w_fine_skip):
    r16 = repeat_matrix(16)
    tiled = [(dot_tn(fine[tap, :, 32:48], r16) * 0.5).astype(BF) for tap in range(27)]
    taps = [tiled[dz * 9 : dz * 9 + 9] for dz in range(3)]
    banded(w_fine_skip, taps, 16, list(range(0, 16, 2)) + list(range(1, 16, 2)), natural(16))


def join_kernel(own, outer, inner, after, also_after, out):
    from_inner = (iota((128, 128), 1) < 64) == (lax.axis_index("gy") % 2 == 0)
    mine = own[...].astype(F32).reshape(128, 128)
    rim = jnp.where(
        from_inner,
        inner[...].astype(F32).reshape(128, 128),
        outer[...].astype(F32).reshape(128, 128),
    )
    both = jnp.concatenate([mine, rim], axis=1).astype(BF)
    row, col = iota((128, 128), 0), iota((128, 128), 1)
    swap = (col == (row % 16) * 8 + row // 16).astype(BF)
    out[...] = dot(swap, both).astype(BF)


def chip_edge_kernel(own, twin, after, out):
    odd = lax.axis_index("gx") % 2 == 1
    for_high = jnp.concatenate([twin[80:], own[...]], axis=0)
    for_low = jnp.concatenate([own[...], twin[:48]], axis=0)
    out[...] = jnp.where(odd, for_high, for_low)


def silu_half(h):
    return h + h * jnp.tanh(h)


def row_flag(cell):
    return jnp.where(cell_inside("gx", 2, cell), 1.0, 0.0)


def put_shifts(out, at, group, value):
    out[group + 1, at] = value.astype(BF)
    out[0 if group else 3, at] = pltpu.roll(value, 1 if group else J - 1, 0).astype(BF)


def put_three(out, at, value):
    out[0, at] = pltpu.roll(value, 1, 0).astype(BF)
    out[1, at] = value.astype(BF)
    out[2, at] = pltpu.roll(value, J - 1, 0).astype(BF)


def encode(field, pick, w_first, pairs, fine, first_x, pooled, pooled_at):
    wide = field.astype(F32)
    shifted = [pltpu.roll(wide, 1, 1).astype(BF), field, pltpu.roll(wide, 255, 1).astype(BF)]
    for at, m in enumerate(pairs):
        window = jnp.concatenate([part[at * 32 : at * 32 + 64] for part in shifted], axis=0)
        lhs = (dot_nt(pick[...], window) * row_flag(m // 2)).astype(BF)
        sums = [jnp.zeros((J, 128), F32) for _ in range(2)]
        for even in range(2):
            value = silu_half(dot(lhs, w_first[even])).reshape(4, J, 256)
            for part in range(2):
                both = value[2 * part] + value[2 * part + 1]
                sums[part] = sums[part] + both[:, :128] + both[:, 128:]
            x = 2 * m + even
            if fine is not None and -1 <= x <= 8:
                for group in range(4):
                    fine[group + 1, x - first_x] = value[group, :32].astype(BF)
                fine[0, x - first_x] = pltpu.roll(value[3], 1, 0)[:32].astype(BF)
                fine[5, x - first_x] = pltpu.roll(value[0], J - 1, 0)[:32].astype(BF)
        for part in range(2):
            put_shifts(pooled, pooled_at + at, part, sums[part])


def for_each_core(work):
    odd = lax.axis_index("gx") % 2

    @pl.when(odd == 0)
    def _():
        work(0)

    @pl.when(odd == 1)
    def _():
        work(1)


def middle_rows(pool_s, w_down, first, count):
    lhs = jnp.concatenate(
        [
            pool_s[dy : dy + 2, dx : dx + count].reshape(2 * count * J, 128)
            for dx in range(3)
            for dy in range(3)
        ],
        axis=1,
    )
    value = silu_half(dot(lhs, w_down[...])).reshape(2, count, J, 256)
    mask = y_mask()
    rows = [
        [value[py, at] * (mask * row_flag((first + at) // 2)) for at in range(count)]
        for py in range(2)
    ]
    pooled = []
    for at in range(0, count, 2):
        cells = rows[0][at] + rows[0][at + 1] + rows[1][at] + rows[1][at + 1]
        pooled.append(cells[:, :128] + cells[:, 128:])
    return rows, pooled


def y_mask():
    return jnp.where(cell_inside("gy", 32, cell_of(iota((J, 256), 0))), 1.0, 0.0)


def encode_near_kernel(
    own, twin, pick, w_first, w_down, fine_taps, after,
    fine, pooled, mid, pool_mid, for_twin, w_fine_skip,
):
    def work(core):
        fine_skip_weights(fine_taps, w_fine_skip)
        if core:
            field = jnp.concatenate([twin[80:], own[:112]], axis=0)
        else:
            field = jnp.concatenate([own[16:], twin[:48]], axis=0)
        pairs = range(-1, 3) if core else range(1, 5)
        encode(field, pick, w_first, pairs, fine, -1 if core else 2, pooled, 0)
        rows, cells = middle_rows(pooled, w_down, 0 if core else 2, 2)
        for at in range(2):
            for py in range(2):
                put_shifts(mid, at, py, rows[py][at])
                for_twin[pl.ds((at * 2 + py) * J, J), :] = rows[py][at].astype(BF)
        pool_mid[...] = cells[0].astype(BF)

    for_each_core(work)


def skip_near_kernel(fine_near, fine, w_fine_skip, out, w_fine_up, tiled):
    lhs = jnp.concatenate(
        [
            fine_near[dy : dy + 4, dx : dx + 5].reshape(640, 256)
            for dx in range(3)
            for dy in range(3)
        ],
        axis=1,
    )
    out[...] = dot(lhs, w_fine_skip[...]).reshape(4, 5, 32, 256)
    r16 = repeat_matrix(16)
    for tap in range(27):
        tiled[tap] = dot_tn(fine[tap, :, 0:32], r16) * 0.5
    folded(w_fine_up, lambda dz, dx, dy: tiled[dz * 9 + dx * 3 + dy], 32, 8, natural(16))


def encode_inner_kernel(
    own, edge, pick, w_first, w_down, pool_near, pool_mid_near, for_twin_near, after,
    fine, pool_far, mid, pool_mid, for_twin, pool_s,
):
    def work(core):
        if core:
            field = jnp.concatenate([own[80:], edge[:48]], axis=0)
            pool_s[:, 0:2] = pool_near[:, 2:4]
        else:
            field = jnp.concatenate([edge[128:], own[:48]], axis=0)
            pool_s[:, 2:4] = pool_near[:, 0:2]
        pairs, far = ((3, 4), 2) if core else ((-1, 0), 0)
        encode(field, pick, w_first, pairs, fine, 6 if core else -1, pool_s, far)
        pool_far[...] = pool_s[:, far : far + 2]
        rows, pooled = middle_rows(pool_s, w_down, 2 if core else 0, 2)
        for at in range(2):
            for py in range(2):
                put_shifts(mid, at, py, rows[py][at])
        near = pool_mid_near[...].astype(F32)
        cells = (near, pooled[0]) if core else (pooled[0], near)
        for at in range(2):
            put_three(pool_mid, at, cells[at])
        for_twin[pl.ds(0, 4 * J), :] = for_twin_near[...]
        for_twin[pl.ds(4 * J, J), :] = jnp.concatenate(cells, axis=1).astype(BF)

    for_each_core(work)


def encode_outer_kernel(
    edge, pick, w_first, w_down, pool_far, fine_near, fine_far, skip_near, w_fine_skip, after,
    mid, pool_mid, skip, pool_s, fine_s,
):
    def work(core):
        if core:
            fine_s[:, 0:2], fine_s[:, 2:5] = fine_near[:, 5:7], fine_far[...]
        else:
            fine_s[:, 0:3], fine_s[:, 3:5] = fine_far[...], fine_near[:, 0:2]
        field = edge[16:] if core else edge[:160]
        far, outer = (0, 2) if core else (4, 0)
        pairs = range(5, 9) if core else range(-5, -1)
        pool_s[:, far : far + 2] = pool_far[...]
        encode(field, pick, w_first, pairs, None, 0, pool_s, outer)
        rows, pooled = middle_rows(pool_s, w_down, 4 if core else -4, 4)
        for at in range(2):
            put_three(pool_mid, at, pooled[at])
            for py in range(2):
                put_shifts(mid, at, py, rows[py][at if core else at + 2])
        lhs = jnp.concatenate(
            [
                fine_s[dy : dy + 4, dx : dx + 3].reshape(384, 256)
                for dx in range(3)
                for dy in range(3)
            ],
            axis=1,
        )
        near, rest = (0, 5) if core else (3, 0)
        skip[:, rest : rest + 3] = dot(lhs, w_fine_skip[...]).reshape(4, 3, 32, 256)
        skip[:, near : near + 5] = skip_near[...]

    for_each_core(work)


def net_kernel(
    from_twin, skip_s, mid_near, mid_far, mid_out, pool_mid_in, pool_mid_out,
    w_coarse, w_mid_skip, w_mid_up, w_fine_up, w_head,
    out,
    mid_s, pool_mid_s, coarse_s, up_s, last_s,
):
    mask = y_mask()

    def gather(core):
        first, last = (6, 0) if core else (0, 6)
        near, far = (2, 4) if core else (4, 2)
        mid_s[:, first : first + 2] = mid_out[...]
        mid_s[:, near : near + 2], mid_s[:, far : far + 2] = mid_near[...], mid_far[...]
        cell = 4 if core else 0
        pool_mid_s[:, cell : cell + 2], pool_mid_s[:, 2:4] = pool_mid_out[...], pool_mid_in[...]
        for at in range(2):
            for py in range(2):
                row = (at * 2 + py) * J
                put_shifts(mid_s, last + at, py, from_twin[row : row + J].astype(F32))
            lanes = slice(at * 128, at * 128 + 128)
            put_three(pool_mid_s, 4 - cell + at, from_twin[4 * J :, lanes].astype(F32))

    for_each_core(gather)

    lhs = jnp.concatenate(
        [
            pool_mid_s[dy, dx : dx + 4].reshape(4 * J, 128)
            for dx in range(3)
            for dy in range(3)
        ],
        axis=1,
    )
    value = silu_half(dot(lhs, w_coarse[...])).reshape(4, J, 256)
    for at in range(4):
        put_three(coarse_s, at, value[at] * (mask * row_flag(at - 1)))

    lhs = jnp.concatenate(
        [
            mid_s[dy : dy + 2, dx : dx + 6].reshape(12 * J, 256)
            for dx in range(3)
            for dy in range(3)
        ],
        axis=1,
    )
    skip = dot(lhs, w_mid_skip[...]).reshape(2, 6, J, 256)
    for py in range(2):
        lhs = jnp.concatenate(
            [
                coarse_s[py + ty, tx : tx + 3].reshape(3 * J, 256)
                for tx in range(2)
                for ty in range(2)
            ],
            axis=1,
        )
        for px in range(2):
            up = dot(lhs, w_mid_up[px * 2 + py]).reshape(3, J, 256)
            for k in range(3):
                at = 2 * k if px else 2 * k + 1
                value = silu_half(skip[py, at] + up[k])
                masked = value * (mask * row_flag((at - 1) // 2))
                up_s[py + 1, at] = masked[:32].astype(BF)
                shift = 1 if py else J - 1
                up_s[0 if py else 3, at] = pltpu.roll(masked, shift, 0)[:32].astype(BF)

    @pl.loop(0, 2)
    def _(py):
        for px in range(2):
            lhs = jnp.concatenate(
                [
                    up_s[pl.ds(py + ty, 2), px + tx : px + tx + 4].reshape(256, 256)
                    for tx in range(2)
                    for ty in range(2)
                ],
                axis=1,
            )
            up = dot(lhs, w_fine_up[px * 2 + py]).reshape(2, 4, 32, 256)
            for half in range(2):
                group = 2 * half + py
                for k in range(4):
                    value = silu_half(skip_s[group, 2 * k + px] + up[half, k])
                    row = pl.multiple_of(group * 32, 32)
                    last_s[2 * k + px, pl.ds(row, 32), :] = value.astype(BF)

    heads = jnp.concatenate([dot_nt(w_head[...], last_s[x]) for x in range(8)], axis=0)
    high = heads.astype(BF)
    rest = heads - high.astype(F32)
    low = rest.astype(BF)
    lowest = (rest - low.astype(F32)).astype(BF)
    row, col = iota((128, 128), 0), iota((128, 128), 1)
    order = (col == 4 * (row % 32) + row // 32).astype(BF)
    noise = dot(
        jnp.concatenate([high, low, lowest], axis=1),
        jnp.concatenate([order, order, order], axis=0),
    ).reshape(8, 16, 128)
    for x in range(8):
        out[:, x, :] = noise[x]


def body(
    noisy_field, first_weight, down_weight, coarse_weight, middle_weight, fine_weight, head_weight
):
    def shape(*dims, kind=BF):
        return jax.ShapeDtypeStruct(dims, kind)

    def cost(flops, moved):
        return pl.CostEstimate(flops=flops, bytes_accessed=moved, transcendentals=0)

    def small(limit):
        return pltpu.CompilerParams(vmem_limit_bytes=limit * 2**20)

    w_first, w_down, w_coarse, w_head, middle, fine, pick = pl.pallas_call(
        encoder_weights_kernel,
        out_shape=(
            shape(2, 192, 256),
            shape(1152, 256),
            shape(1152, 256),
            shape(16, 256),
            shape(27, 32, 96),
            shape(27, 16, 48),
            shape(4 * J, 256),
        ),
        in_specs=[ANY] * 6,
        out_specs=(VMEM,) * 7,
        scratch_shapes=[
            pltpu.VMEM((9, 3, 16), BF),
            pltpu.VMEM((27, 16, 32), BF),
            pltpu.VMEM((27, 32, 64), BF),
            pltpu.VMEM((1, 16), BF),
            pltpu.SemaphoreType.DMA((6,)),
        ],
        compiler_params=small(16),
        cost_estimate=cost(10**9, 3 * 10**6),
    )(
        *(
            pltpu.with_memory_space_constraint(weight, pltpu.HBM)
            for weight in (
                first_weight.transpose(1, 2, 3, 4, 0).reshape(9, 3, 16),
                down_weight.transpose(2, 3, 4, 1, 0).reshape(27, 16, 32),
                coarse_weight.transpose(2, 3, 4, 1, 0).reshape(27, 32, 64),
                middle_weight.transpose(2, 3, 4, 0, 1).reshape(27, 32, 96),
                fine_weight.transpose(2, 3, 4, 0, 1).reshape(27, 16, 48),
                head_weight.reshape(1, 16),
            )
        )
    )

    w_mid_skip = pl.pallas_call(
        mid_skip_weights_kernel,
        out_shape=shape(2304, 256),
        in_specs=[VMEM],
        out_specs=VMEM,
        compiler_params=small(16),
        cost_estimate=cost(10**9, 2 * 10**6),
    )(middle)

    def pairs(axis):
        count = lax.axis_size(axis)
        inner = [(i, i ^ 1) for i in range(count)]
        return inner, [(i, ((i + 1) ^ 1) - 1) for i in range(1, count - 1)]

    swap_in, swap_out = pairs("gy")
    y_outer = lax.ppermute(noisy_field, "gy", swap_out)
    y_inner = lax.ppermute(noisy_field, "gy", swap_in)
    own = pl.pallas_call(
        join_kernel,
        out_shape=shape(128, 256),
        in_specs=[VMEM] * 3 + [ANY] * 2,
        out_specs=VMEM,
        compiler_params=small(4),
        cost_estimate=cost(10**7, 2 * 10**5),
    )(noisy_field, y_outer, y_inner, w_head, w_mid_skip)

    in_chip, between = pairs("gx")
    twin = lax.ppermute(own, "gx", in_chip)
    w_mid_up = pl.pallas_call(
        mid_up_weights_kernel,
        out_shape=shape(4, 1024, 256),
        in_specs=[VMEM, ANY],
        out_specs=VMEM,
        scratch_shapes=[pltpu.VMEM((27, 64, 256), F32)],
        compiler_params=small(24),
        cost_estimate=cost(10**9, 4 * 10**6),
    )(middle, own)
    edge = pl.pallas_call(
        chip_edge_kernel,
        out_shape=shape(176, 256),
        in_specs=[VMEM] * 2 + [ANY],
        out_specs=VMEM,
        compiler_params=small(4),
        cost_estimate=cost(10**5, 3 * 10**5),
    )(own, twin, w_mid_up)
    chip_edge = lax.ppermute(edge, "gx", between)

    fine_near, pool_near, mid_near, pool_mid_near, for_twin_near, w_fine_skip = pl.pallas_call(
        encode_near_kernel,
        out_shape=(
            shape(6, 7, 32, 256),
            shape(4, 4, J, 128),
            shape(4, 2, J, 256),
            shape(J, 128),
            shape(4 * J, 256),
            shape(2304, 256),
        ),
        in_specs=[VMEM] * 6 + [ANY],
        out_specs=(VMEM,) * 6,
        compiler_params=small(16),
        cost_estimate=cost(10**9, 3 * 10**6),
    )(own, twin, pick, w_first, w_down, fine, edge)
    skip_near, w_fine_up = pl.pallas_call(
        skip_near_kernel,
        out_shape=(shape(4, 5, 32, 256, kind=F32), shape(4, 1024, 256)),
        in_specs=[VMEM] * 3,
        out_specs=(VMEM,) * 2,
        scratch_shapes=[pltpu.VMEM((27, 32, 256), F32)],
        compiler_params=small(16),
        cost_estimate=cost(10**9, 4 * 10**6),
    )(fine_near, fine, w_fine_skip)

    fine_far, pool_far, mid_far, pool_mid_in, for_twin = pl.pallas_call(
        encode_inner_kernel,
        out_shape=(
            shape(6, 3, 32, 256),
            shape(4, 2, J, 128),
            shape(4, 2, J, 256),
            shape(3, 2, J, 128),
            shape(5 * J, 256),
        ),
        in_specs=[VMEM] * 8 + [ANY],
        out_specs=(VMEM,) * 5,
        scratch_shapes=[pltpu.VMEM((4, 4, J, 128), BF)],
        compiler_params=small(16),
        cost_estimate=cost(10**9, 3 * 10**6),
    )(
        own, chip_edge, pick, w_first, w_down, pool_near, pool_mid_near, for_twin_near,
        skip_near,
    )
    from_twin = lax.ppermute(for_twin, "gx", in_chip)
    mid_out, pool_mid_out, skip = pl.pallas_call(
        encode_outer_kernel,
        out_shape=(
            shape(4, 2, J, 256),
            shape(3, 2, J, 128),
            shape(4, 8, 32, 256, kind=F32),
        ),
        in_specs=[VMEM] * 9 + [ANY],
        out_specs=(VMEM,) * 3,
        scratch_shapes=[pltpu.VMEM((4, 6, J, 128), BF), pltpu.VMEM((6, 5, 32, 256), BF)],
        compiler_params=small(16),
        cost_estimate=cost(2 * 10**9, 3 * 10**6),
    )(
        chip_edge, pick, w_first, w_down, pool_far, fine_near, fine_far, skip_near, w_fine_skip,
        for_twin,
    )

    return pl.pallas_call(
        net_kernel,
        out_shape=shape(16, 8, 128, kind=F32),
        in_specs=[VMEM] * 12,
        out_specs=VMEM,
        scratch_shapes=[
            pltpu.VMEM((4, 8, J, 256), BF),
            pltpu.VMEM((3, 6, J, 128), BF),
            pltpu.VMEM((3, 4, J, 256), BF),
            pltpu.VMEM((4, 6, 32, 256), BF),
            pltpu.VMEM((8, 128, 256), BF),
        ],
        compiler_params=small(32),
        cost_estimate=pl.CostEstimate(
            flops=6 * 10**9, bytes_accessed=9 * 10**6, transcendentals=10**6
        ),
    )(
        from_twin, skip, mid_near, mid_far, mid_out, pool_mid_in, pool_mid_out,
        w_coarse, w_mid_skip, w_mid_up, w_fine_up, w_head,
    )


def solution(mesh):
    placed = (P(None, "gx", "gy"), P(), P(), P(), P(), P(), P())
    return jax.shard_map(
        body, mesh=mesh, in_specs=placed, out_specs=P(None, "gx", "gy"), check_vma=False
    )
```
